32 devices in a mesh: lon: 16 (over z, y, core), lat: 2 (over x).
Axes of the slice: x: 2, y: 2, z: 4, core: 2. Of those that a mesh axis runs over, the one named last changes fastest.
Arguments:
- features: bfloat16 [20, 224, 768], P('lat', 'lon'), may hold values from -6 to 6
- cotangent: bfloat16 [20, 224, 768], P('lat', 'lon'), may hold values from -6 to 6
- weight_in: float32 [2, 8, 96, 96], replicated, may hold values from -0.4375 to 0.4375
- bias_in: float32 [2, 8, 96], replicated, may hold values from -4 to 4
- weight_out: float32 [2, 8, 96, 96], replicated, may hold values from -0.4375 to 0.4375
Outputs:
- grad_features: bfloat16 [20, 224, 768], P('lat', 'lon')
- grad_weight_in: float32 [2, 8, 96, 96], replicated
- grad_bias_in: float32 [2, 8, 96], replicated
- grad_weight_out: float32 [2, 8, 96, 96], replicated
The draws below stay inside these ranges and needn't reach their ends.
All inputs are finite; a program needn't handle non-finite values.
Results may differ from the reference program's by a relative error of at most 0.001.
Values may be sent and summed in bfloat16 or wider, within the bound.
No kernel may reach another device: no remote copies, remote signals or barrier semaphores. Data moves between devices by JAX's collectives and lax.ppermute only.
A program may use at most 128 MiB of HBM per device.

```python
import math
import jax
import jax.numpy as jnp
from jax import lax

LAT_DEV = 10
BLOCKS = 8
BLOCK_WIDTH = 96
CHANNELS = 768
ROWS = 20
COLS = 224
MODES = 64
N_LAT = 2


def block_levels(stream_key, shape, shards, smallest, top_value):
    level, own = 1.0, jax.random.fold_in(stream_key, 6)
    for position, parts in shards:
        steps = jnp.exp(jax.random.uniform(jax.random.fold_in(own, position), (parts,), jnp.float32, smallest / len(shards), top_value / len(shards)))
        level = level * jnp.repeat(steps, shape[position] // parts).reshape([-1 if axis == position else 1 for axis in range(len(shape))])
    return level


def bell_draw(stream_key, dims, deviation, reach, shards=(), kind=jnp.bfloat16):
    values = jax.random.normal(stream_key, dims, jnp.float32) * deviation
    if len(shards) > 0:
        values = block_levels(stream_key, dims, shards, -0.22, 0.18) * values
    return jnp.clip(values, min=-reach, max=reach).astype(kind)


def setup_inputs(seed: int = 0) -> dict:
    keys = jax.random.split(jax.random.key(seed), 6)
    features = bell_draw(keys[0], (ROWS, COLS, CHANNELS), 1.0, 6.0, ((0, 2), (1, 16)))
    cotangent = bell_draw(keys[1], (ROWS, COLS, CHANNELS), 1.0, 6.0, ((0, 2), (1, 16)))
    weight_in = bell_draw(keys[2], (2, BLOCKS, BLOCK_WIDTH, BLOCK_WIDTH), (2 * BLOCK_WIDTH) ** -0.5, 0.4375, (), jnp.float32)
    bias_in = bell_draw(keys[3], (2, BLOCKS, BLOCK_WIDTH), 1.0, 4.0, (), jnp.float32)
    weight_out = bell_draw(keys[4], (2, BLOCKS, BLOCK_WIDTH, BLOCK_WIDTH), (2 * BLOCK_WIDTH) ** -0.5, 0.4375, (), jnp.float32)
    return {"features": features, "cotangent": cotangent, "weight_in": weight_in, "bias_in": bias_in, "weight_out": weight_out}


precise = lax.Precision.HIGHEST
full_turn = 2.0 * math.pi
root_half = math.sqrt(0.5)
density_norm = 1.0 / math.sqrt(2.0 * math.pi)

def phase_table(first, second, period):
    product = first[:, None] * second[None, :] % period
    angle = product.astype(jnp.float32) * (full_turn / period)
    return (jnp.cos(angle), jnp.sin(angle))

def lon_basis(columns, mode_count):
    cosine_part, sine_part = phase_table(jnp.arange(columns, dtype=jnp.int32), jnp.arange(mode_count, dtype=jnp.int32), columns)
    stacked = jnp.stack([cosine_part, -sine_part], axis=2) * columns ** (-0.5)
    return stacked.reshape(columns, 2 * mode_count)

def lat_basis(first, second, period, orient):
    cosine_part, sine_part = phase_table(first, second, period)
    upper_rows = jnp.stack([cosine_part, orient * sine_part], axis=-1)
    lower_rows = jnp.stack([-orient * sine_part, cosine_part], axis=-1)
    return jnp.stack([upper_rows, lower_rows], axis=1) * period ** (-0.5)

def gelu_parts(values):
    normal_cdf = 0.5 * (1.0 + lax.erf(values * root_half))
    return (values * normal_cdf, normal_cdf + values * jnp.exp(-0.5 * values * values) * density_norm)

def block_product(left_side, right_side, pattern):
    return jnp.einsum(pattern, left_side, right_side, precision=precise)

def complex_apply(values, matrix):
    pattern = 'pbi,bio->pbo'
    real_part = block_product(values[:, 0], matrix[0], pattern) - block_product(values[:, 1], matrix[1], pattern)
    imag_part = block_product(values[:, 0], matrix[1], pattern) + block_product(values[:, 1], matrix[0], pattern)
    return jnp.stack([real_part, imag_part], axis=1)

def complex_back(values, matrix):
    pattern = 'pbo,bio->pbi'
    real_part = block_product(values[:, 0], matrix[0], pattern) + block_product(values[:, 1], matrix[1], pattern)
    imag_part = block_product(values[:, 1], matrix[0], pattern) - block_product(values[:, 0], matrix[1], pattern)
    return jnp.stack([real_part, imag_part], axis=1)

def complex_outer(left_side, right_side):
    pattern = 'pbi,pbo->bio'
    real_part = block_product(left_side[:, 0], right_side[:, 0], pattern) + block_product(left_side[:, 1], right_side[:, 1], pattern)
    imag_part = block_product(left_side[:, 0], right_side[:, 1], pattern) - block_product(left_side[:, 1], right_side[:, 0], pattern)
    return jnp.stack([real_part, imag_part], axis=0)

def mlp_backward(spec_x, spec_g, mode_index, weight_in, bias_in, weight_out, scaling):
    point_count = spec_x.shape[0]
    blocks = weight_in.shape[1]
    inner_width = weight_in.shape[2]
    shaped_x = spec_x.reshape(point_count, 2, blocks, inner_width)
    shaped_g = spec_g.reshape(point_count, 2, blocks, inner_width)
    factor = jnp.where(mode_index == 0, 1.0, 2.0).astype(jnp.float32)
    grad_out = shaped_g * factor[:, None, None, None]
    pre_act = complex_apply(shaped_x, weight_in) + bias_in[None]
    hidden, slopes = gelu_parts(pre_act)
    grad_hidden = complex_back(grad_out, weight_out)
    grad_pre = grad_hidden * slopes
    grad_spec = complex_back(grad_pre, weight_in)
    grad_w_in = complex_outer(shaped_x, grad_pre) * scaling
    grad_b_in = lax.optimization_barrier(jnp.sum(grad_pre, axis=0)) * scaling
    grad_w_out = complex_outer(hidden, grad_out) * scaling
    return (grad_spec.reshape(point_count, 2, blocks * inner_width), grad_w_in, grad_b_in, grad_w_out)

def reference(features, cotangent, weight_in, bias_in, weight_out):
    lat_total, lon_total, channels = features.shape
    mode_total = MODES
    lon_table = lon_basis(lon_total, mode_total)
    every_row = jnp.arange(lat_total, dtype=jnp.int32)
    forward_table = lat_basis(every_row, every_row, lat_total, 1.0)
    inverse_table = lat_basis(every_row, every_row, lat_total, -1.0)

    def lon_forward(field):

        def one_row(row_data):
            return jnp.einsum('wc,wk->kc', row_data.astype(jnp.float32), lon_table, precision=precise)
        return lax.map(one_row, field).reshape(lat_total, mode_total, 2, channels)

    def lat_forward(spread):
        return jnp.einsum('kphq,hmqc->kmpc', forward_table, spread, precision=precise)
    group_points = LAT_DEV * mode_total
    spec_x = lat_forward(lon_forward(features)).reshape(N_LAT, group_points, 2, channels)
    spec_g = lat_forward(lon_forward(cotangent)).reshape(N_LAT, group_points, 2, channels)
    group_modes = jnp.arange(group_points, dtype=jnp.int32) % mode_total
    scaling = (lat_total * mode_total) ** (-0.5)

    def accumulate(totals, group_data):
        spec_part, cot_part = group_data
        grad_spec, grad_w_in, grad_b_in, grad_w_out = mlp_backward(spec_part, cot_part, group_modes, weight_in, bias_in, weight_out, scaling)
        return ((totals[0] + grad_w_in, totals[1] + grad_b_in, totals[2] + grad_w_out), grad_spec)
    start = (jnp.zeros(weight_in.shape, jnp.float32), jnp.zeros(bias_in.shape, jnp.float32), jnp.zeros(weight_out.shape, jnp.float32))
    totals, grad_spec = lax.scan(accumulate, start, (spec_x, spec_g))
    grad_spec = grad_spec.reshape(lat_total, mode_total, 2, channels)
    returning = jnp.einsum('kphq,hmqc->kmpc', inverse_table, grad_spec, precision=precise)
    returning = returning.reshape(lat_total, 2 * mode_total, channels)

    def synth_row(pair_data):
        spectrum_row, cot_row = pair_data
        summed_row = cot_row.astype(jnp.float32) + jnp.einsum('kc,wk->wc', spectrum_row, lon_table, precision=precise)
        return summed_row.astype(jnp.bfloat16)
    grad_features = lax.map(synth_row, (returning, cotangent))
    return (grad_features, totals[0], totals[1], totals[2])
```

```python
import functools
import math

import jax
import jax.numpy as jnp
import ml_dtypes
import numpy as np
from jax import lax
from jax.experimental import pallas as pl
from jax.experimental.pallas import tpu as pltpu
from jax.sharding import PartitionSpec as P

MODE_DEV = 4
PAD = 16
HALF = PAD // 2
POWER = 13.0
TOP = 2.0**9
VMEM = 40 * 2**20

root_half = math.sqrt(0.5)
density_norm = 1.0 / math.sqrt(2.0 * math.pi)


def halves(table):
    table = table.astype(np.float32)
    high = table.astype(ml_dtypes.bfloat16)
    low = (table - high.astype(np.float32)).astype(ml_dtypes.bfloat16)
    return high, low


def lon_table(columns, mode_count):
    product = np.arange(columns)[:, None] * np.arange(mode_count)[None, :] % columns
    angle = product * (2.0 * math.pi / columns)
    stacked = np.stack([np.cos(angle), -np.sin(angle)], axis=2) * columns**-0.5
    return stacked.reshape(columns, 2 * mode_count)


def lon_tables(blocks, inner, cols):
    modes = MODE_DEV * blocks
    table = lon_table(blocks * inner * cols, modes * inner)
    table = table.reshape(blocks, inner, cols, inner, 2 * modes)
    table = np.pad(table, ((0, 0), (0, 0), (0, PAD - cols), (0, 0), (0, 0)))
    forward = table.transpose(3, 1, 4, 0, 2).reshape(inner, inner, 2 * modes, blocks * PAD)
    split = table.reshape(blocks, inner, 2, HALF, inner, 2 * modes)
    synth = split.transpose(1, 4, 2, 0, 3, 5).reshape(inner, inner, 2 * blocks * HALF, 2 * modes)
    high, low = halves(forward)
    return np.concatenate([high, low], axis=2), *halves(synth)


def lat_table(rows, lat_count, group):
    total = rows * lat_count
    product = np.arange(total)[:, None] * np.arange(total)[None, :] % total
    angle = product * (2.0 * math.pi / total)
    c, s = np.cos(angle), np.sin(angle)
    basis = np.stack([np.stack([c, s], -1), np.stack([-s, c], -1)], axis=0) * total**-0.5
    basis = basis.reshape(2, total, lat_count, rows // 2, 2, 2).transpose(0, 1, 2, 4, 3, 5)
    size = 2 * total * group
    return np.einsum("akxhqb,mn->akmxhqnb", basis, np.eye(group)).reshape(size, size)


def split(values):
    high = values.astype(jnp.bfloat16)
    return high, (values - high.astype(jnp.float32)).astype(jnp.bfloat16)


def dot(left, right, dims=((1,), (0,))):
    return lax.dot_general(left, right, (dims, ((), ())), preferred_element_type=jnp.float32)


def dot3(left, right, dims=((1,), (0,))):
    return dot(left[0], right[0], dims) + (dot(left[0], right[1], dims) + dot(left[1], right[0], dims))


def scaled(values, top):
    level = jnp.maximum(top, 1e-30).astype(jnp.bfloat16).astype(jnp.float32)
    return values * (TOP / level), level


def encode(values):
    square = values * values
    fourth = square * square
    return (values * fourth * (fourth * fourth)).astype(jnp.bfloat16)


def decode(coded):
    coded = coded.astype(jnp.float32)
    size = jnp.abs(coded)
    root = jnp.exp(jnp.log(jnp.maximum(size, 1e-37)) * (1.0 / POWER))
    root = jnp.where(size > 0.0, root, 0.0)
    return jnp.where(coded < 0.0, -root, root)


def call(kernel, scalars, inputs, outputs, specs=None, scratch=(), flops=0):
    def full(shape):
        return pl.BlockSpec(shape, lambda i, s: (0,) * len(shape))

    specs = specs or {}
    in_specs = [specs.get(n, full(x.shape)) for n, x in enumerate(inputs)]
    out_specs = [full(o.shape) for o in outputs]
    moved = sum(math.prod(x.shape) * x.dtype.itemsize for x in (*inputs, *outputs))
    return pl.pallas_call(
        kernel,
        grid_spec=pltpu.PrefetchScalarGridSpec(
            num_scalar_prefetch=1,
            grid=(1,),
            in_specs=in_specs,
            out_specs=out_specs,
            scratch_shapes=list(scratch),
        ),
        out_shape=list(outputs),
        compiler_params=pltpu.CompilerParams(vmem_limit_bytes=VMEM),
        cost_estimate=pl.CostEstimate(flops=flops, bytes_accessed=moved, transcendentals=0),
    )(scalars, *inputs)


def pack_kernel(width, place_ref, x_ref, g_ref, out_ref):
    rows, cols, channels = x_ref.shape
    blocks = channels // width
    for q in range(rows // 2):
        lanes = [ref[2 * q + h].astype(jnp.float32) for h in range(2) for ref in (x_ref, g_ref)]
        lanes = [jnp.pad(x, ((0, PAD - cols), (0, 0))) for x in lanes]
        for b in range(blocks):
            pieces = [x[:, b * width : (b + 1) * width] for x in lanes]
            out_ref[b, q * PAD : (q + 1) * PAD, :] = jnp.concatenate(pieces, axis=1).astype(jnp.bfloat16)


def lon_kernel(inner, place_ref, table_ref, *refs):
    fields, (coded_ref, spec_ref) = refs[:inner], refs[inner:]
    member = place_ref[1]
    pairs, modes, lanes = spec_ref.shape
    blocks = fields[0].shape[0]
    tops = []
    for q in range(pairs):
        total = None
        for s, field in enumerate(fields):
            source = lax.rem(member - s + inner, inner)
            data = field[:, q * PAD : (q + 1) * PAD, :].reshape(blocks * PAD, lanes)
            term = dot(table_ref[0, source], data)
            total = term if total is None else total + term
        spec = total[:modes] + total[modes:]
        spec_ref[q] = spec
        tops.append(jnp.max(jnp.abs(spec), axis=0, keepdims=True))
    values, level = scaled(spec_ref[...], functools.reduce(jnp.maximum, tops))
    coded_ref[: pairs * modes, :] = encode(values).reshape(pairs * modes, lanes)
    coded_ref[pairs * modes :, :] = jnp.broadcast_to(level, (PAD, lanes)).astype(jnp.bfloat16)


def mlp_kernel(lat, inner, pairs, scaling, place_ref, *refs):
    spec_refs = refs[:lat]
    l_high, l_low, t_high, t_low, win_ref, bin_ref, wout_ref = refs[lat : lat + 7]
    back_ref, keep_ref, *rest = refs[lat + 7 :]
    send_refs, (z_ref, w_ref) = rest[: inner - 1], rest[inner - 1 :]
    place, member, x = place_ref[0], place_ref[1], place_ref[2]
    modes = (spec_refs[0].shape[0] - PAD) // pairs
    width = win_ref.shape[2]
    wide = 2 * width
    band = modes // lat
    group = band // 2
    size = l_high.shape[0]
    points = size // 2
    part = size // lat

    for s, ref in enumerate(spec_refs):
        source = lax.rem(x - s + lat, lat)
        start = pl.multiple_of(source * part, part)
        level = ref[pairs * modes :, :].astype(jnp.float32)[:1] * (1.0 / TOP)
        for q in range(pairs):
            values = decode(ref[q * modes : (q + 1) * modes, :]) * level
            for n in range(lat):
                for h in range(2):
                    row = start + (h * pairs + q) * band
                    piece = values[n * band : (n + 1) * band, h * wide : (h + 1) * wide]
                    z_ref[n, pl.ds(pl.multiple_of(row, 8), band), :] = piece

    def real_form(ref):
        re, im = ref[0, 0], ref[1, 0]
        return split(
            jnp.concatenate([jnp.concatenate([re, im], axis=1), jnp.concatenate([-im, re], axis=1)], axis=0)
        )

    m_in, m_out = real_form(win_ref), real_form(wout_ref)
    bias = jnp.concatenate([bin_ref[0, pl.ds(place, 1), :], bin_ref[1, pl.ds(place, 1), :]], axis=1)
    table = (l_high[...], l_low[...])
    inverse = (t_high[0], t_low[0])
    local = lax.broadcasted_iota(jnp.int32, (points, 1), 0) & (group - 1)
    sums = [None, None, None]
    for n in range(lat):
        spectra = dot3(table, split(z_ref[n]))
        spec_x = jnp.concatenate([spectra[:points, :width], spectra[points:, :width]], axis=1)
        spec_g = jnp.concatenate([spectra[:points, width:], spectra[points:, width:]], axis=1)
        first = (local + (member * (modes // 2) + n * group)) == 0
        grad_out = spec_g * jnp.where(first, 1.0, 2.0)
        x_parts, g_parts = split(spec_x), split(grad_out)
        pre = dot3(x_parts, m_in) + bias
        cdf = 0.5 * (1.0 + lax.erf(pre * root_half))
        hidden = pre * cdf
        slopes = cdf + pre * jnp.exp(-0.5 * pre * pre) * density_norm
        grad_pre = dot3(g_parts, m_out, ((1,), (1,))) * slopes
        p_parts = split(grad_pre)
        grad_spec = dot3(p_parts, m_in, ((1,), (1,)))
        stacked = jnp.concatenate([grad_spec[:, :width], grad_spec[:, width:]], axis=0)
        back = dot3(inverse, split(stacked))
        for q in range(pairs):
            pieces = [back[(h * pairs + q) * band : (h * pairs + q + 1) * band] for h in range(2)]
            back_ref[q, n * band : (n + 1) * band, :] = jnp.concatenate(pieces, axis=1)
        terms = (
            dot3(x_parts, p_parts, ((0,), (0,))),
            dot3(split(hidden), g_parts, ((0,), (0,))),
            jnp.sum(grad_pre, axis=0, keepdims=True),
        )
        sums = [t if a is None else a + t for a, t in zip(sums, terms)]

    pieces = []
    for total in sums[:2]:
        pieces.append(total[:width, :width] + total[width:, width:])
        pieces.append(total[:width, width:] - total[width:, :width])
    weights = jnp.concatenate(pieces, axis=1) * scaling
    share = width // inner
    w_ref[...] = jnp.zeros_like(w_ref)
    for n in range(inner):
        w_ref[n, :share, :] = weights[n * share : (n + 1) * share]
    w_ref[0, share : share + 1, :wide] = sums[2] * scaling
    keep_ref[...] = w_ref[member]
    for s in range(1, inner):
        send_refs[s - 1][...] = w_ref[lax.rem(member + s, inner)]


def synth_kernel(inner, place_ref, high_ref, low_ref, *refs):
    backs, sums, (out_ref, wide_ref) = refs[:inner], refs[inner : 2 * inner], refs[2 * inner :]
    member = place_ref[1]
    pairs, modes, lanes = backs[0].shape
    blocks, total_rows, wide = out_ref.shape
    data_rows = pairs * HALF
    for q in range(pairs):
        total = None
        for s, back in enumerate(backs):
            source = lax.rem(member - s + inner, inner)
            term = dot3((high_ref[0, source], low_ref[0, source]), split(back[q]))
            total = term if total is None else total + term
        part = blocks * HALF
        columns = jnp.concatenate([total[:part], total[part:]], axis=1)
        wide_ref[:, q * HALF : (q + 1) * HALF, :] = columns.reshape(blocks, HALF, wide)
    weights = sums[0][...]
    for ref in sums[1:]:
        weights = weights + ref[...]

    top_w = jnp.max(jnp.abs(weights), axis=0, keepdims=True)
    weights, level_w = scaled(weights, top_w)
    columns = wide_ref[:, :data_rows, :]
    top = jnp.max(jnp.max(jnp.abs(columns), axis=0), axis=0, keepdims=True)
    columns, level = scaled(columns, top)
    sum_rows = weights.shape[0]
    place_row = lax.broadcasted_iota(jnp.int32, (sum_rows, 1), 0)
    tail = jnp.where(place_row == sum_rows - 2, level_w, encode(weights).astype(jnp.float32))
    tail = jnp.where(place_row == sum_rows - 1, level, tail)
    coded = encode(columns).astype(jnp.float32)
    for b in range(blocks):
        out_ref[b] = jnp.concatenate([coded[b], tail], axis=0).astype(jnp.bfloat16)


def columns_kernel(place_ref, data_ref, cot_ref, out_ref):
    rows, cols, _ = cot_ref.shape
    blocks, total_rows, wide = data_ref.shape
    width = wide // 4
    pairs = rows // 2
    top = -(-pairs * HALF // 16) * 16
    values = []
    for b in range(blocks):
        level = data_ref[b, total_rows - 16 :, :].astype(jnp.float32)[15:16]
        values.append(decode(data_ref[b, :top, :]) * (level * (1.0 / TOP)))
    for q in range(pairs):
        for h in range(2):
            parts = []
            for half in range(2):
                start = (2 * half + h) * width
                pieces = [v[q * HALF : (q + 1) * HALF, start : start + width] for v in values]
                parts.append(jnp.concatenate(pieces, axis=1))
            column = jnp.concatenate(parts, axis=0)[:cols]
            row = 2 * q + h
            out_ref[row] = (cot_ref[row].astype(jnp.float32) + column).astype(jnp.bfloat16)


def weights_kernel(inner, data_rows, place_ref, *refs):
    pieces, (win_ref, bin_ref, wout_ref) = refs[:inner], refs[inner:]
    member = place_ref[1]
    blocks, total_rows, wide = pieces[0].shape
    width = wide // 4
    share = width // inner
    base = data_rows // 16 * 16
    skip = data_rows - base
    for b in range(blocks):
        held = []
        for ref in pieces:
            raw = ref[b, base:, :]
            level = raw.astype(jnp.float32)[total_rows - base - 2 : total_rows - base - 1]
            held.append(decode(raw)[skip:] * (level * (1.0 / TOP)))
        for n in range(inner):
            part = held[0]
            for s in range(1, inner):
                part = jnp.where(lax.rem(member - s + inner, inner) == n, held[s], part)
            for i, (ref, k) in enumerate(((win_ref, 0), (win_ref, 1), (wout_ref, 0), (wout_ref, 1))):
                ref[k, b, n * share : (n + 1) * share, :] = part[:share, i * width : (i + 1) * width]
            if n == 0:
                for k in range(2):
                    bin_ref[k, b : b + 1, :] = part[share : share + 1, k * width : (k + 1) * width]


def body(features, cotangent, weight_in, bias_in, weight_out):
    lon_count, lat_count = lax.axis_size("lon"), lax.axis_size("lat")
    blocks, width = weight_in.shape[1:3]
    rows, cols, _ = features.shape
    inner = lon_count // blocks
    pairs = rows // 2
    wide = 4 * width
    modes = 2 * MODE_DEV * blocks
    group = modes // 2 // lat_count
    size = 2 * rows * lat_count * group
    lon_place = lax.axis_index("lon")
    lat_place = lax.axis_index("lat")
    scalars = jnp.stack([lon_place // inner, lon_place % inner, lat_place]).astype(jnp.int32)
    scaling = (rows * lat_count * modes // 2 * inner) ** -0.5
    forward, synth_high, synth_low = lon_tables(blocks, inner, cols)
    table = lat_table(rows, lat_count, group)
    l_high, l_low = halves(table)
    t_high, t_low = halves(table.T.reshape(lat_count, size // lat_count, size))
    share = width // inner
    total_rows = -(-(pairs * HALF + share + 1 + 2) // 16) * 16
    sum_rows = total_rows - pairs * HALF
    f32, bf16 = jnp.float32, jnp.bfloat16
    shape = jax.ShapeDtypeStruct

    places = [[g * inner + i for g in range(blocks)] for i in range(inner)]

    def exchange(values):
        return lax.all_to_all(
            values, "lon", split_axis=0, concat_axis=0, tiled=True, axis_index_groups=places
        )

    def to_member(values, step):
        turn = [(i, i // inner * inner + (i + step) % inner) for i in range(lon_count)]
        return lax.ppermute(values, "lon", turn)

    def to_lat(values, step):
        return lax.ppermute(values, "lat", [(i, (i + step) % lat_count) for i in range(lat_count)])

    def member_block(array):
        rest = array.shape[1:]
        return pl.BlockSpec((1, *rest), lambda i, s: (s[1],) + (0,) * len(rest))

    (packed,) = call(
        functools.partial(pack_kernel, width),
        scalars,
        (features, cotangent),
        (shape((blocks, pairs * PAD, wide), bf16),),
    )
    arrived = exchange(packed)
    fields = [arrived] + [to_member(arrived, s) for s in range(1, inner)]
    (coded,) = call(
        functools.partial(lon_kernel, inner),
        scalars,
        (forward, *fields),
        (shape((pairs * modes + PAD, wide), bf16),),
        specs={0: member_block(forward)},
        scratch=(pltpu.VMEM((pairs, modes, wide), f32),),
    )
    spectra = [coded] + [to_lat(coded, s) for s in range(1, lat_count)]
    n = lat_count
    lat_block = pl.BlockSpec((1, *t_high.shape[1:]), lambda i, s: (s[2], 0, 0))
    block_spec = pl.BlockSpec((2, 1, width, width), lambda i, s: (0, s[0], 0, 0))
    back, keep, *send = call(
        functools.partial(mlp_kernel, lat_count, inner, pairs, scaling),
        scalars,
        (*spectra, l_high, l_low, t_high, t_low, weight_in, bias_in, weight_out),
        (shape((pairs, modes, 2 * width), f32), *[shape((sum_rows, wide), f32)] * inner),
        specs={n + 2: lat_block, n + 3: lat_block, n + 4: block_spec, n + 6: block_spec},
        scratch=(
            pltpu.VMEM((lat_count, size, 2 * width), f32),
            pltpu.VMEM((inner, sum_rows, wide), f32),
        ),
    )
    backs = [back] + [to_member(back, s) for s in range(1, inner)]
    sums = [keep] + [to_member(send[s - 1], s) for s in range(1, inner)]
    (payload,) = call(
        functools.partial(synth_kernel, inner),
        scalars,
        (synth_high, synth_low, *backs, *sums),
        (shape((blocks, total_rows, wide), bf16),),
        specs={0: member_block(synth_high), 1: member_block(synth_low)},
        scratch=(pltpu.VMEM((blocks, pairs * HALF, wide), f32),),
    )
    returned = exchange(payload)
    gathered = [returned] + [to_member(returned, s) for s in range(1, inner)]
    (grad_features,) = call(
        columns_kernel, scalars, (returned, cotangent), (shape(features.shape, bf16),)
    )
    grad_w_in, grad_b_in, grad_w_out = call(
        functools.partial(weights_kernel, inner, pairs * HALF),
        scalars,
        gathered,
        (shape(weight_in.shape, f32), shape(bias_in.shape, f32), shape(weight_out.shape, f32)),
    )
    return grad_features, grad_w_in, grad_b_in, grad_w_out


def solution(mesh):
    placed = (P("lat", "lon", None), P("lat", "lon", None), P(), P(), P())
    return jax.shard_map(
        body,
        mesh=mesh,
        in_specs=placed,
        out_specs=(P("lat", "lon", None), P(), P(), P()),
        check_vma=False,
    )
```

```python
import functools
import math

import jax
import jax.numpy as jnp
import ml_dtypes
import numpy as np
from jax import lax
from jax.experimental import pallas as pl
from jax.experimental.pallas import tpu as pltpu
from jax.sharding import PartitionSpec as P

MODE_DEV = 4
PAD = 16
HALF = PAD // 2
SUB = 4
POWER = 13.0
TOP = 2.0**9
VMEM = 40 * 2**20

root_half = math.sqrt(0.5)
density_norm = 1.0 / math.sqrt(2.0 * math.pi)


def halves(table):
    table = table.astype(np.float32)
    high = table.astype(ml_dtypes.bfloat16)
    low = (table - high.astype(np.float32)).astype(ml_dtypes.bfloat16)
    return high, low


def lon_table(columns, mode_count):
    product = np.arange(columns)[:, None] * np.arange(mode_count)[None, :] % columns
    angle = product * (2.0 * math.pi / columns)
    stacked = np.stack([np.cos(angle), -np.sin(angle)], axis=2) * columns**-0.5
    return stacked.reshape(columns, 2 * mode_count)


def lon_tables(blocks, inner, cols):
    modes = MODE_DEV * blocks
    table = lon_table(blocks * inner * cols, modes * inner)
    table = table.reshape(blocks, inner, cols, inner, 2 * modes)
    table = np.pad(table, ((0, 0), (0, 0), (0, PAD - cols), (0, 0), (0, 0)))
    forward = table.transpose(3, 1, 4, 0, 2).reshape(inner, inner, 2 * modes, blocks * PAD)
    split = table.reshape(blocks, inner, 2, HALF, inner, 2 * modes)
    synth = split.transpose(1, 4, 2, 0, 3, 5).reshape(inner, inner, 2 * blocks * HALF, 2 * modes)
    high, low = halves(forward)
    return np.concatenate([high, low], axis=2), *halves(synth)


def lat_table(rows, lat_count, group):
    total = rows * lat_count
    product = np.arange(total)[:, None] * np.arange(total)[None, :] % total
    angle = product * (2.0 * math.pi / total)
    c, s = np.cos(angle), np.sin(angle)
    basis = np.stack([np.stack([c, s], -1), np.stack([-s, c], -1)], axis=0) * total**-0.5
    basis = basis.reshape(2, total, lat_count, rows // 2, 2, 2).transpose(0, 1, 2, 4, 3, 5)
    size = 2 * total * group
    return np.einsum("akxhqb,mn->akmxhqnb", basis, np.eye(group)).reshape(size, size)


def split(values):
    high = values.astype(jnp.bfloat16)
    return high, (values - high.astype(jnp.float32)).astype(jnp.bfloat16)


def dot(left, right, dims=((1,), (0,))):
    return lax.dot_general(left, right, (dims, ((), ())), preferred_element_type=jnp.float32)


def dot3(left, right, dims=((1,), (0,))):
    return dot(left[0], right[0], dims) + (dot(left[0], right[1], dims) + dot(left[1], right[0], dims))


def scaled(values, top):
    level = jnp.maximum(top, 1e-30).astype(jnp.bfloat16).astype(jnp.float32)
    return values * (TOP / level), level


def encode(values):
    square = values * values
    fourth = square * square
    return (values * fourth * (fourth * fourth)).astype(jnp.bfloat16)


def decode(coded):
    coded = coded.astype(jnp.float32)
    size = jnp.abs(coded)
    root = jnp.exp(jnp.log(jnp.maximum(size, 1e-37)) * (1.0 / POWER))
    root = jnp.where(size > 0.0, root, 0.0)
    return jnp.where(coded < 0.0, -root, root)


def call(kernel, scalars, inputs, outputs, specs=None, scratch=(), flops=0):
    def full(shape):
        return pl.BlockSpec(shape, lambda i, s: (0,) * len(shape))

    specs = specs or {}
    in_specs = [specs.get(n, full(x.shape)) for n, x in enumerate(inputs)]
    out_specs = [full(o.shape) for o in outputs]
    moved = sum(math.prod(x.shape) * x.dtype.itemsize for x in (*inputs, *outputs))
    return pl.pallas_call(
        kernel,
        grid_spec=pltpu.PrefetchScalarGridSpec(
            num_scalar_prefetch=1,
            grid=(1,),
            in_specs=in_specs,
            out_specs=out_specs,
            scratch_shapes=list(scratch),
        ),
        out_shape=list(outputs),
        compiler_params=pltpu.CompilerParams(vmem_limit_bytes=VMEM),
        cost_estimate=pl.CostEstimate(flops=flops, bytes_accessed=moved, transcendentals=0),
    )(scalars, *inputs)


def pack_kernel(width, place_ref, x_hbm, g_hbm, table_hbm, out_ref, table_ref, x_ref, g_ref, sems, table_sem):
    rows, cols, channels = x_ref.shape
    blocks = channels // width
    pairs = rows // 2

    def fetch(q, n):
        source, target = ((x_hbm, x_ref), (g_hbm, g_ref))[n]
        part = pl.ds(2 * q, 2)
        return pltpu.make_async_copy(source.at[part], target.at[part], sems.at[n, q])

    for q in range(pairs):
        for n in range(2):
            fetch(q, n).start()
    table = pltpu.make_async_copy(table_hbm.at[place_ref[1]], table_ref, table_sem)
    table.start()
    for q in range(pairs):
        for n in range(2):
            fetch(q, n).wait()
        lanes = [ref[2 * q + h].astype(jnp.float32) for h in range(2) for ref in (x_ref, g_ref)]
        lanes = [jnp.pad(x, ((0, PAD - cols), (0, 0))) for x in lanes]
        for b in range(blocks):
            pieces = [x[:, b * width : (b + 1) * width] for x in lanes]
            out_ref[b, q * PAD : (q + 1) * PAD, :] = jnp.concatenate(pieces, axis=1).astype(jnp.bfloat16)
    table.wait()


def lon_kernel(inner, place_ref, table_ref, *refs):
    fields, (coded_ref, spec_ref) = refs[:inner], refs[inner:]
    member = place_ref[1]
    pairs, modes, lanes = spec_ref.shape
    blocks = fields[0].shape[0]
    tops = []
    for q in range(pairs):
        total = None
        for s, field in enumerate(fields):
            source = lax.rem(member - s + inner, inner)
            data = field[:, q * PAD : (q + 1) * PAD, :].reshape(blocks * PAD, lanes)
            term = dot(table_ref[source], data)
            total = term if total is None else total + term
        spec = total[:modes] + total[modes:]
        spec_ref[q] = spec
        tops.append(jnp.max(jnp.abs(spec), axis=0, keepdims=True))
    values, level = scaled(spec_ref[...], functools.reduce(jnp.maximum, tops))
    coded_ref[: pairs * modes, :] = encode(values).reshape(pairs * modes, lanes)
    coded_ref[pairs * modes :, :] = jnp.broadcast_to(level, (PAD, lanes)).astype(jnp.bfloat16)


def lat_rows(ref, pairs):
    modes = (ref.shape[0] - PAD) // pairs
    wide = ref.shape[1] // 2
    tile = 2 * SUB
    level = ref[pairs * modes :, :].astype(jnp.float32)[:1] * (1.0 / TOP)
    values = [decode(ref[q * modes : (q + 1) * modes, :]) * level for q in range(pairs)]
    rows = []
    for h in range(2):
        for q in range(pairs):
            parts = [
                values[q][n * tile : (n + 1) * tile, h * wide : (h + 1) * wide] for n in range(modes // tile)
            ]
            rows.append(jnp.concatenate(parts, axis=1))
    return jnp.concatenate(rows, axis=0)


def ready_kernel(pairs, place_ref, spec_ref, l_high, l_low, win_ref, bin_ref, wout_ref, *outs):
    part_ref, form_ref, bias_ref = outs
    place, x = place_ref[0], place_ref[2]
    for n, ref in enumerate((win_ref, wout_ref)):
        re, im = ref[0, 0], ref[1, 0]
        form = jnp.concatenate([jnp.concatenate([re, im], axis=1), jnp.concatenate([-im, re], axis=1)], axis=0)
        form_ref[2 * n], form_ref[2 * n + 1] = split(form)
    bias = jnp.concatenate([bin_ref[0, pl.ds(place, 1), :], bin_ref[1, pl.ds(place, 1), :]], axis=1)
    bias_ref[...] = jnp.broadcast_to(bias, bias_ref.shape)
    part_ref[...] = dot3((l_high[x], l_low[x]), split(lat_rows(spec_ref, pairs)))


def mlp_kernel(lat, inner, pairs, scaling, place_ref, *refs):
    others = refs[: lat - 1]
    part_ref, form_ref, bias_ref, l_high, l_low, t_high, t_low = refs[lat - 1 : lat + 6]
    back_ref, keep_ref, *rest = refs[lat + 6 :]
    send_refs, (w_ref,) = rest[: inner - 1], rest[inner - 1 :]
    member, x = place_ref[1], place_ref[2]
    wide = form_ref.shape[1]
    width = wide // 2
    tile = 2 * SUB
    points = l_high.shape[1] // 2
    subs = part_ref.shape[1] // wide

    spectra = part_ref[...]
    for s, ref in enumerate(others):
        source = lax.rem(x - s - 1 + lat, lat)
        spectra = spectra + dot3((l_high[source], l_low[source]), split(lat_rows(ref, pairs)))

    def of_points(start):
        rows = []
        for n in range(subs):
            lanes = slice(n * wide + start, n * wide + start + width)
            rows.append(jnp.concatenate([spectra[:points, lanes], spectra[points:, lanes]], axis=1))
        return jnp.concatenate(rows, axis=0)

    spec_x, spec_g = of_points(0), of_points(width)
    m_in, m_out = (form_ref[0], form_ref[1]), (form_ref[2], form_ref[3])
    point = lax.broadcasted_iota(jnp.int32, (subs * points, 1), 0)
    first = ((point & (SUB - 1)) + jnp.where(point < points, 0, SUB) + member * SUB) == 0
    grad_out = spec_g * jnp.where(first, 1.0, 2.0)
    x_parts, g_parts = split(spec_x), split(grad_out)
    pre = dot3(x_parts, m_in) + bias_ref[:1]
    cdf = 0.5 * (1.0 + lax.erf(pre * root_half))
    hidden = pre * cdf
    slopes = cdf + pre * jnp.exp(-0.5 * pre * pre) * density_norm
    grad_pre = dot3(g_parts, m_out, ((1,), (1,))) * slopes
    p_parts = split(grad_pre)
    grad_spec = dot3(p_parts, m_in, ((1,), (1,)))
    lanes = []
    for n in range(subs):
        piece = grad_spec[n * points : (n + 1) * points]
        lanes.append(jnp.concatenate([piece[:, :width], piece[:, width:]], axis=0))
    back = dot3((t_high[0], t_low[0]), split(jnp.concatenate(lanes, axis=1)))
    for q in range(pairs):
        for n in range(subs):
            pieces = [
                back[(h * pairs + q) * tile : (h * pairs + q + 1) * tile, n * width : (n + 1) * width]
                for h in range(2)
            ]
            back_ref[q, n * tile : (n + 1) * tile, :] = jnp.concatenate(pieces, axis=1)

    pieces = []
    for left, right in ((x_parts, p_parts), (split(hidden), g_parts)):
        total = dot3(left, right, ((0,), (0,)))
        pieces.append(total[:width, :width] + total[width:, width:])
        pieces.append(total[:width, width:] - total[width:, :width])
    weights = jnp.concatenate(pieces, axis=1) * scaling
    share = width // inner
    w_ref[...] = jnp.zeros_like(w_ref)
    for n in range(inner):
        w_ref[n, :share, :] = weights[n * share : (n + 1) * share]
    w_ref[0, share : share + 1, :wide] = jnp.sum(grad_pre, axis=0, keepdims=True) * scaling
    keep_ref[...] = w_ref[member]
    for s in range(1, inner):
        send_refs[s - 1][...] = w_ref[lax.rem(member + s, inner)]


def synth_kernel(inner, place_ref, high_ref, low_ref, *refs):
    backs, sums, (out_ref, wide_ref) = refs[:inner], refs[inner : 2 * inner], refs[2 * inner :]
    member = place_ref[1]
    pairs, modes, lanes = backs[0].shape
    blocks, total_rows, wide = out_ref.shape
    data_rows = pairs * HALF
    for q in range(pairs):
        total = None
        for s, back in enumerate(backs):
            source = lax.rem(member - s + inner, inner)
            term = dot3((high_ref[0, source], low_ref[0, source]), split(back[q]))
            total = term if total is None else total + term
        part = blocks * HALF
        columns = jnp.concatenate([total[:part], total[part:]], axis=1)
        wide_ref[:, q * HALF : (q + 1) * HALF, :] = columns.reshape(blocks, HALF, wide)
    weights = sums[0][...]
    for ref in sums[1:]:
        weights = weights + ref[...]

    top_w = jnp.max(jnp.abs(weights), axis=0, keepdims=True)
    weights, level_w = scaled(weights, top_w)
    columns = wide_ref[:, :data_rows, :]
    top = jnp.max(jnp.max(jnp.abs(columns), axis=0), axis=0, keepdims=True)
    columns, level = scaled(columns, top)
    sum_rows = weights.shape[0]
    place_row = lax.broadcasted_iota(jnp.int32, (sum_rows, 1), 0)
    tail = jnp.where(place_row == sum_rows - 2, level_w, encode(weights).astype(jnp.float32))
    tail = jnp.where(place_row == sum_rows - 1, level, tail)
    coded = encode(columns).astype(jnp.float32)
    for b in range(blocks):
        out_ref[b] = jnp.concatenate([coded[b], tail], axis=0).astype(jnp.bfloat16)


def columns_kernel(place_ref, data_ref, cot_ref, out_ref):
    rows, cols, _ = cot_ref.shape
    blocks, total_rows, wide = data_ref.shape
    width = wide // 4
    pairs = rows // 2
    top = -(-pairs * HALF // 16) * 16
    values = []
    for b in range(blocks):
        level = data_ref[b, total_rows - 16 :, :].astype(jnp.float32)[15:16]
        values.append(decode(data_ref[b, :top, :]) * (level * (1.0 / TOP)))
    for q in range(pairs):
        for h in range(2):
            parts = []
            for half in range(2):
                start = (2 * half + h) * width
                pieces = [v[q * HALF : (q + 1) * HALF, start : start + width] for v in values]
                parts.append(jnp.concatenate(pieces, axis=1))
            column = jnp.concatenate(parts, axis=0)[:cols]
            row = 2 * q + h
            out_ref[row] = (cot_ref[row].astype(jnp.float32) + column).astype(jnp.bfloat16)


def weights_kernel(inner, data_rows, place_ref, *refs):
    pieces, (win_ref, bin_ref, wout_ref) = refs[:inner], refs[inner:]
    member = place_ref[1]
    blocks, total_rows, wide = pieces[0].shape
    width = wide // 4
    share = width // inner
    base = data_rows // 16 * 16
    skip = data_rows - base
    for b in range(blocks):
        held = []
        for ref in pieces:
            raw = ref[b, base:, :]
            level = raw.astype(jnp.float32)[total_rows - base - 2 : total_rows - base - 1]
            held.append(decode(raw)[skip:] * (level * (1.0 / TOP)))
        for n in range(inner):
            part = held[0]
            for s in range(1, inner):
                part = jnp.where(lax.rem(member - s + inner, inner) == n, held[s], part)
            for i, (ref, k) in enumerate(((win_ref, 0), (win_ref, 1), (wout_ref, 0), (wout_ref, 1))):
                ref[k, b, n * share : (n + 1) * share, :] = part[:share, i * width : (i + 1) * width]
            if n == 0:
                for k in range(2):
                    bin_ref[k, b : b + 1, :] = part[share : share + 1, k * width : (k + 1) * width]


def body(features, cotangent, weight_in, bias_in, weight_out):
    lon_count, lat_count = lax.axis_size("lon"), lax.axis_size("lat")
    blocks, width = weight_in.shape[1:3]
    rows, cols, _ = features.shape
    inner = lon_count // blocks
    pairs = rows // 2
    wide = 4 * width
    modes = 2 * MODE_DEV * blocks
    size = 2 * rows * lat_count * SUB
    subs = modes // (2 * SUB)
    lon_place = lax.axis_index("lon")
    lat_place = lax.axis_index("lat")
    scalars = jnp.stack([lon_place // inner, lon_place % inner, lat_place]).astype(jnp.int32)
    scaling = (rows * lat_count * modes // 2 * inner) ** -0.5
    forward, synth_high, synth_low = lon_tables(blocks, inner, cols)
    table = lat_table(rows, lat_count, SUB)
    l_high, l_low = halves(table.reshape(size, lat_count, -1).transpose(1, 0, 2))
    t_high, t_low = halves(table.T.reshape(lat_count, size // lat_count, size))
    share = width // inner
    total_rows = -(-(pairs * HALF + share + 1 + 2) // 16) * 16
    sum_rows = total_rows - pairs * HALF
    f32, bf16 = jnp.float32, jnp.bfloat16
    shape = jax.ShapeDtypeStruct

    places = [[g * inner + i for g in range(blocks)] for i in range(inner)]

    def exchange(values):
        return lax.all_to_all(
            values, "lon", split_axis=0, concat_axis=0, tiled=True, axis_index_groups=places
        )

    def to_member(values, step):
        turn = [(i, i // inner * inner + (i + step) % inner) for i in range(lon_count)]
        return lax.ppermute(values, "lon", turn)

    def to_lat(values, step):
        return lax.ppermute(values, "lat", [(i, (i + step) % lat_count) for i in range(lat_count)])

    def member_block(array):
        rest = array.shape[1:]
        return pl.BlockSpec((1, *rest), lambda i, s: (s[1],) + (0,) * len(rest))

    in_hbm = pl.BlockSpec(memory_space=pltpu.HBM)
    field = pltpu.VMEM(features.shape, bf16)
    packed, lon_part = call(
        functools.partial(pack_kernel, width),
        scalars,
        (features, cotangent, forward),
        (shape((blocks, pairs * PAD, wide), bf16), shape(forward.shape[1:], bf16)),
        specs={0: in_hbm, 1: in_hbm, 2: in_hbm},
        scratch=(field, field, pltpu.SemaphoreType.DMA((2, pairs)), pltpu.SemaphoreType.DMA(())),
    )
    arrived = exchange(packed)
    fields = [arrived] + [to_member(arrived, s) for s in range(1, inner)]
    (coded,) = call(
        functools.partial(lon_kernel, inner),
        scalars,
        (lon_part, *fields),
        (shape((pairs * modes + PAD, wide), bf16),),
        scratch=(pltpu.VMEM((pairs, modes, wide), f32),),
    )
    others = [to_lat(coded, s) for s in range(1, lat_count)]
    block_spec = pl.BlockSpec((2, 1, width, width), lambda i, s: (0, s[0], 0, 0))
    part, forms, bias = call(
        functools.partial(ready_kernel, pairs),
        scalars,
        (coded, l_high, l_low, weight_in, bias_in, weight_out),
        (
            shape((size, 2 * subs * width), f32),
            shape((4, 2 * width, 2 * width), bf16),
            shape((8, 2 * width), f32),
        ),
        specs={3: block_spec, 5: block_spec},
        flops=6 * size * size // lat_count * 2 * subs * width,
    )
    n = lat_count - 1
    lat_block = pl.BlockSpec((1, *t_high.shape[1:]), lambda i, s: (s[2], 0, 0))
    back, keep, *send = call(
        functools.partial(mlp_kernel, lat_count, inner, pairs, scaling),
        scalars,
        (*others, part, forms, bias, l_high, l_low, t_high, t_low),
        (shape((pairs, modes, 2 * width), f32), *[shape((sum_rows, wide), f32)] * inner),
        specs={n + 5: lat_block, n + 6: lat_block},
        scratch=(pltpu.VMEM((inner, sum_rows, wide), f32),),
    )
    backs = [back] + [to_member(back, s) for s in range(1, inner)]
    sums = [keep] + [to_member(send[s - 1], s) for s in range(1, inner)]
    (payload,) = call(
        functools.partial(synth_kernel, inner),
        scalars,
        (synth_high, synth_low, *backs, *sums),
        (shape((blocks, total_rows, wide), bf16),),
        specs={0: member_block(synth_high), 1: member_block(synth_low)},
        scratch=(pltpu.VMEM((blocks, pairs * HALF, wide), f32),),
    )
    returned = exchange(payload)
    gathered = [returned] + [to_member(returned, s) for s in range(1, inner)]
    (grad_features,) = call(
        columns_kernel, scalars, (returned, cotangent), (shape(features.shape, bf16),)
    )
    grad_w_in, grad_b_in, grad_w_out = call(
        functools.partial(weights_kernel, inner, pairs * HALF),
        scalars,
        gathered,
        (shape(weight_in.shape, f32), shape(bias_in.shape, f32), shape(weight_out.shape, f32)),
    )
    return grad_features, grad_w_in, grad_b_in, grad_w_out


def solution(mesh):
    placed = (P("lat", "lon", None), P("lat", "lon", None), P(), P(), P())
    return jax.shard_map(
        body,
        mesh=mesh,
        in_specs=placed,
        out_specs=(P("lat", "lon", None), P(), P(), P()),
        check_vma=False,
    )
```

```python
import functools
import math

import jax
import jax.numpy as jnp
import ml_dtypes
import numpy as np
from jax import lax
from jax.experimental import pallas as pl
from jax.experimental.pallas import tpu as pltpu
from jax.sharding import PartitionSpec as P

MODE_DEV = 4
PAD = 16
HALF = PAD // 2
SUB = 4
SPARE = 6
POWER = 13.0
TOP = 2.0**9
VMEM = 40 * 2**20

root_half = math.sqrt(0.5)
density_norm = 1.0 / math.sqrt(2.0 * math.pi)


def halves(table):
    table = table.astype(np.float32)
    high = table.astype(ml_dtypes.bfloat16)
    low = (table - high.astype(np.float32)).astype(ml_dtypes.bfloat16)
    return high, low


def lon_table(columns, mode_count):
    product = np.arange(columns)[:, None] * np.arange(mode_count)[None, :] % columns
    angle = product * (2.0 * math.pi / columns)
    stacked = np.stack([np.cos(angle), -np.sin(angle)], axis=2) * columns**-0.5
    return stacked.reshape(columns, 2 * mode_count)


def lon_tables(blocks, inner, cols):
    modes = MODE_DEV * blocks
    table = lon_table(blocks * inner * cols, modes * inner)
    table = table.reshape(blocks, inner, cols, inner, 2 * modes)
    table = np.pad(table, ((0, 0), (0, 0), (0, PAD - cols), (0, 0), (0, 0)))
    forward = table.transpose(3, 1, 4, 0, 2).reshape(inner, inner, 2 * modes, blocks * PAD)
    split = table.reshape(blocks, inner, 2, HALF, inner, 2 * modes)
    synth = split.transpose(1, 4, 2, 0, 3, 5).reshape(inner, inner, 2 * blocks * HALF, 2 * modes)
    forward, synth = np.concatenate(halves(forward), axis=2), np.concatenate(halves(synth), axis=3)
    return forward.reshape(-1, blocks * PAD), synth.reshape(-1, 4 * modes)


def lat_table(rows, lat_count, group):
    total = rows * lat_count
    product = np.arange(total)[:, None] * np.arange(total)[None, :] % total
    angle = product * (2.0 * math.pi / total)
    c, s = np.cos(angle), np.sin(angle)
    basis = np.stack([np.stack([c, s], -1), np.stack([-s, c], -1)], axis=0) * total**-0.5
    basis = basis.reshape(2, total, lat_count, rows // 2, 2, 2).transpose(0, 1, 2, 4, 3, 5)
    size = 2 * total * group
    return np.einsum("akxhqb,mn->akmxhqnb", basis, np.eye(group)).reshape(size, size)


def all_tables(blocks, inner, cols, rows, lat_count):
    forward, synth = lon_tables(blocks, inner, cols)
    table = lat_table(rows, lat_count, SUB)
    size = table.shape[0]
    lat = np.concatenate(halves(table.reshape(size, lat_count, -1).transpose(1, 0, 2)), axis=1)
    parts = [forward, lat.reshape(2 * lat_count * size, -1), synth]
    lanes = max(p.shape[1] for p in parts)
    parts = [np.pad(p, ((0, 0), (0, lanes - p.shape[1]))) for p in parts]
    starts = np.cumsum([0] + [len(p) for p in parts])
    return np.concatenate(parts), [int(n) for n in starts]


def split(values):
    high = values.astype(jnp.bfloat16)
    return high, (values - high.astype(jnp.float32)).astype(jnp.bfloat16)


def dot(left, right, dims=((1,), (0,))):
    return lax.dot_general(left, right, (dims, ((), ())), preferred_element_type=jnp.float32)


def dot3(left, right, dims=((1,), (0,))):
    return dot(left[0], right[0], dims) + (dot(left[0], right[1], dims) + dot(left[1], right[0], dims))


def scaled(values, top):
    level = jnp.maximum(top, 1e-30).astype(jnp.bfloat16).astype(jnp.float32)
    return values * (TOP / level), level


def table_rows(ref, start, count, place):
    return ref[pl.ds(pl.multiple_of(start + place * count, PAD), count), :]


def lat_part(ref, start, size, part, x):
    rows = table_rows(ref, start, 2 * size, x)[:, :part]
    return rows[:size], rows[size:]


def encode(values):
    square = values * values
    fourth = square * square
    return (values * fourth * (fourth * fourth)).astype(jnp.bfloat16)


def decode(coded):
    coded = coded.astype(jnp.float32)
    size = jnp.abs(coded)
    root = jnp.exp(jnp.log(jnp.maximum(size, 1e-37)) * (1.0 / POWER))
    root = jnp.where(size > 0.0, root, 0.0)
    return jnp.where(coded < 0.0, -root, root)


def call(kernel, scalars, inputs, outputs, specs=None, scratch=(), flops=0):
    whole = pl.BlockSpec(memory_space=pltpu.VMEM)
    specs = specs or {}
    in_specs = [specs.get(n, whole) for n in range(len(inputs))]
    out_specs = [whole] * len(outputs)
    moved = sum(math.prod(x.shape) * x.dtype.itemsize for x in (*inputs, *outputs))
    return pl.pallas_call(
        kernel,
        grid_spec=pltpu.PrefetchScalarGridSpec(
            num_scalar_prefetch=1,
            grid=(1,),
            in_specs=in_specs,
            out_specs=out_specs,
            scratch_shapes=list(scratch),
        ),
        out_shape=list(outputs),
        compiler_params=pltpu.CompilerParams(vmem_limit_bytes=VMEM),
        cost_estimate=pl.CostEstimate(flops=flops, bytes_accessed=moved, transcendentals=0),
    )(scalars, *inputs)


def pack_kernel(width, place_ref, x_ref, g_ref, out_ref):
    rows, cols, channels = x_ref.shape
    blocks = channels // width
    pairs = rows // 2
    for q in range(pairs):
        lanes = [ref[2 * q + h].astype(jnp.float32) for h in range(2) for ref in (x_ref, g_ref)]
        lanes = [jnp.pad(x, ((0, PAD - cols), (0, 0))) for x in lanes]
        for b in range(blocks):
            pieces = [x[:, b * width : (b + 1) * width] for x in lanes]
            out_ref[b, q * PAD : (q + 1) * PAD, :] = jnp.concatenate(pieces, axis=1).astype(jnp.bfloat16)


def lon_kernel(inner, place_ref, table_ref, *refs):
    fields, (coded_ref, spec_ref) = refs[:inner], refs[inner:]
    member = place_ref[1]
    pairs, modes, lanes = spec_ref.shape
    blocks = fields[0].shape[0]
    tops = []
    for q in range(pairs):
        total = None
        for s, field in enumerate(fields):
            source = lax.rem(member - s + inner, inner)
            data = field[:, q * PAD : (q + 1) * PAD, :].reshape(blocks * PAD, lanes)
            term = dot(table_rows(table_ref, 0, 2 * modes, member * inner + source), data)
            total = term if total is None else total + term
        spec = total[:modes] + total[modes:]
        spec_ref[q] = spec
        tops.append(jnp.max(jnp.abs(spec), axis=0, keepdims=True))
    values, level = scaled(spec_ref[...], functools.reduce(jnp.maximum, tops))
    coded_ref[: pairs * modes, :] = encode(values).reshape(pairs * modes, lanes)
    coded_ref[pairs * modes :, :] = jnp.broadcast_to(level, (PAD, lanes)).astype(jnp.bfloat16)


def lat_rows(ref, pairs):
    modes = (ref.shape[0] - PAD) // pairs
    wide = ref.shape[1] // 2
    tile = 2 * SUB
    level = ref[pairs * modes :, :].astype(jnp.float32)[:1] * (1.0 / TOP)
    values = [decode(ref[q * modes : (q + 1) * modes, :]) * level for q in range(pairs)]
    rows = []
    for h in range(2):
        for q in range(pairs):
            parts = [
                values[q][n * tile : (n + 1) * tile, h * wide : (h + 1) * wide] for n in range(modes // tile)
            ]
            rows.append(jnp.concatenate(parts, axis=1))
    return jnp.concatenate(rows, axis=0)


def ready_kernel(pairs, start, place_ref, table_ref, spec_ref, win_ref, bin_ref, wout_ref, *outs):
    part_ref, form_ref, bias_ref = outs
    place, x = place_ref[0], place_ref[2]
    for n, ref in enumerate((win_ref, wout_ref)):
        re, im = ref[0, 0], ref[1, 0]
        form = jnp.concatenate([jnp.concatenate([re, im], axis=1), jnp.concatenate([-im, re], axis=1)], axis=0)
        form_ref[2 * n], form_ref[2 * n + 1] = split(form)
    bias = jnp.concatenate([bin_ref[0, pl.ds(place, 1), :], bin_ref[1, pl.ds(place, 1), :]], axis=1)
    bias_ref[...] = jnp.broadcast_to(bias, bias_ref.shape)
    rows = split(lat_rows(spec_ref, pairs))
    part_ref[...] = dot3(lat_part(table_ref, start, part_ref.shape[0], rows[0].shape[0], x), rows)


def mlp_kernel(lat, inner, pairs, start, scaling, place_ref, table_ref, *refs):
    others = refs[: lat - 1]
    part_ref, form_ref, bias_ref = refs[lat - 1 : lat + 2]
    back_ref, keep_ref, *rest = refs[lat + 2 :]
    send_refs, (w_ref,) = rest[: inner - 1], rest[inner - 1 :]
    member, x = place_ref[1], place_ref[2]
    wide = form_ref.shape[1]
    width = wide // 2
    tile = 2 * SUB
    size = part_ref.shape[0]
    points = size // 2
    part = size // lat
    subs = part_ref.shape[1] // wide

    spectra = part_ref[...]
    for s, ref in enumerate(others):
        source = lax.rem(x - s - 1 + lat, lat)
        matrix = lat_part(table_ref, start, size, part, source)
        spectra = spectra + dot3(matrix, split(lat_rows(ref, pairs)))

    def of_points(start):
        rows = []
        for n in range(subs):
            lanes = slice(n * wide + start, n * wide + start + width)
            rows.append(jnp.concatenate([spectra[:points, lanes], spectra[points:, lanes]], axis=1))
        return jnp.concatenate(rows, axis=0)

    spec_x, spec_g = of_points(0), of_points(width)
    m_in, m_out = (form_ref[0], form_ref[1]), (form_ref[2], form_ref[3])
    point = lax.broadcasted_iota(jnp.int32, (subs * points, 1), 0)
    first = ((point & (SUB - 1)) + jnp.where(point < points, 0, SUB) + member * SUB) == 0
    grad_out = spec_g * jnp.where(first, 1.0, 2.0)
    x_parts, g_parts = split(spec_x), split(grad_out)
    pre = dot3(x_parts, m_in) + bias_ref[:1]
    cdf = 0.5 * (1.0 + lax.erf(pre * root_half))
    hidden = pre * cdf
    slopes = cdf + pre * jnp.exp(-0.5 * pre * pre) * density_norm
    grad_pre = dot3(g_parts, m_out, ((1,), (1,))) * slopes
    p_parts = split(grad_pre)
    grad_spec = dot3(p_parts, m_in, ((1,), (1,)))
    lanes = []
    for n in range(subs):
        piece = grad_spec[n * points : (n + 1) * points]
        lanes.append(jnp.concatenate([piece[:, :width], piece[:, width:]], axis=0))
    matrix = lat_part(table_ref, start, size, part, x)
    back = dot3(matrix, split(jnp.concatenate(lanes, axis=1)), ((0,), (0,)))
    for q in range(pairs):
        for n in range(subs):
            pieces = [
                back[(h * pairs + q) * tile : (h * pairs + q + 1) * tile, n * width : (n + 1) * width]
                for h in range(2)
            ]
            back_ref[q, n * tile : (n + 1) * tile, :] = jnp.concatenate(pieces, axis=1)

    pieces = []
    for left, right in ((x_parts, p_parts), (split(hidden), g_parts)):
        total = dot3(left, right, ((0,), (0,)))
        pieces.append(total[:width, :width] + total[width:, width:])
        pieces.append(total[:width, width:] - total[width:, :width])
    weights = jnp.concatenate(pieces, axis=1) * scaling
    share = width // inner
    w_ref[...] = jnp.zeros_like(w_ref)
    for n in range(inner):
        w_ref[n, :share, :] = weights[n * share : (n + 1) * share]
    w_ref[0, share : share + 1, :wide] = jnp.sum(grad_pre, axis=0, keepdims=True) * scaling
    keep_ref[...] = w_ref[member]
    for s in range(1, inner):
        send_refs[s - 1][...] = w_ref[lax.rem(member + s, inner)]


def synth_kernel(inner, start, place_ref, table_ref, *refs):
    backs, sums, (out_ref, wide_ref) = refs[:inner], refs[inner : 2 * inner], refs[2 * inner :]
    member = place_ref[1]
    pairs, modes, lanes = backs[0].shape
    blocks, total_rows, wide = out_ref.shape
    data_rows = pairs * HALF
    share = lanes // 2 // inner
    for q in range(pairs):
        total = None
        for s, back in enumerate(backs):
            source = lax.rem(member - s + inner, inner)
            rows = table_rows(table_ref, start, 2 * blocks * HALF, member * inner + source)
            term = dot3((rows[:, :modes], rows[:, modes : 2 * modes]), split(back[q]))
            total = term if total is None else total + term
        part = blocks * HALF
        columns = jnp.concatenate([total[:part], total[part:]], axis=1)
        wide_ref[:, q * HALF : (q + 1) * HALF, :] = columns.reshape(blocks, HALF, wide)
    weights = sums[0][...]
    for ref in sums[1:]:
        weights = weights + ref[...]

    top_w = jnp.max(jnp.abs(weights), axis=0, keepdims=True)
    weights, level_w = scaled(weights, top_w)
    columns = wide_ref[...]
    top = jnp.max(jnp.max(jnp.abs(columns), axis=0), axis=0, keepdims=True)
    columns, level = scaled(columns, top)
    coded_w = encode(weights).astype(jnp.float32)
    bias = coded_w[share : share + 1, :lanes]
    spare = (bias, level_w[:, :lanes], level_w[:, lanes:], level[:, :lanes], level[:, lanes:])
    extra = []
    for n in range(pairs):
        row = jnp.zeros((1, lanes), jnp.float32) if n >= len(spare) else spare[n]
        row = jnp.concatenate([jnp.zeros((1, lanes), jnp.float32), row], axis=1)
        place_row = lax.broadcasted_iota(jnp.int32, (HALF, 1), 0)
        extra.append(jnp.where(place_row == SPARE, row, 0.0))
    extra = jnp.concatenate(extra, axis=0)
    coded = encode(columns).astype(jnp.float32)
    tail = coded_w[: total_rows - data_rows]
    for b in range(blocks):
        out_ref[b] = jnp.concatenate([coded[b] + extra, tail], axis=0).astype(jnp.bfloat16)


def spare_rows(raw, first, count):
    lanes = raw.shape[1] // 2
    rows = [raw[n * HALF + SPARE : n * HALF + SPARE + 1, lanes:] for n in range(first, first + count)]
    return jnp.concatenate(rows, axis=1)


def weight_rows(raw, data_rows):
    level = spare_rows(raw, 1, 2) * (1.0 / TOP)
    bias = decode(spare_rows(raw, 0, 1)) * level[:, : raw.shape[1] // 2]
    return decode(raw[data_rows:]) * level, bias


def columns_kernel(place_ref, data_ref, cot_ref, out_ref, held_ref, bias_ref):
    rows, cols, _ = cot_ref.shape
    blocks, total_rows, wide = data_ref.shape
    width = wide // 4
    pairs = rows // 2
    values = []
    for b in range(blocks):
        raw = data_ref[b].astype(jnp.float32)
        values.append(decode(raw[: pairs * HALF]) * (spare_rows(raw, 3, 2) * (1.0 / TOP)))
        held_ref[b], bias_ref[b : b + 1, :] = weight_rows(raw, pairs * HALF)
    for q in range(pairs):
        for h in range(2):
            parts = []
            for half in range(2):
                start = (2 * half + h) * width
                pieces = [v[q * HALF : (q + 1) * HALF, start : start + width] for v in values]
                parts.append(jnp.concatenate(pieces, axis=1))
            column = jnp.concatenate(parts, axis=0)[:cols]
            row = 2 * q + h
            out_ref[row] = (cot_ref[row].astype(jnp.float32) + column).astype(jnp.bfloat16)


def weights_kernel(inner, share, place_ref, held_ref, own_bias_ref, *refs):
    pieces, (win_ref, bin_ref, wout_ref) = refs[: inner - 1], refs[inner - 1 :]
    member = place_ref[1]
    blocks, rows, wide = held_ref.shape
    width = wide // 4
    data_rows = pieces[0].shape[1] - rows
    for b in range(blocks):
        held = [(held_ref[b], own_bias_ref[b : b + 1, :])]
        held += [weight_rows(ref[b].astype(jnp.float32), data_rows) for ref in pieces]
        for n in range(inner):
            part, bias = held[0]
            for s in range(1, inner):
                chosen = lax.rem(member - s + inner, inner) == n
                part = jnp.where(chosen, held[s][0], part)
                bias = jnp.where(chosen, held[s][1], bias)
            for i in range(4):
                target = (win_ref, wout_ref)[i // 2]
                target[i % 2, b, n * share : (n + 1) * share, :] = part[:share, i * width : (i + 1) * width]
            if n == 0:
                for k in range(2):
                    bin_ref[k, b : b + 1, :] = bias[:, k * width : (k + 1) * width]


def body(features, cotangent, weight_in, bias_in, weight_out):
    lon_count, lat_count = lax.axis_size("lon"), lax.axis_size("lat")
    blocks, width = weight_in.shape[1:3]
    rows, cols, _ = features.shape
    inner = lon_count // blocks
    pairs = rows // 2
    wide = 4 * width
    modes = 2 * MODE_DEV * blocks
    size = 2 * rows * lat_count * SUB
    subs = modes // (2 * SUB)
    lon_place = lax.axis_index("lon")
    lat_place = lax.axis_index("lat")
    scalars = jnp.stack([lon_place // inner, lon_place % inner, lat_place]).astype(jnp.int32)
    scaling = (rows * lat_count * modes // 2 * inner) ** -0.5
    tables, (lon_start, lat_start, synth_start, _) = all_tables(blocks, inner, cols, rows, lat_count)
    share = width // inner
    total_rows = pairs * HALF + -(-share // 8) * 8
    sum_rows = -(-(share + 1) // 8) * 8
    f32, bf16 = jnp.float32, jnp.bfloat16
    shape = jax.ShapeDtypeStruct

    places = [[g * inner + i for g in range(blocks)] for i in range(inner)]

    def exchange(values):
        return lax.all_to_all(
            values, "lon", split_axis=0, concat_axis=0, tiled=True, axis_index_groups=places
        )

    def to_member(values, step):
        turn = [(i, i // inner * inner + (i + step) % inner) for i in range(lon_count)]
        return lax.ppermute(values, "lon", turn)

    def to_lat(values, step):
        return lax.ppermute(values, "lat", [(i, (i + step) % lat_count) for i in range(lat_count)])

    (packed,) = call(
        functools.partial(pack_kernel, width),
        scalars,
        (features, cotangent),
        (shape((blocks, pairs * PAD, wide), bf16),),
    )
    arrived = exchange(packed)
    fields = [arrived] + [to_member(arrived, s) for s in range(1, inner)]
    (coded,) = call(
        functools.partial(lon_kernel, inner),
        scalars,
        (tables, *fields),
        (shape((pairs * modes + PAD, wide), bf16),),
        scratch=(pltpu.VMEM((pairs, modes, wide), f32),),
    )
    others = [to_lat(coded, s) for s in range(1, lat_count)]
    block_spec = pl.BlockSpec((2, 1, width, width), lambda i, s: (0, s[0], 0, 0))
    part, forms, bias = call(
        functools.partial(ready_kernel, pairs, lat_start),
        scalars,
        (tables, coded, weight_in, bias_in, weight_out),
        (
            shape((size, 2 * subs * width), f32),
            shape((4, 2 * width, 2 * width), bf16),
            shape((8, 2 * width), f32),
        ),
        specs={2: block_spec, 4: block_spec},
        flops=6 * size * size // lat_count * 2 * subs * width,
    )
    back, keep, *send = call(
        functools.partial(mlp_kernel, lat_count, inner, pairs, lat_start, scaling),
        scalars,
        (tables, *others, part, forms, bias),
        (shape((pairs, modes, 2 * width), f32), *[shape((sum_rows, wide), f32)] * inner),
        scratch=(pltpu.VMEM((inner, sum_rows, wide), f32),),
    )
    backs = [back] + [to_member(back, s) for s in range(1, inner)]
    sums = [keep] + [to_member(send[s - 1], s) for s in range(1, inner)]
    (payload,) = call(
        functools.partial(synth_kernel, inner, synth_start),
        scalars,
        (tables, *backs, *sums),
        (shape((blocks, total_rows, wide), bf16),),
        scratch=(pltpu.VMEM((blocks, pairs * HALF, wide), f32),),
    )
    returned = exchange(payload)
    gathered = [to_member(returned, s) for s in range(1, inner)]
    weight_part = total_rows - pairs * HALF
    grad_features, held, held_bias = call(
        columns_kernel,
        scalars,
        (returned, cotangent),
        (
            shape(features.shape, bf16),
            shape((blocks, weight_part, wide), f32),
            shape((blocks, 2 * width), f32),
        ),
    )
    grad_w_in, grad_b_in, grad_w_out = call(
        functools.partial(weights_kernel, inner, share),
        scalars,
        (held, held_bias, *gathered),
        (shape(weight_in.shape, f32), shape(bias_in.shape, f32), shape(weight_out.shape, f32)),
    )
    return grad_features, grad_w_in, grad_b_in, grad_w_out


def solution(mesh):
    placed = (P("lat", "lon", None), P("lat", "lon", None), P(), P(), P())
    return jax.shard_map(
        body,
        mesh=mesh,
        in_specs=placed,
        out_specs=(P("lat", "lon", None), P(), P(), P()),
        check_vma=False,
    )
```

```python
import functools
import math

import jax
import jax.numpy as jnp
import ml_dtypes
import numpy as np
from jax import lax
from jax.experimental import pallas as pl
from jax.experimental.pallas import tpu as pltpu
from jax.sharding import PartitionSpec as P

MODE_DEV = 4
PAD = 16
HALF = PAD // 2
BASES = (4, 6, 2)
SUB = 4
SPARE = 6
POWER = 13.0
TOP = 2.0**9
VMEM = 40 * 2**20

root_half = math.sqrt(0.5)
density_norm = 1.0 / math.sqrt(2.0 * math.pi)


def halves(table):
    table = table.astype(np.float32)
    high = table.astype(ml_dtypes.bfloat16)
    low = (table - high.astype(np.float32)).astype(ml_dtypes.bfloat16)
    return high, low


def lon_table(columns, mode_count):
    product = np.arange(columns)[:, None] * np.arange(mode_count)[None, :] % columns
    angle = product * (2.0 * math.pi / columns)
    stacked = np.stack([np.cos(angle), -np.sin(angle)], axis=2) * columns**-0.5
    return stacked.reshape(columns, 2 * mode_count)


def lon_tables(blocks, inner, cols):
    modes = MODE_DEV * blocks
    table = lon_table(blocks * inner * cols, modes * inner)
    table = table.reshape(blocks, inner, cols, inner, 2 * modes)
    table = np.pad(table, ((0, 0), (0, 0), (0, PAD - cols), (0, 0), (0, 0)))
    forward = table.transpose(3, 1, 4, 0, 2).reshape(inner, inner, 2 * modes, blocks * PAD)
    split = table.reshape(blocks, inner, 2, HALF, inner, 2 * modes)
    synth = split.transpose(1, 4, 2, 0, 3, 5).reshape(inner, inner, 2 * blocks * HALF, 2 * modes)
    forward, synth = np.concatenate(halves(forward), axis=2), np.concatenate(halves(synth), axis=3)
    return forward.reshape(-1, blocks * PAD), synth.reshape(-1, 4 * modes)


def served(member):
    return [(0, member), (1, member)] + [(base + member, m) for base in BASES for m in range(2)]


def served_table(blocks, cols):
    modes = 2 * MODE_DEV * blocks
    table = lon_table(blocks * 2 * cols, modes).reshape(blocks, 2, cols, 2, modes)
    table = np.pad(table, ((0, 0), (0, 0), (0, PAD - cols), (0, 0), (0, 0)))
    whole = []
    for place in range(blocks):
        for member in range(2):
            rows = np.stack([table[place ^ k, m] for k, m in served(member)])
            rows = np.stack([rows[:, :, member], rows[:, :, 1 - member]], axis=2)
            rows = rows.reshape(len(rows), 2, HALF, 2 * modes).transpose(1, 0, 2, 3)
            whole.append(np.concatenate(halves(rows.reshape(-1, 2 * modes)), axis=1))
    return np.stack(whole).reshape(blocks, 2, *whole[0].shape)


def lat_table(rows, lat_count, group):
    total = rows * lat_count
    product = np.arange(total)[:, None] * np.arange(total)[None, :] % total
    angle = product * (2.0 * math.pi / total)
    c, s = np.cos(angle), np.sin(angle)
    basis = np.stack([np.stack([c, s], -1), np.stack([-s, c], -1)], axis=0) * total**-0.5
    basis = basis.reshape(2, total, lat_count, rows // 2, 2, 2).transpose(0, 1, 2, 4, 3, 5)
    size = 2 * total * group
    return np.einsum("akxhqb,mn->akmxhqnb", basis, np.eye(group)).reshape(size, size)


def all_tables(blocks, inner, cols, rows, lat_count):
    forward, synth = lon_tables(blocks, inner, cols)
    table = lat_table(rows, lat_count, SUB)
    size = table.shape[0]
    lat = np.concatenate(halves(table.reshape(size, lat_count, -1).transpose(1, 0, 2)), axis=1)
    parts = [forward, lat.reshape(2 * lat_count * size, -1), synth]
    lanes = max(p.shape[1] for p in parts)
    parts = [np.pad(p, ((0, 0), (0, lanes - p.shape[1]))) for p in parts]
    starts = np.cumsum([0] + [len(p) for p in parts])
    return np.concatenate(parts), [int(n) for n in starts]


def split(values):
    high = values.astype(jnp.bfloat16)
    return high, (values - high.astype(jnp.float32)).astype(jnp.bfloat16)


def dot(left, right, dims=((1,), (0,))):
    return lax.dot_general(left, right, (dims, ((), ())), preferred_element_type=jnp.float32)


def dot3(left, right, dims=((1,), (0,))):
    return dot(left[0], right[0], dims) + (dot(left[0], right[1], dims) + dot(left[1], right[0], dims))


def scaled(values, top):
    level = jnp.maximum(top, 1e-30).astype(jnp.bfloat16).astype(jnp.float32)
    return values * (TOP / level), level


def table_rows(ref, start, count, place):
    return ref[pl.ds(pl.multiple_of(start + place * count, PAD), count), :]


def lat_part(ref, start, size, part, x):
    rows = table_rows(ref, start, 2 * size, x)[:, :part]
    return rows[:size], rows[size:]


def encode(values):
    square = values * values
    fourth = square * square
    return (values * fourth * (fourth * fourth)).astype(jnp.bfloat16)


def decode(coded):
    coded = coded.astype(jnp.float32)
    size = jnp.abs(coded)
    root = jnp.exp(jnp.log(jnp.maximum(size, 1e-37)) * (1.0 / POWER))
    root = jnp.where(size > 0.0, root, 0.0)
    return jnp.where(coded < 0.0, -root, root)


def call(kernel, scalars, inputs, outputs, specs=None, scratch=(), flops=0):
    whole = pl.BlockSpec(memory_space=pltpu.VMEM)
    specs = specs or {}
    in_specs = [specs.get(n, whole) for n in range(len(inputs))]
    out_specs = [whole] * len(outputs)
    moved = sum(math.prod(x.shape) * x.dtype.itemsize for x in (*inputs, *outputs))
    return pl.pallas_call(
        kernel,
        grid_spec=pltpu.PrefetchScalarGridSpec(
            num_scalar_prefetch=1,
            grid=(1,),
            in_specs=in_specs,
            out_specs=out_specs,
            scratch_shapes=list(scratch),
        ),
        out_shape=list(outputs),
        compiler_params=pltpu.CompilerParams(vmem_limit_bytes=VMEM),
        cost_estimate=pl.CostEstimate(flops=flops, bytes_accessed=moved, transcendentals=0),
    )(scalars, *inputs)


def pack_kernel(width, place_ref, x_ref, g_ref, out_ref):
    rows, cols, channels = x_ref.shape
    blocks = channels // width
    pairs = rows // 2
    for q in range(pairs):
        lanes = [ref[2 * q + h].astype(jnp.float32) for h in range(2) for ref in (x_ref, g_ref)]
        lanes = [jnp.pad(x, ((0, PAD - cols), (0, 0))) for x in lanes]
        for b in range(blocks):
            pieces = [x[:, b * width : (b + 1) * width] for x in lanes]
            out_ref[b, q * PAD : (q + 1) * PAD, :] = jnp.concatenate(pieces, axis=1).astype(jnp.bfloat16)


def lon_kernel(inner, place_ref, table_ref, *refs):
    fields, (coded_ref, spec_ref) = refs[:inner], refs[inner:]
    member = place_ref[1]
    pairs, modes, lanes = spec_ref.shape
    blocks = fields[0].shape[0]
    tops = []
    for q in range(pairs):
        total = None
        for s, field in enumerate(fields):
            source = lax.rem(member - s + inner, inner)
            data = field[:, q * PAD : (q + 1) * PAD, :].reshape(blocks * PAD, lanes)
            term = dot(table_rows(table_ref, 0, 2 * modes, member * inner + source), data)
            total = term if total is None else total + term
        spec = total[:modes] + total[modes:]
        spec_ref[q] = spec
        tops.append(jnp.max(jnp.abs(spec), axis=0, keepdims=True))
    values, level = scaled(spec_ref[...], functools.reduce(jnp.maximum, tops))
    coded_ref[: pairs * modes, :] = encode(values).reshape(pairs * modes, lanes)
    coded_ref[pairs * modes :, :] = jnp.broadcast_to(level, (PAD, lanes)).astype(jnp.bfloat16)


def lat_rows(ref, pairs):
    modes = (ref.shape[0] - PAD) // pairs
    wide = ref.shape[1] // 2
    tile = 2 * SUB
    level = ref[pairs * modes :, :].astype(jnp.float32)[:1] * (1.0 / TOP)
    values = [decode(ref[q * modes : (q + 1) * modes, :]) * level for q in range(pairs)]
    rows = []
    for h in range(2):
        for q in range(pairs):
            parts = [
                values[q][n * tile : (n + 1) * tile, h * wide : (h + 1) * wide] for n in range(modes // tile)
            ]
            rows.append(jnp.concatenate(parts, axis=1))
    return jnp.concatenate(rows, axis=0)


def ready_kernel(pairs, start, place_ref, table_ref, spec_ref, win_ref, bin_ref, wout_ref, *outs):
    part_ref, form_ref, bias_ref = outs
    place, x = place_ref[0], place_ref[2]
    for n, ref in enumerate((win_ref, wout_ref)):
        re, im = ref[0, 0], ref[1, 0]
        form = jnp.concatenate([jnp.concatenate([re, im], axis=1), jnp.concatenate([-im, re], axis=1)], axis=0)
        form_ref[2 * n], form_ref[2 * n + 1] = split(form)
    bias = jnp.concatenate([bin_ref[0, pl.ds(place, 1), :], bin_ref[1, pl.ds(place, 1), :]], axis=1)
    bias_ref[...] = jnp.broadcast_to(bias, bias_ref.shape)
    rows = split(lat_rows(spec_ref, pairs))
    part_ref[...] = dot3(lat_part(table_ref, start, part_ref.shape[0], rows[0].shape[0], x), rows)


def mlp_kernel(lat, inner, shares, pairs, start, scaling, place_ref, table_ref, *refs):
    others = refs[: lat - 1]
    part_ref, form_ref, bias_ref = refs[lat - 1 : lat + 2]
    back_ref, keep_ref, *rest = refs[lat + 2 :]
    send_refs, (w_ref,) = rest[: shares - 1], rest[shares - 1 :]
    member, x = place_ref[1], place_ref[2]
    wide = form_ref.shape[1]
    width = wide // 2
    tile = 2 * SUB
    size = part_ref.shape[0]
    points = size // 2
    part = size // lat
    subs = part_ref.shape[1] // wide

    spectra = part_ref[...]
    for s, ref in enumerate(others):
        source = lax.rem(x - s - 1 + lat, lat)
        matrix = lat_part(table_ref, start, size, part, source)
        spectra = spectra + dot3(matrix, split(lat_rows(ref, pairs)))

    def of_points(start):
        rows = []
        for n in range(subs):
            lanes = slice(n * wide + start, n * wide + start + width)
            rows.append(jnp.concatenate([spectra[:points, lanes], spectra[points:, lanes]], axis=1))
        return jnp.concatenate(rows, axis=0)

    spec_x, spec_g = of_points(0), of_points(width)
    m_in, m_out = (form_ref[0], form_ref[1]), (form_ref[2], form_ref[3])
    point = lax.broadcasted_iota(jnp.int32, (subs * points, 1), 0)
    first = ((point & (SUB - 1)) + jnp.where(point < points, 0, SUB) + member * SUB) == 0
    grad_out = spec_g * jnp.where(first, 1.0, 2.0)
    x_parts, g_parts = split(spec_x), split(grad_out)
    pre = dot3(x_parts, m_in) + bias_ref[:1]
    cdf = 0.5 * (1.0 + lax.erf(pre * root_half))
    hidden = pre * cdf
    slopes = cdf + pre * jnp.exp(-0.5 * pre * pre) * density_norm
    grad_pre = dot3(g_parts, m_out, ((1,), (1,))) * slopes
    p_parts = split(grad_pre)
    grad_spec = dot3(p_parts, m_in, ((1,), (1,)))
    lanes = []
    for n in range(subs):
        piece = grad_spec[n * points : (n + 1) * points]
        lanes.append(jnp.concatenate([piece[:, :width], piece[:, width:]], axis=0))
    matrix = lat_part(table_ref, start, size, part, x)
    back = dot3(matrix, split(jnp.concatenate(lanes, axis=1)), ((0,), (0,)))
    for q in range(pairs):
        for n in range(subs):
            pieces = [
                back[(h * pairs + q) * tile : (h * pairs + q + 1) * tile, n * width : (n + 1) * width]
                for h in range(2)
            ]
            back_ref[q, n * tile : (n + 1) * tile, :] = jnp.concatenate(pieces, axis=1)

    pieces = []
    for left, right in ((x_parts, p_parts), (split(hidden), g_parts)):
        total = dot3(left, right, ((0,), (0,)))
        pieces.append(total[:width, :width] + total[width:, width:])
        pieces.append(total[:width, width:] - total[width:, :width])
    weights = jnp.concatenate(pieces, axis=1) * scaling
    share = width // shares
    w_ref[...] = jnp.zeros_like(w_ref)
    for n in range(shares):
        w_ref[n, :share, :] = weights[n * share : (n + 1) * share]
    w_ref[0, share : share + 1, :wide] = jnp.sum(grad_pre, axis=0, keepdims=True) * scaling
    if shares == 1:
        keep_ref[...] = w_ref[0]
        return
    keep_ref[...] = w_ref[member]
    for s in range(1, shares):
        send_refs[s - 1][...] = w_ref[lax.rem(member + s, shares)]


def synth_kernel(inner, start, place_ref, table_ref, *refs):
    backs, sums, (out_ref, wide_ref) = refs[:inner], refs[inner : 2 * inner], refs[2 * inner :]
    member = place_ref[1]
    pairs, modes, lanes = backs[0].shape
    blocks, total_rows, wide = out_ref.shape
    data_rows = pairs * HALF
    share = lanes // 2 // inner
    for q in range(pairs):
        total = None
        for s, back in enumerate(backs):
            source = lax.rem(member - s + inner, inner)
            rows = table_rows(table_ref, start, 2 * blocks * HALF, member * inner + source)
            term = dot3((rows[:, :modes], rows[:, modes : 2 * modes]), split(back[q]))
            total = term if total is None else total + term
        part = blocks * HALF
        columns = jnp.concatenate([total[:part], total[part:]], axis=1)
        wide_ref[:, q * HALF : (q + 1) * HALF, :] = columns.reshape(blocks, HALF, wide)
    weights = sums[0][...]
    for ref in sums[1:]:
        weights = weights + ref[...]
    coded, tail = code_all(wide_ref[...], weights, share)
    tail = tail[: total_rows - data_rows]
    for b in range(blocks):
        out_ref[b] = jnp.concatenate([coded[b], tail], axis=0).astype(jnp.bfloat16)


def code_all(columns, weights, share):
    rows, wide = columns.shape[1:]
    lanes = wide // 2
    weights, level_w = scaled(weights, jnp.max(jnp.abs(weights), axis=0, keepdims=True))
    top = jnp.max(jnp.max(jnp.abs(columns), axis=0), axis=0, keepdims=True)
    columns, level = scaled(columns, top)
    tail = encode(weights).astype(jnp.float32)
    bias = tail[share : share + 1, :lanes]
    spare = (bias, level_w[:, :lanes], level_w[:, lanes:], level[:, :lanes], level[:, lanes:])
    extra = []
    for n in range(rows // HALF):
        row = jnp.zeros((1, lanes), jnp.float32) if n >= len(spare) else spare[n]
        row = jnp.concatenate([jnp.zeros((1, lanes), jnp.float32), row], axis=1)
        place_row = lax.broadcasted_iota(jnp.int32, (HALF, 1), 0)
        extra.append(jnp.where(place_row == SPARE, row, 0.0))
    extra = jnp.concatenate(extra, axis=0)
    return encode(columns).astype(jnp.float32) + extra, tail


def serve_kernel(place_ref, table_ref, own_ref, other_ref, sum_ref, more_ref, *refs):
    outs, wide_ref = refs[:-1], refs[-1]
    pairs, modes, lanes = own_ref.shape
    count = wide_ref.shape[0]
    share = lanes // 2
    table = table_ref[0, 0]
    matrix = (table[:, : 2 * modes], table[:, 2 * modes :])
    for q in range(pairs):
        total = dot3(matrix, split(jnp.concatenate([own_ref[q], other_ref[q]], axis=0)))
        part = count * HALF
        columns = jnp.concatenate([total[:part], total[part:]], axis=1)
        wide_ref[:, q * HALF : (q + 1) * HALF, :] = columns.reshape(count, HALF, 2 * lanes)
    coded, tail = code_all(wide_ref[...], sum_ref[...] + more_ref[...], share)
    tail = tail[:share]
    for n, ref in enumerate(outs):
        parts = [coded[n]] if n < 2 else [coded[2 * n - 2], coded[2 * n - 1]]
        ref[...] = jnp.concatenate([*parts, tail], axis=0).astype(jnp.bfloat16)


def arrived(ref, member, data_rows):
    raw = ref[...].astype(jnp.float32)
    level = spare_rows(raw, 3, 2) * (1.0 / TOP)
    columns = raw[:data_rows]
    start = data_rows
    if raw.shape[0] == 2 * data_rows + raw.shape[1] // 4:
        start = 2 * data_rows
        columns = jnp.where(member == 0, columns, raw[data_rows:start])
    weights, bias = weight_rows(raw, start)
    return decode(columns) * level, weights, bias


def first_kernel(data_rows, place_ref, *refs):
    member = place_ref[1]
    count = len(refs) - 3
    columns_ref, weights_ref, bias_ref = refs[count:]
    for n in range(count):
        columns_ref[n], weights_ref[n], bias_ref[n : n + 1, :] = arrived(refs[n], member, data_rows)


def last_kernel(data_rows, place_ref, columns_ref, weights_ref, bias_ref, cot_ref, *refs):
    place, member = place_ref[0], place_ref[1]
    lates = refs[: len(BASES)]
    out_ref, win_ref, bin_ref, wout_ref, held_ref = refs[len(BASES) :]
    rows, cols, _ = cot_ref.shape
    blocks = win_ref.shape[1]
    width = win_ref.shape[2]
    pairs = rows // 2

    def settle(source, columns, weights, bias):
        held_ref[source] = columns
        for i in range(4):
            target = (win_ref, wout_ref)[i // 2]
            target[i % 2, source] = weights[:, i * width : (i + 1) * width]
        for k in range(2):
            bin_ref[k, pl.ds(source, 1), :] = bias[:, k * width : (k + 1) * width]

    for n, base in enumerate((0, 1) + BASES):
        source = place ^ (base + member) if n >= 2 else place ^ base
        settle(source, columns_ref[n], weights_ref[n], bias_ref[n : n + 1, :])
    for ref, base in zip(lates, BASES):
        settle(place ^ (base + 1 - member), *arrived(ref, member, data_rows))
    for q in range(pairs):
        for h in range(2):
            parts = []
            for half in range(2):
                start = (2 * half + h) * width
                pieces = [
                    held_ref[b, q * HALF : (q + 1) * HALF, :][:, start : start + width] for b in range(blocks)
                ]
                parts.append(jnp.concatenate(pieces, axis=1))
            column = jnp.concatenate(parts, axis=0)[:cols]
            row = 2 * q + h
            out_ref[row] = (cot_ref[row].astype(jnp.float32) + column).astype(jnp.bfloat16)


def spare_rows(raw, first, count):
    lanes = raw.shape[1] // 2
    rows = [raw[n * HALF + SPARE : n * HALF + SPARE + 1, lanes:] for n in range(first, first + count)]
    return jnp.concatenate(rows, axis=1)


def weight_rows(raw, data_rows):
    level = spare_rows(raw, 1, 2) * (1.0 / TOP)
    bias = decode(spare_rows(raw, 0, 1)) * level[:, : raw.shape[1] // 2]
    return decode(raw[data_rows:]) * level, bias


def columns_kernel(place_ref, data_ref, cot_ref, out_ref, held_ref, bias_ref):
    rows, cols, _ = cot_ref.shape
    blocks, total_rows, wide = data_ref.shape
    width = wide // 4
    pairs = rows // 2
    values = []
    for b in range(blocks):
        raw = data_ref[b].astype(jnp.float32)
        values.append(decode(raw[: pairs * HALF]) * (spare_rows(raw, 3, 2) * (1.0 / TOP)))
        held_ref[b], bias_ref[b : b + 1, :] = weight_rows(raw, pairs * HALF)
    for q in range(pairs):
        for h in range(2):
            parts = []
            for half in range(2):
                start = (2 * half + h) * width
                pieces = [v[q * HALF : (q + 1) * HALF, start : start + width] for v in values]
                parts.append(jnp.concatenate(pieces, axis=1))
            column = jnp.concatenate(parts, axis=0)[:cols]
            row = 2 * q + h
            out_ref[row] = (cot_ref[row].astype(jnp.float32) + column).astype(jnp.bfloat16)


def weights_kernel(inner, share, place_ref, held_ref, own_bias_ref, *refs):
    pieces, (win_ref, bin_ref, wout_ref) = refs[: inner - 1], refs[inner - 1 :]
    member = place_ref[1]
    blocks, rows, wide = held_ref.shape
    width = wide // 4
    data_rows = pieces[0].shape[1] - rows
    for b in range(blocks):
        held = [(held_ref[b], own_bias_ref[b : b + 1, :])]
        held += [weight_rows(ref[b].astype(jnp.float32), data_rows) for ref in pieces]
        for n in range(inner):
            part, bias = held[0]
            for s in range(1, inner):
                chosen = lax.rem(member - s + inner, inner) == n
                part = jnp.where(chosen, held[s][0], part)
                bias = jnp.where(chosen, held[s][1], bias)
            for i in range(4):
                target = (win_ref, wout_ref)[i // 2]
                target[i % 2, b, n * share : (n + 1) * share, :] = part[:share, i * width : (i + 1) * width]
            if n == 0:
                for k in range(2):
                    bin_ref[k, b : b + 1, :] = bias[:, k * width : (k + 1) * width]


def body(features, cotangent, weight_in, bias_in, weight_out):
    lon_count, lat_count = lax.axis_size("lon"), lax.axis_size("lat")
    blocks, width = weight_in.shape[1:3]
    rows, cols, _ = features.shape
    inner = lon_count // blocks
    pairs = rows // 2
    wide = 4 * width
    modes = 2 * MODE_DEV * blocks
    size = 2 * rows * lat_count * SUB
    subs = modes // (2 * SUB)
    lon_place = lax.axis_index("lon")
    lat_place = lax.axis_index("lat")
    scalars = jnp.stack([lon_place // inner, lon_place % inner, lat_place]).astype(jnp.int32)
    scaling = (rows * lat_count * modes // 2 * inner) ** -0.5
    tables, (lon_start, lat_start, synth_start, _) = all_tables(blocks, inner, cols, rows, lat_count)
    paired = inner == 2 and blocks == 2 + 2 * len(BASES)
    shares = 1 if paired else inner
    share = width // shares
    data_rows = pairs * HALF
    total_rows = data_rows + -(-share // 8) * 8
    sum_rows = -(-(share + 1) // 8) * 8
    f32, bf16 = jnp.float32, jnp.bfloat16
    shape = jax.ShapeDtypeStruct

    places = [[g * inner + i for g in range(blocks)] for i in range(inner)]

    def exchange(values):
        return lax.all_to_all(
            values, "lon", split_axis=0, concat_axis=0, tiled=True, axis_index_groups=places
        )

    def to_member(values, step):
        turn = [(i, i // inner * inner + (i + step) % inner) for i in range(lon_count)]
        return lax.ppermute(values, "lon", turn)

    def to_place(values, first, second):
        turn = [(i, (i // 2 ^ (second if i % 2 else first)) * 2 + i % 2) for i in range(lon_count)]
        return lax.ppermute(values, "lon", turn)

    def to_lat(values, step):
        return lax.ppermute(values, "lat", [(i, (i + step) % lat_count) for i in range(lat_count)])

    (packed,) = call(
        functools.partial(pack_kernel, width),
        scalars,
        (features, cotangent),
        (shape((blocks, pairs * PAD, wide), bf16),),
    )
    arrived = exchange(packed)
    fields = [arrived] + [to_member(arrived, s) for s in range(1, inner)]
    (coded,) = call(
        functools.partial(lon_kernel, inner),
        scalars,
        (tables, *fields),
        (shape((pairs * modes + PAD, wide), bf16),),
        scratch=(pltpu.VMEM((pairs, modes, wide), f32),),
    )
    others = [to_lat(coded, s) for s in range(1, lat_count)]
    block_spec = pl.BlockSpec((2, 1, width, width), lambda i, s: (0, s[0], 0, 0))
    part, forms, bias = call(
        functools.partial(ready_kernel, pairs, lat_start),
        scalars,
        (tables, coded, weight_in, bias_in, weight_out),
        (
            shape((size, 2 * subs * width), f32),
            shape((4, 2 * width, 2 * width), bf16),
            shape((8, 2 * width), f32),
        ),
        specs={2: block_spec, 4: block_spec},
        flops=6 * size * size // lat_count * 2 * subs * width,
    )
    back, keep, *send = call(
        functools.partial(mlp_kernel, lat_count, inner, shares, pairs, lat_start, scaling),
        scalars,
        (tables, *others, part, forms, bias),
        (shape((pairs, modes, 2 * width), f32), *[shape((sum_rows, wide), f32)] * shares),
        scratch=(pltpu.VMEM((shares, sum_rows, wide), f32),),
    )
    backs = [back] + [to_member(back, s) for s in range(1, inner)]
    if paired:
        table = served_table(blocks, cols)
        count = table.shape[2] // PAD
        outs = [share + data_rows] * 2 + [share + 2 * data_rows] * len(BASES)
        own, side, *slots = call(
            serve_kernel,
            scalars,
            (table, *backs, keep, to_member(keep, 1)),
            [shape((n, wide), bf16) for n in outs],
            specs={0: pl.BlockSpec((1, 1, *table.shape[2:]), lambda i, s: (s[0], s[1], 0, 0))},
            scratch=(pltpu.VMEM((count, data_rows, wide), f32),),
        )
        sent = [to_place(x, base, base + 1) for x, base in zip(slots, BASES)]
        side, sent[-1] = lax.optimization_barrier((to_place(side, 1, 1), sent[-1]))
        firsts = [own, side, *sent]
        late = [to_member(x, 1) for x in sent]
        held = call(
            functools.partial(first_kernel, data_rows),
            scalars,
            firsts,
            (
                shape((len(firsts), data_rows, wide), f32),
                shape((len(firsts), share, wide), f32),
                shape((len(firsts), 2 * width), f32),
            ),
        )
        return call(
            functools.partial(last_kernel, data_rows),
            scalars,
            (*held, cotangent, *late),
            [shape(x.shape, x.dtype) for x in (features, weight_in, bias_in, weight_out)],
            scratch=(pltpu.VMEM((blocks, data_rows, wide), f32),),
        )
    sums = [keep] + [to_member(send[s - 1], s) for s in range(1, inner)]
    (payload,) = call(
        functools.partial(synth_kernel, inner, synth_start),
        scalars,
        (tables, *backs, *sums),
        (shape((blocks, total_rows, wide), bf16),),
        scratch=(pltpu.VMEM((blocks, pairs * HALF, wide), f32),),
    )
    returned = exchange(payload)
    gathered = [to_member(returned, s) for s in range(1, inner)]
    weight_part = total_rows - pairs * HALF
    grad_features, held, held_bias = call(
        columns_kernel,
        scalars,
        (returned, cotangent),
        (
            shape(features.shape, bf16),
            shape((blocks, weight_part, wide), f32),
            shape((blocks, 2 * width), f32),
        ),
    )
    grad_w_in, grad_b_in, grad_w_out = call(
        functools.partial(weights_kernel, inner, share),
        scalars,
        (held, held_bias, *gathered),
        (shape(weight_in.shape, f32), shape(bias_in.shape, f32), shape(weight_out.shape, f32)),
    )
    return grad_features, grad_w_in, grad_b_in, grad_w_out


def solution(mesh):
    placed = (P("lat", "lon", None), P("lat", "lon", None), P(), P(), P())
    return jax.shard_map(
        body,
        mesh=mesh,
        in_specs=placed,
        out_specs=(P("lat", "lon", None), P(), P(), P()),
        check_vma=False,
    )
```

```python
import functools
import math

import jax
import jax.numpy as jnp
import ml_dtypes
import numpy as np
from jax import lax
from jax.experimental import pallas as pl
from jax.experimental.pallas import tpu as pltpu
from jax.sharding import PartitionSpec as P

MODE_DEV = 4
PAD = 16
HALF = PAD // 2
BASES = (4, 6, 2)
SUB = 4
SPARE = 6
POWER = 13.0
TOP = 2.0**9
VMEM = 40 * 2**20

root_half = math.sqrt(0.5)
density_norm = 1.0 / math.sqrt(2.0 * math.pi)


def halves(table):
    table = table.astype(np.float32)
    high = table.astype(ml_dtypes.bfloat16)
    low = (table - high.astype(np.float32)).astype(ml_dtypes.bfloat16)
    return high, low


def lon_table(columns, mode_count):
    product = np.arange(columns)[:, None] * np.arange(mode_count)[None, :] % columns
    angle = product * (2.0 * math.pi / columns)
    stacked = np.stack([np.cos(angle), -np.sin(angle)], axis=2) * columns**-0.5
    return stacked.reshape(columns, 2 * mode_count)


def lon_tables(blocks, inner, cols):
    modes = MODE_DEV * blocks
    table = lon_table(blocks * inner * cols, modes * inner)
    table = table.reshape(blocks, inner, cols, inner, 2 * modes)
    table = np.pad(table, ((0, 0), (0, 0), (0, PAD - cols), (0, 0), (0, 0)))
    forward = table.transpose(3, 1, 4, 0, 2).reshape(inner, inner, 2 * modes, blocks * PAD)
    split = table.reshape(blocks, inner, 2, HALF, inner, 2 * modes)
    synth = split.transpose(1, 4, 2, 0, 3, 5).reshape(inner, inner, 2 * blocks * HALF, 2 * modes)
    forward, synth = np.concatenate(halves(forward), axis=2), np.concatenate(halves(synth), axis=3)
    return forward.reshape(-1, blocks * PAD), synth.reshape(-1, 4 * modes)


def served(member):
    return [(0, member), (1, member)] + [(base + member, m) for base in BASES for m in range(2)]


def served_table(blocks, cols):
    modes = 2 * MODE_DEV * blocks
    table = lon_table(blocks * 2 * cols, modes).reshape(blocks, 2, cols, 2, modes)
    table = np.pad(table, ((0, 0), (0, 0), (0, PAD - cols), (0, 0), (0, 0)))
    whole = []
    for place in range(blocks):
        for member in range(2):
            rows = np.stack([table[place ^ k, m] for k, m in served(member)])
            rows = np.stack([rows[:, :, member], rows[:, :, 1 - member]], axis=2)
            rows = rows.reshape(len(rows), 2, HALF, 2 * modes).transpose(1, 0, 2, 3)
            whole.append(np.concatenate(halves(rows.reshape(-1, 2 * modes)), axis=1))
    return np.stack(whole).reshape(blocks, 2, *whole[0].shape)


def paired_table(blocks, cols):
    modes = 2 * MODE_DEV * blocks
    table = lon_table(blocks * 2 * cols, modes).reshape(blocks, 2, cols, 2, modes)
    table = np.pad(table, ((0, 0), (0, 0), (0, PAD - cols), (0, 0), (0, 0)))
    whole = []
    for place in range(blocks):
        for member in range(2):
            sources = [place, place ^ 1]
            sources += [place ^ (base + m) for m in (member, 1 - member) for base in BASES]
            rows = table[sources][:, :, :, member].transpose(3, 1, 0, 2).reshape(modes, -1)
            whole.append(np.concatenate(halves(rows)))
    return np.stack(whole).reshape(blocks, 2, *whole[0].shape)


def lat_table(rows, lat_count, group):
    total = rows * lat_count
    product = np.arange(total)[:, None] * np.arange(total)[None, :] % total
    angle = product * (2.0 * math.pi / total)
    c, s = np.cos(angle), np.sin(angle)
    basis = np.stack([np.stack([c, s], -1), np.stack([-s, c], -1)], axis=0) * total**-0.5
    basis = basis.reshape(2, total, lat_count, rows // 2, 2, 2).transpose(0, 1, 2, 4, 3, 5)
    size = 2 * total * group
    return np.einsum("akxhqb,mn->akmxhqnb", basis, np.eye(group)).reshape(size, size)


def all_tables(blocks, inner, cols, rows, lat_count, paired):
    table = lat_table(rows, lat_count, SUB)
    size = table.shape[0]
    lat = np.concatenate(halves(table.reshape(size, lat_count, -1).transpose(1, 0, 2)), axis=1)
    lat = lat.reshape(2 * lat_count * size, -1)
    if paired:
        return lat, [0] * 4
    forward, synth = lon_tables(blocks, inner, cols)
    parts = [forward, lat, synth]
    lanes = max(p.shape[1] for p in parts)
    parts = [np.pad(p, ((0, 0), (0, lanes - p.shape[1]))) for p in parts]
    starts = np.cumsum([0] + [len(p) for p in parts])
    return np.concatenate(parts), [int(n) for n in starts]


def split(values):
    high = values.astype(jnp.bfloat16)
    return high, (values - high.astype(jnp.float32)).astype(jnp.bfloat16)


def dot(left, right, dims=((1,), (0,))):
    return lax.dot_general(left, right, (dims, ((), ())), preferred_element_type=jnp.float32)


def dot3(left, right, dims=((1,), (0,))):
    return dot(left[0], right[0], dims) + (dot(left[0], right[1], dims) + dot(left[1], right[0], dims))


def scaled(values, top):
    level = jnp.maximum(top, 1e-30).astype(jnp.bfloat16).astype(jnp.float32)
    return values * (TOP / level), level


def table_rows(ref, start, count, place):
    return ref[pl.ds(pl.multiple_of(start + place * count, PAD), count), :]


def lat_part(ref, start, size, part, x):
    rows = table_rows(ref, start, 2 * size, x)[:, :part]
    return rows[:size], rows[size:]


def encode(values):
    square = values * values
    fourth = square * square
    return (values * fourth * (fourth * fourth)).astype(jnp.bfloat16)


def decode(coded):
    coded = coded.astype(jnp.float32)
    size = jnp.abs(coded)
    root = jnp.exp(jnp.log(jnp.maximum(size, 1e-37)) * (1.0 / POWER))
    root = jnp.where(size > 0.0, root, 0.0)
    return jnp.where(coded < 0.0, -root, root)


def call(kernel, scalars, inputs, outputs, specs=None, scratch=(), flops=0):
    whole = pl.BlockSpec(memory_space=pltpu.VMEM)
    specs = specs or {}
    in_specs = [specs.get(n, whole) for n in range(len(inputs))]
    out_specs = [whole] * len(outputs)
    moved = sum(math.prod(x.shape) * x.dtype.itemsize for x in (*inputs, *outputs))
    return pl.pallas_call(
        kernel,
        grid_spec=pltpu.PrefetchScalarGridSpec(
            num_scalar_prefetch=1,
            grid=(1,),
            in_specs=in_specs,
            out_specs=out_specs,
            scratch_shapes=list(scratch),
        ),
        out_shape=list(outputs),
        compiler_params=pltpu.CompilerParams(vmem_limit_bytes=VMEM),
        cost_estimate=pl.CostEstimate(flops=flops, bytes_accessed=moved, transcendentals=0),
    )(scalars, *inputs)


def pack_kernel(width, place_ref, x_ref, g_ref, out_ref):
    rows, cols, channels = x_ref.shape
    blocks = channels // width
    pairs = rows // 2
    for q in range(pairs):
        lanes = [ref[2 * q + h].astype(jnp.float32) for h in range(2) for ref in (x_ref, g_ref)]
        lanes = [jnp.pad(x, ((0, PAD - cols), (0, 0))) for x in lanes]
        for b in range(blocks):
            pieces = [x[:, b * width : (b + 1) * width] for x in lanes]
            out_ref[b, q * PAD : (q + 1) * PAD, :] = jnp.concatenate(pieces, axis=1).astype(jnp.bfloat16)


def pack_served(width, place, member, x_ref, g_ref, pack_ref):
    rows, cols, channels = x_ref.shape
    lanes = []
    for q in range(rows // 2):
        order = [ref[2 * q + h].astype(jnp.float32) for h in range(2) for ref in (x_ref, g_ref)]
        lanes.append([jnp.pad(x, ((0, PAD - cols), (0, 0))) for x in order])
    for b in range(channels // width):
        other = place ^ b

        @pl.when((other < 2) | ((other & 1) == member))
        def _(b=b, other=other):
            slot = jnp.where(other < 2, other, 2 + (other >> 1))
            for q, order in enumerate(lanes):
                pieces = [x[:, b * width : (b + 1) * width] for x in order]
                piece = jnp.concatenate(pieces, axis=1).astype(jnp.bfloat16)
                pack_ref[slot, q * PAD : (q + 1) * PAD, :] = piece


def own_pack_kernel(width, place_ref, x_ref, g_ref, pack_ref):
    pack_ref[2] = jnp.zeros_like(pack_ref[2])
    pack_served(width, place_ref[0], place_ref[1], x_ref, g_ref, pack_ref)


def pair_kernel(width, place_ref, own_ref, x_ref, g_ref, *refs):
    outs, pack_ref = refs[:-1], refs[-1]
    member = place_ref[1]
    pack_served(width, place_ref[0], member, x_ref, g_ref, pack_ref)
    for n, ref in enumerate(outs):
        slot = n if n < 2 else 2 + BASES[n - 2] // 2
        ref[member] = own_ref[slot]
        ref[1 - member] = pack_ref[slot]


def paired_lon_kernel(place_ref, table_ref, *refs):
    payloads, (coded_ref, spec_ref) = refs[:-2], refs[-2:]
    pairs, modes, lanes = spec_ref.shape
    table = table_ref[0, 0]
    tops = []
    for q in range(pairs):
        data = [ref[m, q * PAD : (q + 1) * PAD, :] for m in range(2) for ref in payloads]
        total = dot(table, jnp.concatenate(data, axis=0))
        spec = total[:modes] + total[modes:]
        spec_ref[q] = spec
        tops.append(jnp.max(jnp.abs(spec), axis=0, keepdims=True))
    code_spectrum(coded_ref, spec_ref, tops)


def code_spectrum(coded_ref, spec_ref, tops):
    pairs, modes, lanes = spec_ref.shape
    values, level = scaled(spec_ref[...], functools.reduce(jnp.maximum, tops))
    coded_ref[: pairs * modes, :] = encode(values).reshape(pairs * modes, lanes)
    coded_ref[pairs * modes :, :] = jnp.broadcast_to(level, (PAD, lanes)).astype(jnp.bfloat16)


def lon_kernel(inner, place_ref, table_ref, *refs):
    fields, (coded_ref, spec_ref) = refs[:inner], refs[inner:]
    member = place_ref[1]
    pairs, modes, lanes = spec_ref.shape
    blocks = fields[0].shape[0]
    tops = []
    for q in range(pairs):
        total = None
        for s, field in enumerate(fields):
            source = lax.rem(member - s + inner, inner)
            data = field[:, q * PAD : (q + 1) * PAD, :].reshape(blocks * PAD, lanes)
            term = dot(table_rows(table_ref, 0, 2 * modes, member * inner + source), data)
            total = term if total is None else total + term
        spec = total[:modes] + total[modes:]
        spec_ref[q] = spec
        tops.append(jnp.max(jnp.abs(spec), axis=0, keepdims=True))
    code_spectrum(coded_ref, spec_ref, tops)


def lat_rows(ref, pairs):
    modes = (ref.shape[0] - PAD) // pairs
    wide = ref.shape[1] // 2
    tile = 2 * SUB
    level = ref[pairs * modes :, :].astype(jnp.float32)[:1] * (1.0 / TOP)
    values = [decode(ref[q * modes : (q + 1) * modes, :]) * level for q in range(pairs)]
    rows = []
    for h in range(2):
        for q in range(pairs):
            parts = [
                values[q][n * tile : (n + 1) * tile, h * wide : (h + 1) * wide] for n in range(modes // tile)
            ]
            rows.append(jnp.concatenate(parts, axis=1))
    return jnp.concatenate(rows, axis=0)


def ready_kernel(pairs, start, place_ref, table_ref, spec_ref, win_ref, bin_ref, wout_ref, *outs):
    part_ref, form_ref, bias_ref = outs
    place, x = place_ref[0], place_ref[2]
    for n, ref in enumerate((win_ref, wout_ref)):
        re, im = ref[0, 0], ref[1, 0]
        form = jnp.concatenate([jnp.concatenate([re, im], axis=1), jnp.concatenate([-im, re], axis=1)], axis=0)
        form_ref[2 * n], form_ref[2 * n + 1] = split(form)
    bias = jnp.concatenate([bin_ref[0, pl.ds(place, 1), :], bin_ref[1, pl.ds(place, 1), :]], axis=1)
    bias_ref[...] = jnp.broadcast_to(bias, bias_ref.shape)
    rows = split(lat_rows(spec_ref, pairs))
    part_ref[...] = dot3(lat_part(table_ref, start, part_ref.shape[0], rows[0].shape[0], x), rows)


def mlp_kernel(lat, inner, shares, pairs, start, scaling, place_ref, table_ref, *refs):
    others = refs[: lat - 1]
    part_ref, form_ref, bias_ref = refs[lat - 1 : lat + 2]
    back_ref, keep_ref, *rest = refs[lat + 2 :]
    send_refs, (w_ref,) = rest[: shares - 1], rest[shares - 1 :]
    member, x = place_ref[1], place_ref[2]
    wide = form_ref.shape[1]
    width = wide // 2
    tile = 2 * SUB
    size = part_ref.shape[0]
    points = size // 2
    part = size // lat
    subs = part_ref.shape[1] // wide

    spectra = part_ref[...]
    for s, ref in enumerate(others):
        source = lax.rem(x - s - 1 + lat, lat)
        matrix = lat_part(table_ref, start, size, part, source)
        spectra = spectra + dot3(matrix, split(lat_rows(ref, pairs)))

    def of_points(start):
        rows = []
        for n in range(subs):
            lanes = slice(n * wide + start, n * wide + start + width)
            rows.append(jnp.concatenate([spectra[:points, lanes], spectra[points:, lanes]], axis=1))
        return jnp.concatenate(rows, axis=0)

    spec_x, spec_g = of_points(0), of_points(width)
    m_in, m_out = (form_ref[0], form_ref[1]), (form_ref[2], form_ref[3])
    point = lax.broadcasted_iota(jnp.int32, (subs * points, 1), 0)
    first = ((point & (SUB - 1)) + jnp.where(point < points, 0, SUB) + member * SUB) == 0
    grad_out = spec_g * jnp.where(first, 1.0, 2.0)
    x_parts, g_parts = split(spec_x), split(grad_out)
    pre = dot3(x_parts, m_in) + bias_ref[:1]
    cdf = 0.5 * (1.0 + lax.erf(pre * root_half))
    hidden = pre * cdf
    slopes = cdf + pre * jnp.exp(-0.5 * pre * pre) * density_norm
    grad_pre = dot3(g_parts, m_out, ((1,), (1,))) * slopes
    p_parts = split(grad_pre)
    grad_spec = dot3(p_parts, m_in, ((1,), (1,)))
    lanes = []
    for n in range(subs):
        piece = grad_spec[n * points : (n + 1) * points]
        lanes.append(jnp.concatenate([piece[:, :width], piece[:, width:]], axis=0))
    matrix = lat_part(table_ref, start, size, part, x)
    back = dot3(matrix, split(jnp.concatenate(lanes, axis=1)), ((0,), (0,)))
    for q in range(pairs):
        for n in range(subs):
            pieces = [
                back[(h * pairs + q) * tile : (h * pairs + q + 1) * tile, n * width : (n + 1) * width]
                for h in range(2)
            ]
            back_ref[q, n * tile : (n + 1) * tile, :] = jnp.concatenate(pieces, axis=1)

    pieces = []
    for left, right in ((x_parts, p_parts), (split(hidden), g_parts)):
        total = dot3(left, right, ((0,), (0,)))
        pieces.append(total[:width, :width] + total[width:, width:])
        pieces.append(total[:width, width:] - total[width:, :width])
    weights = jnp.concatenate(pieces, axis=1) * scaling
    share = width // shares
    w_ref[...] = jnp.zeros_like(w_ref)
    for n in range(shares):
        w_ref[n, :share, :] = weights[n * share : (n + 1) * share]
    w_ref[0, share : share + 1, :wide] = jnp.sum(grad_pre, axis=0, keepdims=True) * scaling
    if shares == 1:
        keep_ref[...] = w_ref[0]
        return
    keep_ref[...] = w_ref[member]
    for s in range(1, shares):
        send_refs[s - 1][...] = w_ref[lax.rem(member + s, shares)]


def synth_kernel(inner, start, place_ref, table_ref, *refs):
    backs, sums, (out_ref, wide_ref) = refs[:inner], refs[inner : 2 * inner], refs[2 * inner :]
    member = place_ref[1]
    pairs, modes, lanes = backs[0].shape
    blocks, total_rows, wide = out_ref.shape
    data_rows = pairs * HALF
    share = lanes // 2 // inner
    for q in range(pairs):
        total = None
        for s, back in enumerate(backs):
            source = lax.rem(member - s + inner, inner)
            rows = table_rows(table_ref, start, 2 * blocks * HALF, member * inner + source)
            term = dot3((rows[:, :modes], rows[:, modes : 2 * modes]), split(back[q]))
            total = term if total is None else total + term
        part = blocks * HALF
        columns = jnp.concatenate([total[:part], total[part:]], axis=1)
        wide_ref[:, q * HALF : (q + 1) * HALF, :] = columns.reshape(blocks, HALF, wide)
    weights = sums[0][...]
    for ref in sums[1:]:
        weights = weights + ref[...]
    coded, tail = code_all(wide_ref[...], weights, share)
    tail = tail[: total_rows - data_rows]
    for b in range(blocks):
        out_ref[b] = jnp.concatenate([coded[b], tail], axis=0).astype(jnp.bfloat16)


def code_all(columns, weights, share):
    rows, wide = columns.shape[1:]
    lanes = wide // 2
    weights, level_w = scaled(weights, jnp.max(jnp.abs(weights), axis=0, keepdims=True))
    top = jnp.max(jnp.max(jnp.abs(columns), axis=0), axis=0, keepdims=True)
    columns, level = scaled(columns, top)
    tail = encode(weights).astype(jnp.float32)
    bias = tail[share : share + 1, :lanes]
    spare = (bias, level_w[:, :lanes], level_w[:, lanes:], level[:, :lanes], level[:, lanes:])
    extra = []
    for n in range(rows // HALF):
        row = jnp.zeros((1, lanes), jnp.float32) if n >= len(spare) else spare[n]
        row = jnp.concatenate([jnp.zeros((1, lanes), jnp.float32), row], axis=1)
        place_row = lax.broadcasted_iota(jnp.int32, (HALF, 1), 0)
        extra.append(jnp.where(place_row == SPARE, row, 0.0))
    extra = jnp.concatenate(extra, axis=0)
    return encode(columns).astype(jnp.float32) + extra, tail


def serve_kernel(place_ref, table_ref, own_ref, other_ref, sum_ref, more_ref, *refs):
    outs, wide_ref = refs[:-1], refs[-1]
    pairs, modes, lanes = own_ref.shape
    count = wide_ref.shape[0]
    share = lanes // 2
    table = table_ref[0, 0]
    matrix = (table[:, : 2 * modes], table[:, 2 * modes :])
    for q in range(pairs):
        total = dot3(matrix, split(jnp.concatenate([own_ref[q], other_ref[q]], axis=0)))
        part = count * HALF
        columns = jnp.concatenate([total[:part], total[part:]], axis=1)
        wide_ref[:, q * HALF : (q + 1) * HALF, :] = columns.reshape(count, HALF, 2 * lanes)
    coded, tail = code_all(wide_ref[...], sum_ref[...] + more_ref[...], share)
    tail = tail[:share]
    for n, ref in enumerate(outs):
        parts = [coded[n]] if n < 2 else [coded[2 * n - 2], coded[2 * n - 1]]
        ref[...] = jnp.concatenate([*parts, tail], axis=0).astype(jnp.bfloat16)


def arrived(ref, member, data_rows):
    raw = ref[...].astype(jnp.float32)
    level = spare_rows(raw, 3, 2) * (1.0 / TOP)
    columns = raw[:data_rows]
    start = data_rows
    if raw.shape[0] == 2 * data_rows + raw.shape[1] // 4:
        start = 2 * data_rows
        columns = jnp.where(member == 0, columns, raw[data_rows:start])
    weights, bias = weight_rows(raw, start)
    return decode(columns) * level, weights, bias


def first_kernel(data_rows, place_ref, *refs):
    member = place_ref[1]
    count = len(refs) - 3
    columns_ref, weights_ref, bias_ref = refs[count:]
    for n in range(count):
        columns_ref[n], weights_ref[n], bias_ref[n : n + 1, :] = arrived(refs[n], member, data_rows)


def last_kernel(data_rows, place_ref, columns_ref, weights_ref, bias_ref, cot_ref, *refs):
    place, member = place_ref[0], place_ref[1]
    lates = refs[: len(BASES)]
    out_ref, win_ref, bin_ref, wout_ref, held_ref = refs[len(BASES) :]
    rows, cols, _ = cot_ref.shape
    blocks = win_ref.shape[1]
    width = win_ref.shape[2]
    pairs = rows // 2

    def settle(source, columns, weights, bias):
        held_ref[source] = columns
        for i in range(4):
            target = (win_ref, wout_ref)[i // 2]
            target[i % 2, source] = weights[:, i * width : (i + 1) * width]
        for k in range(2):
            bin_ref[k, pl.ds(source, 1), :] = bias[:, k * width : (k + 1) * width]

    for n, base in enumerate((0, 1) + BASES):
        source = place ^ (base + member) if n >= 2 else place ^ base
        settle(source, columns_ref[n], weights_ref[n], bias_ref[n : n + 1, :])
    for ref, base in zip(lates, BASES):
        settle(place ^ (base + 1 - member), *arrived(ref, member, data_rows))
    for q in range(pairs):
        for h in range(2):
            parts = []
            for half in range(2):
                start = (2 * half + h) * width
                pieces = [
                    held_ref[b, q * HALF : (q + 1) * HALF, :][:, start : start + width] for b in range(blocks)
                ]
                parts.append(jnp.concatenate(pieces, axis=1))
            column = jnp.concatenate(parts, axis=0)[:cols]
            row = 2 * q + h
            out_ref[row] = (cot_ref[row].astype(jnp.float32) + column).astype(jnp.bfloat16)


def spare_rows(raw, first, count):
    lanes = raw.shape[1] // 2
    rows = [raw[n * HALF + SPARE : n * HALF + SPARE + 1, lanes:] for n in range(first, first + count)]
    return jnp.concatenate(rows, axis=1)


def weight_rows(raw, data_rows):
    level = spare_rows(raw, 1, 2) * (1.0 / TOP)
    bias = decode(spare_rows(raw, 0, 1)) * level[:, : raw.shape[1] // 2]
    return decode(raw[data_rows:]) * level, bias


def columns_kernel(place_ref, data_ref, cot_ref, out_ref, held_ref, bias_ref):
    rows, cols, _ = cot_ref.shape
    blocks, total_rows, wide = data_ref.shape
    width = wide // 4
    pairs = rows // 2
    values = []
    for b in range(blocks):
        raw = data_ref[b].astype(jnp.float32)
        values.append(decode(raw[: pairs * HALF]) * (spare_rows(raw, 3, 2) * (1.0 / TOP)))
        held_ref[b], bias_ref[b : b + 1, :] = weight_rows(raw, pairs * HALF)
    for q in range(pairs):
        for h in range(2):
            parts = []
            for half in range(2):
                start = (2 * half + h) * width
                pieces = [v[q * HALF : (q + 1) * HALF, start : start + width] for v in values]
                parts.append(jnp.concatenate(pieces, axis=1))
            column = jnp.concatenate(parts, axis=0)[:cols]
            row = 2 * q + h
            out_ref[row] = (cot_ref[row].astype(jnp.float32) + column).astype(jnp.bfloat16)


def weights_kernel(inner, share, place_ref, held_ref, own_bias_ref, *refs):
    pieces, (win_ref, bin_ref, wout_ref) = refs[: inner - 1], refs[inner - 1 :]
    member = place_ref[1]
    blocks, rows, wide = held_ref.shape
    width = wide // 4
    data_rows = pieces[0].shape[1] - rows
    for b in range(blocks):
        held = [(held_ref[b], own_bias_ref[b : b + 1, :])]
        held += [weight_rows(ref[b].astype(jnp.float32), data_rows) for ref in pieces]
        for n in range(inner):
            part, bias = held[0]
            for s in range(1, inner):
                chosen = lax.rem(member - s + inner, inner) == n
                part = jnp.where(chosen, held[s][0], part)
                bias = jnp.where(chosen, held[s][1], bias)
            for i in range(4):
                target = (win_ref, wout_ref)[i // 2]
                target[i % 2, b, n * share : (n + 1) * share, :] = part[:share, i * width : (i + 1) * width]
            if n == 0:
                for k in range(2):
                    bin_ref[k, b : b + 1, :] = bias[:, k * width : (k + 1) * width]


def body(features, cotangent, weight_in, bias_in, weight_out):
    lon_count, lat_count = lax.axis_size("lon"), lax.axis_size("lat")
    blocks, width = weight_in.shape[1:3]
    rows, cols, _ = features.shape
    inner = lon_count // blocks
    pairs = rows // 2
    wide = 4 * width
    modes = 2 * MODE_DEV * blocks
    size = 2 * rows * lat_count * SUB
    subs = modes // (2 * SUB)
    lon_place = lax.axis_index("lon")
    lat_place = lax.axis_index("lat")
    scalars = jnp.stack([lon_place // inner, lon_place % inner, lat_place]).astype(jnp.int32)
    scaling = (rows * lat_count * modes // 2 * inner) ** -0.5
    paired = inner == 2 and blocks == 2 + 2 * len(BASES)
    tables, starts = all_tables(blocks, inner, cols, rows, lat_count, paired)
    lon_start, lat_start, synth_start, _ = starts
    shares = 1 if paired else inner
    share = width // shares
    data_rows = pairs * HALF
    total_rows = data_rows + -(-share // 8) * 8
    sum_rows = -(-(share + 1) // 8) * 8
    f32, bf16 = jnp.float32, jnp.bfloat16
    shape = jax.ShapeDtypeStruct

    places = [[g * inner + i for g in range(blocks)] for i in range(inner)]

    def exchange(values):
        return lax.all_to_all(
            values, "lon", split_axis=0, concat_axis=0, tiled=True, axis_index_groups=places
        )

    def to_member(values, step):
        turn = [(i, i // inner * inner + (i + step) % inner) for i in range(lon_count)]
        return lax.ppermute(values, "lon", turn)

    def to_place(values, first, second):
        turn = [(i, (i // 2 ^ (second if i % 2 else first)) * 2 + i % 2) for i in range(lon_count)]
        return lax.ppermute(values, "lon", turn)

    def to_lat(values, step):
        return lax.ppermute(values, "lat", [(i, (i + step) % lat_count) for i in range(lat_count)])

    def by_place(table):
        return pl.BlockSpec((1, 1, *table.shape[2:]), lambda i, s: (s[0], s[1], 0, 0))

    def serve(side, slots):
        sent = [to_place(x, base, base + 1) for x, base in zip(slots, BASES)]
        side, sent[0] = lax.optimization_barrier((to_place(side, 1, 1), sent[0]))
        return [side, *sent], [to_member(x, 1) for x in sent]

    spectrum = dict(
        outputs=(shape((pairs * modes + PAD, wide), bf16),),
        scratch=(pltpu.VMEM((pairs, modes, wide), f32),),
    )
    if paired:
        rows_in = pairs * PAD
        (packed,) = call(
            functools.partial(own_pack_kernel, width),
            scalars,
            (features, cotangent),
            (shape((2 + blocks // 2, rows_in, wide), bf16),),
            flops=10**8,
        )
        own, side, *slots = call(
            functools.partial(pair_kernel, width),
            scalars,
            (packed, to_member(features, 1), to_member(cotangent, 1)),
            [shape((2, rows_in, wide), bf16)] * (2 + len(BASES)),
            scratch=(pltpu.VMEM((2 + blocks // 2, rows_in, wide), bf16),),
        )
        sent, late = serve(side, slots)
        table = paired_table(blocks, cols)
        (coded,) = call(
            paired_lon_kernel, scalars, (table, own, *sent, *late), specs={0: by_place(table)}, **spectrum
        )
    else:
        (packed,) = call(
            functools.partial(pack_kernel, width),
            scalars,
            (features, cotangent),
            (shape((blocks, pairs * PAD, wide), bf16),),
        )
        whole = exchange(packed)
        fields = [whole] + [to_member(whole, s) for s in range(1, inner)]
        (coded,) = call(functools.partial(lon_kernel, inner), scalars, (tables, *fields), **spectrum)
    others = [to_lat(coded, s) for s in range(1, lat_count)]
    block_spec = pl.BlockSpec((2, 1, width, width), lambda i, s: (0, s[0], 0, 0))
    part, forms, bias = call(
        functools.partial(ready_kernel, pairs, lat_start),
        scalars,
        (tables, coded, weight_in, bias_in, weight_out),
        (
            shape((size, 2 * subs * width), f32),
            shape((4, 2 * width, 2 * width), bf16),
            shape((8, 2 * width), f32),
        ),
        specs={2: block_spec, 4: block_spec},
        flops=6 * size * size // lat_count * 2 * subs * width,
    )
    back, keep, *send = call(
        functools.partial(mlp_kernel, lat_count, inner, shares, pairs, lat_start, scaling),
        scalars,
        (tables, *others, part, forms, bias),
        (shape((pairs, modes, 2 * width), f32), *[shape((sum_rows, wide), f32)] * shares),
        scratch=(pltpu.VMEM((shares, sum_rows, wide), f32),),
    )
    backs = [back] + [to_member(back, s) for s in range(1, inner)]
    if paired:
        table = served_table(blocks, cols)
        count = table.shape[2] // PAD
        outs = [share + data_rows] * 2 + [share + 2 * data_rows] * len(BASES)
        own, side, *slots = call(
            serve_kernel,
            scalars,
            (table, *backs, keep, to_member(keep, 1)),
            [shape((n, wide), bf16) for n in outs],
            specs={0: by_place(table)},
            scratch=(pltpu.VMEM((count, data_rows, wide), f32),),
        )
        sent, late = serve(side, slots)
        firsts = [own, *sent]
        held = call(
            functools.partial(first_kernel, data_rows),
            scalars,
            firsts,
            (
                shape((len(firsts), data_rows, wide), f32),
                shape((len(firsts), share, wide), f32),
                shape((len(firsts), 2 * width), f32),
            ),
        )
        return call(
            functools.partial(last_kernel, data_rows),
            scalars,
            (*held, cotangent, *late),
            [shape(x.shape, x.dtype) for x in (features, weight_in, bias_in, weight_out)],
            scratch=(pltpu.VMEM((blocks, data_rows, wide), f32),),
        )
    sums = [keep] + [to_member(send[s - 1], s) for s in range(1, inner)]
    (payload,) = call(
        functools.partial(synth_kernel, inner, synth_start),
        scalars,
        (tables, *backs, *sums),
        (shape((blocks, total_rows, wide), bf16),),
        scratch=(pltpu.VMEM((blocks, pairs * HALF, wide), f32),),
    )
    returned = exchange(payload)
    gathered = [to_member(returned, s) for s in range(1, inner)]
    weight_part = total_rows - pairs * HALF
    grad_features, held, held_bias = call(
        columns_kernel,
        scalars,
        (returned, cotangent),
        (
            shape(features.shape, bf16),
            shape((blocks, weight_part, wide), f32),
            shape((blocks, 2 * width), f32),
        ),
    )
    grad_w_in, grad_b_in, grad_w_out = call(
        functools.partial(weights_kernel, inner, share),
        scalars,
        (held, held_bias, *gathered),
        (shape(weight_in.shape, f32), shape(bias_in.shape, f32), shape(weight_out.shape, f32)),
    )
    return grad_features, grad_w_in, grad_b_in, grad_w_out


def solution(mesh):
    placed = (P("lat", "lon", None), P("lat", "lon", None), P(), P(), P())
    return jax.shard_map(
        body,
        mesh=mesh,
        in_specs=placed,
        out_specs=(P("lat", "lon", None), P(), P(), P()),
        check_vma=False,
    )
```

```python
import functools
import math

import jax
import jax.numpy as jnp
import ml_dtypes
import numpy as np
from jax import lax
from jax.experimental import pallas as pl
from jax.experimental.pallas import tpu as pltpu
from jax.sharding import PartitionSpec as P

MODE_DEV = 4
PAD = 16
HALF = PAD // 2
BASES = (4, 6, 2)
SUB = 4
SPARE = 6
POWER = 13.0
TOP = 2.0**9
VMEM = 40 * 2**20

root_half = math.sqrt(0.5)
density_norm = 1.0 / math.sqrt(2.0 * math.pi)


def halves(table):
    table = table.astype(np.float32)
    high = table.astype(ml_dtypes.bfloat16)
    low = (table - high.astype(np.float32)).astype(ml_dtypes.bfloat16)
    return high, low


def lon_table(columns, mode_count):
    product = np.arange(columns)[:, None] * np.arange(mode_count)[None, :] % columns
    angle = product * (2.0 * math.pi / columns)
    stacked = np.stack([np.cos(angle), -np.sin(angle)], axis=2) * columns**-0.5
    return stacked.reshape(columns, 2 * mode_count)


def lon_tables(blocks, inner, cols):
    modes = MODE_DEV * blocks
    table = lon_table(blocks * inner * cols, modes * inner)
    table = table.reshape(blocks, inner, cols, inner, 2 * modes)
    table = np.pad(table, ((0, 0), (0, 0), (0, PAD - cols), (0, 0), (0, 0)))
    forward = table.transpose(3, 1, 4, 0, 2).reshape(inner, inner, 2 * modes, blocks * PAD)
    split = table.reshape(blocks, inner, 2, HALF, inner, 2 * modes)
    synth = split.transpose(1, 4, 2, 0, 3, 5).reshape(inner, inner, 2 * blocks * HALF, 2 * modes)
    forward, synth = np.concatenate(halves(forward), axis=2), np.concatenate(halves(synth), axis=3)
    return forward.reshape(-1, blocks * PAD), synth.reshape(-1, 4 * modes)


def served(member):
    return [(0, member), (1, member)] + [(base + member, m) for base in BASES for m in range(2)]


def served_table(blocks, cols):
    modes = 2 * MODE_DEV * blocks
    table = lon_table(blocks * 2 * cols, modes).reshape(blocks, 2, cols, 2, modes)
    table = np.pad(table, ((0, 0), (0, 0), (0, PAD - cols), (0, 0), (0, 0)))
    whole = []
    for place in range(blocks):
        for member in range(2):
            rows = np.stack([table[place ^ k, m] for k, m in served(member)])
            rows = np.stack([rows[:, :, member], rows[:, :, 1 - member]], axis=2)
            rows = rows.reshape(len(rows), 2, HALF, 2 * modes).transpose(1, 0, 2, 3)
            whole.append(np.concatenate(halves(rows.reshape(-1, 2 * modes)), axis=1))
    return np.stack(whole).reshape(blocks, 2, *whole[0].shape)


def paired_table(blocks, cols):
    modes = 2 * MODE_DEV * blocks
    table = lon_table(blocks * 2 * cols, modes).reshape(blocks, 2, cols, 2, modes)
    table = np.pad(table, ((0, 0), (0, 0), (0, PAD - cols), (0, 0), (0, 0)))
    whole = []
    for place in range(blocks):
        for member in range(2):
            sources = [(0, 0), (0, 1), (1, member), (1, 1 - member)]
            sources += [(base + m, n) for m in (member, 1 - member) for base in BASES for n in range(2)]
            rows = np.stack([table[place ^ k, n, :, member] for k, n in sources])
            rows = rows.transpose(2, 0, 1).reshape(modes, -1)
            whole.append(np.concatenate(halves(rows)))
    return np.stack(whole).reshape(blocks, 2, *whole[0].shape)


def lat_table(rows, lat_count, group):
    total = rows * lat_count
    product = np.arange(total)[:, None] * np.arange(total)[None, :] % total
    angle = product * (2.0 * math.pi / total)
    c, s = np.cos(angle), np.sin(angle)
    basis = np.stack([np.stack([c, s], -1), np.stack([-s, c], -1)], axis=0) * total**-0.5
    basis = basis.reshape(2, total, lat_count, rows // 2, 2, 2).transpose(0, 1, 2, 4, 3, 5)
    size = 2 * total * group
    return np.einsum("akxhqb,mn->akmxhqnb", basis, np.eye(group)).reshape(size, size)


def all_tables(blocks, inner, cols, rows, lat_count, paired):
    table = lat_table(rows, lat_count, SUB)
    size = table.shape[0]
    lat = np.concatenate(halves(table.reshape(size, lat_count, -1).transpose(1, 0, 2)), axis=1)
    lat = lat.reshape(2 * lat_count * size, -1)
    if paired:
        return lat, [0] * 4
    forward, synth = lon_tables(blocks, inner, cols)
    parts = [forward, lat, synth]
    lanes = max(p.shape[1] for p in parts)
    parts = [np.pad(p, ((0, 0), (0, lanes - p.shape[1]))) for p in parts]
    starts = np.cumsum([0] + [len(p) for p in parts])
    return np.concatenate(parts), [int(n) for n in starts]


def split(values):
    high = values.astype(jnp.bfloat16)
    return high, (values - high.astype(jnp.float32)).astype(jnp.bfloat16)


def dot(left, right, dims=((1,), (0,))):
    return lax.dot_general(left, right, (dims, ((), ())), preferred_element_type=jnp.float32)


def dot3(left, right, dims=((1,), (0,))):
    return dot(left[0], right[0], dims) + (dot(left[0], right[1], dims) + dot(left[1], right[0], dims))


def scaled(values, top):
    level = jnp.maximum(top, 1e-30).astype(jnp.bfloat16).astype(jnp.float32)
    return values * (TOP / level), level


def table_rows(ref, start, count, place):
    return ref[pl.ds(pl.multiple_of(start + place * count, PAD), count), :]


def lat_part(ref, start, size, part, x):
    rows = table_rows(ref, start, 2 * size, x)[:, :part]
    return rows[:size], rows[size:]


def encode(values):
    square = values * values
    fourth = square * square
    return (values * fourth * (fourth * fourth)).astype(jnp.bfloat16)


def decode(coded):
    coded = coded.astype(jnp.float32)
    size = jnp.abs(coded)
    root = jnp.exp(jnp.log(jnp.maximum(size, 1e-37)) * (1.0 / POWER))
    root = jnp.where(size > 0.0, root, 0.0)
    return jnp.where(coded < 0.0, -root, root)


def call(kernel, scalars, inputs, outputs, specs=None, scratch=(), flops=0):
    whole = pl.BlockSpec(memory_space=pltpu.VMEM)
    specs = specs or {}
    in_specs = [specs.get(n, whole) for n in range(len(inputs))]
    out_specs = [whole] * len(outputs)
    moved = sum(math.prod(x.shape) * x.dtype.itemsize for x in (*inputs, *outputs))
    return pl.pallas_call(
        kernel,
        grid_spec=pltpu.PrefetchScalarGridSpec(
            num_scalar_prefetch=1,
            grid=(1,),
            in_specs=in_specs,
            out_specs=out_specs,
            scratch_shapes=list(scratch),
        ),
        out_shape=list(outputs),
        compiler_params=pltpu.CompilerParams(vmem_limit_bytes=VMEM),
        cost_estimate=pl.CostEstimate(flops=flops, bytes_accessed=moved, transcendentals=0),
    )(scalars, *inputs)


def pack_kernel(width, place_ref, x_ref, g_ref, out_ref):
    rows, cols, channels = x_ref.shape
    blocks = channels // width
    pairs = rows // 2
    for q in range(pairs):
        lanes = [ref[2 * q + h].astype(jnp.float32) for h in range(2) for ref in (x_ref, g_ref)]
        lanes = [jnp.pad(x, ((0, PAD - cols), (0, 0))) for x in lanes]
        for b in range(blocks):
            pieces = [x[:, b * width : (b + 1) * width] for x in lanes]
            out_ref[b, q * PAD : (q + 1) * PAD, :] = jnp.concatenate(pieces, axis=1).astype(jnp.bfloat16)


def pack_served(width, place, member, x_ref, g_ref, pack_ref):
    rows, cols, channels = x_ref.shape
    lanes = []
    for q in range(rows // 2):
        order = [ref[2 * q + h].astype(jnp.float32) for h in range(2) for ref in (x_ref, g_ref)]
        lanes.append([jnp.pad(x, ((0, PAD - cols), (0, 0))) for x in order])
    for b in range(channels // width):
        other = place ^ b

        @pl.when((other < 2) | ((other & 1) == member))
        def _(b=b, other=other):
            slot = jnp.where(other < 2, other, 2 + (other >> 1))
            for q, order in enumerate(lanes):
                pieces = [x[:, b * width : (b + 1) * width] for x in order]
                piece = jnp.concatenate(pieces, axis=1).astype(jnp.bfloat16)
                pack_ref[slot, q * PAD : (q + 1) * PAD, :] = piece


def own_pack_kernel(width, place_ref, fields_ref, pack_ref, side_ref):
    pack_ref[2] = jnp.zeros_like(pack_ref[2])
    pack_served(width, place_ref[0], place_ref[1], fields_ref.at[0], fields_ref.at[1], pack_ref)
    side_ref[...] = pack_ref[1]


def pair_kernel(width, place_ref, own_ref, x_ref, g_ref, *refs):
    outs, pack_ref = refs[:-1], refs[-1]
    member = place_ref[1]
    pack_served(width, place_ref[0], member, x_ref, g_ref, pack_ref)
    for n, ref in enumerate(outs):
        slot = 0 if n == 0 else 2 + BASES[n - 1] // 2
        ref[member] = own_ref[slot]
        ref[1 - member] = pack_ref[slot]


def paired_lon_kernel(place_ref, table_ref, own_ref, side_ref, other_side_ref, *refs):
    pieces = [own_ref.at[0], own_ref.at[1], side_ref, other_side_ref]
    pieces += [ref.at[n] for ref in refs[:-2] for n in range(2)]
    coded_ref, spec_ref = refs[-2:]
    pairs, modes, lanes = spec_ref.shape
    table = table_ref[0, 0]
    tops = []
    for q in range(pairs):
        data = [piece[q * PAD : (q + 1) * PAD, :] for piece in pieces]
        total = dot(table, jnp.concatenate(data, axis=0))
        spec = total[:modes] + total[modes:]
        spec_ref[q] = spec
        tops.append(jnp.max(jnp.abs(spec), axis=0, keepdims=True))
    code_spectrum(coded_ref, spec_ref, tops)


def code_spectrum(coded_ref, spec_ref, tops):
    pairs, modes, lanes = spec_ref.shape
    values, level = scaled(spec_ref[...], functools.reduce(jnp.maximum, tops))
    coded_ref[: pairs * modes, :] = encode(values).reshape(pairs * modes, lanes)
    coded_ref[pairs * modes :, :] = jnp.broadcast_to(level, (PAD, lanes)).astype(jnp.bfloat16)


def lon_kernel(inner, place_ref, table_ref, *refs):
    fields, (coded_ref, spec_ref) = refs[:inner], refs[inner:]
    member = place_ref[1]
    pairs, modes, lanes = spec_ref.shape
    blocks = fields[0].shape[0]
    tops = []
    for q in range(pairs):
        total = None
        for s, field in enumerate(fields):
            source = lax.rem(member - s + inner, inner)
            data = field[:, q * PAD : (q + 1) * PAD, :].reshape(blocks * PAD, lanes)
            term = dot(table_rows(table_ref, 0, 2 * modes, member * inner + source), data)
            total = term if total is None else total + term
        spec = total[:modes] + total[modes:]
        spec_ref[q] = spec
        tops.append(jnp.max(jnp.abs(spec), axis=0, keepdims=True))
    code_spectrum(coded_ref, spec_ref, tops)


def lat_rows(ref, pairs):
    modes = (ref.shape[0] - PAD) // pairs
    wide = ref.shape[1] // 2
    tile = 2 * SUB
    level = ref[pairs * modes :, :].astype(jnp.float32)[:1] * (1.0 / TOP)
    values = [decode(ref[q * modes : (q + 1) * modes, :]) * level for q in range(pairs)]
    rows = []
    for h in range(2):
        for q in range(pairs):
            parts = [
                values[q][n * tile : (n + 1) * tile, h * wide : (h + 1) * wide] for n in range(modes // tile)
            ]
            rows.append(jnp.concatenate(parts, axis=1))
    return jnp.concatenate(rows, axis=0)


def ready_kernel(pairs, start, place_ref, table_ref, spec_ref, win_ref, bin_ref, wout_ref, *outs):
    part_ref, form_ref, bias_ref = outs
    place, x = place_ref[0], place_ref[2]
    for n, ref in enumerate((win_ref, wout_ref)):
        re, im = ref[0, 0], ref[1, 0]
        form = jnp.concatenate([jnp.concatenate([re, im], axis=1), jnp.concatenate([-im, re], axis=1)], axis=0)
        form_ref[2 * n], form_ref[2 * n + 1] = split(form)
    bias = jnp.concatenate([bin_ref[0, pl.ds(place, 1), :], bin_ref[1, pl.ds(place, 1), :]], axis=1)
    bias_ref[...] = jnp.broadcast_to(bias, bias_ref.shape)
    rows = split(lat_rows(spec_ref, pairs))
    part_ref[...] = dot3(lat_part(table_ref, start, part_ref.shape[0], rows[0].shape[0], x), rows)


def mlp_kernel(lat, inner, shares, pairs, start, scaling, place_ref, table_ref, *refs):
    others = refs[: lat - 1]
    part_ref, form_ref, bias_ref = refs[lat - 1 : lat + 2]
    back_ref, keep_ref, *rest = refs[lat + 2 :]
    send_refs, (w_ref,) = rest[: shares - 1], rest[shares - 1 :]
    member, x = place_ref[1], place_ref[2]
    wide = form_ref.shape[1]
    width = wide // 2
    tile = 2 * SUB
    size = part_ref.shape[0]
    points = size // 2
    part = size // lat
    subs = part_ref.shape[1] // wide

    spectra = part_ref[...]
    for s, ref in enumerate(others):
        source = lax.rem(x - s - 1 + lat, lat)
        matrix = lat_part(table_ref, start, size, part, source)
        spectra = spectra + dot3(matrix, split(lat_rows(ref, pairs)))

    def of_points(start):
        rows = []
        for n in range(subs):
            lanes = slice(n * wide + start, n * wide + start + width)
            rows.append(jnp.concatenate([spectra[:points, lanes], spectra[points:, lanes]], axis=1))
        return jnp.concatenate(rows, axis=0)

    spec_x, spec_g = of_points(0), of_points(width)
    m_in, m_out = (form_ref[0], form_ref[1]), (form_ref[2], form_ref[3])
    point = lax.broadcasted_iota(jnp.int32, (subs * points, 1), 0)
    first = ((point & (SUB - 1)) + jnp.where(point < points, 0, SUB) + member * SUB) == 0
    grad_out = spec_g * jnp.where(first, 1.0, 2.0)
    x_parts, g_parts = split(spec_x), split(grad_out)
    pre = dot3(x_parts, m_in) + bias_ref[:1]
    cdf = 0.5 * (1.0 + lax.erf(pre * root_half))
    hidden = pre * cdf
    slopes = cdf + pre * jnp.exp(-0.5 * pre * pre) * density_norm
    grad_pre = dot3(g_parts, m_out, ((1,), (1,))) * slopes
    p_parts = split(grad_pre)
    grad_spec = dot3(p_parts, m_in, ((1,), (1,)))
    lanes = []
    for n in range(subs):
        piece = grad_spec[n * points : (n + 1) * points]
        lanes.append(jnp.concatenate([piece[:, :width], piece[:, width:]], axis=0))
    matrix = lat_part(table_ref, start, size, part, x)
    back = dot3(matrix, split(jnp.concatenate(lanes, axis=1)), ((0,), (0,)))
    for q in range(pairs):
        for n in range(subs):
            pieces = [
                back[(h * pairs + q) * tile : (h * pairs + q + 1) * tile, n * width : (n + 1) * width]
                for h in range(2)
            ]
            back_ref[q, n * tile : (n + 1) * tile, :] = jnp.concatenate(pieces, axis=1)

    pieces = []
    for left, right in ((x_parts, p_parts), (split(hidden), g_parts)):
        total = dot3(left, right, ((0,), (0,)))
        pieces.append(total[:width, :width] + total[width:, width:])
        pieces.append(total[:width, width:] - total[width:, :width])
    weights = jnp.concatenate(pieces, axis=1) * scaling
    share = width // shares
    w_ref[...] = jnp.zeros_like(w_ref)
    for n in range(shares):
        w_ref[n, :share, :] = weights[n * share : (n + 1) * share]
    w_ref[0, share : share + 1, :wide] = jnp.sum(grad_pre, axis=0, keepdims=True) * scaling
    if shares == 1:
        keep_ref[...] = w_ref[0]
        return
    keep_ref[...] = w_ref[member]
    for s in range(1, shares):
        send_refs[s - 1][...] = w_ref[lax.rem(member + s, shares)]


def synth_kernel(inner, start, place_ref, table_ref, *refs):
    backs, sums, (out_ref, wide_ref) = refs[:inner], refs[inner : 2 * inner], refs[2 * inner :]
    member = place_ref[1]
    pairs, modes, lanes = backs[0].shape
    blocks, total_rows, wide = out_ref.shape
    data_rows = pairs * HALF
    share = lanes // 2 // inner
    for q in range(pairs):
        total = None
        for s, back in enumerate(backs):
            source = lax.rem(member - s + inner, inner)
            rows = table_rows(table_ref, start, 2 * blocks * HALF, member * inner + source)
            term = dot3((rows[:, :modes], rows[:, modes : 2 * modes]), split(back[q]))
            total = term if total is None else total + term
        part = blocks * HALF
        columns = jnp.concatenate([total[:part], total[part:]], axis=1)
        wide_ref[:, q * HALF : (q + 1) * HALF, :] = columns.reshape(blocks, HALF, wide)
    weights = sums[0][...]
    for ref in sums[1:]:
        weights = weights + ref[...]
    coded, tail = code_all(wide_ref[...], weights, share)
    tail = tail[: total_rows - data_rows]
    for b in range(blocks):
        out_ref[b] = jnp.concatenate([coded[b], tail], axis=0).astype(jnp.bfloat16)


def code_all(columns, weights, share):
    rows, wide = columns.shape[1:]
    lanes = wide // 2
    weights, level_w = scaled(weights, jnp.max(jnp.abs(weights), axis=0, keepdims=True))
    top = jnp.max(jnp.max(jnp.abs(columns), axis=0), axis=0, keepdims=True)
    columns, level = scaled(columns, top)
    tail = encode(weights).astype(jnp.float32)
    bias = tail[share : share + 1, :lanes]
    spare = (bias, level_w[:, :lanes], level_w[:, lanes:], level[:, :lanes], level[:, lanes:])
    extra = []
    for n in range(rows // HALF):
        row = jnp.zeros((1, lanes), jnp.float32) if n >= len(spare) else spare[n]
        row = jnp.concatenate([jnp.zeros((1, lanes), jnp.float32), row], axis=1)
        place_row = lax.broadcasted_iota(jnp.int32, (HALF, 1), 0)
        extra.append(jnp.where(place_row == SPARE, row, 0.0))
    extra = jnp.concatenate(extra, axis=0)
    return encode(columns).astype(jnp.float32) + extra, tail


def serve_kernel(place_ref, table_ref, own_ref, other_ref, sum_ref, more_ref, *refs):
    outs, wide_ref = refs[:-1], refs[-1]
    pairs, modes, lanes = own_ref.shape
    count = wide_ref.shape[0]
    share = lanes // 2
    table = table_ref[0, 0]
    matrix = (table[:, : 2 * modes], table[:, 2 * modes :])
    for q in range(pairs):
        total = dot3(matrix, split(jnp.concatenate([own_ref[q], other_ref[q]], axis=0)))
        part = count * HALF
        columns = jnp.concatenate([total[:part], total[part:]], axis=1)
        wide_ref[:, q * HALF : (q + 1) * HALF, :] = columns.reshape(count, HALF, 2 * lanes)
    coded, tail = code_all(wide_ref[...], sum_ref[...] + more_ref[...], share)
    tail = tail[:share]
    for n, ref in enumerate(outs):
        parts = [coded[n]] if n < 2 else [coded[2 * n - 2], coded[2 * n - 1]]
        ref[...] = jnp.concatenate([*parts, tail], axis=0).astype(jnp.bfloat16)


def arrived(ref, member, data_rows):
    raw = ref[...].astype(jnp.float32)
    level = spare_rows(raw, 3, 2) * (1.0 / TOP)
    columns = raw[:data_rows]
    start = data_rows
    if raw.shape[0] == 2 * data_rows + raw.shape[1] // 4:
        start = 2 * data_rows
        columns = jnp.where(member == 0, columns, raw[data_rows:start])
    weights, bias = weight_rows(raw, start)
    return decode(columns) * level, weights, bias


def first_kernel(data_rows, place_ref, *refs):
    member = place_ref[1]
    count = len(refs) - 3
    columns_ref, weights_ref, bias_ref = refs[count:]
    for n in range(count):
        columns_ref[n], weights_ref[n], bias_ref[n : n + 1, :] = arrived(refs[n], member, data_rows)


def last_kernel(data_rows, place_ref, columns_ref, weights_ref, bias_ref, cot_ref, *refs):
    place, member = place_ref[0], place_ref[1]
    lates = refs[: len(BASES)]
    out_ref, win_ref, bin_ref, wout_ref, held_ref = refs[len(BASES) :]
    rows, cols, _ = cot_ref.shape
    blocks = win_ref.shape[1]
    width = win_ref.shape[2]
    pairs = rows // 2

    def settle(source, columns, weights, bias):
        held_ref[source] = columns
        for i in range(4):
            target = (win_ref, wout_ref)[i // 2]
            target[i % 2, source] = weights[:, i * width : (i + 1) * width]
        for k in range(2):
            bin_ref[k, pl.ds(source, 1), :] = bias[:, k * width : (k + 1) * width]

    for n, base in enumerate((0, 1) + BASES):
        source = place ^ (base + member) if n >= 2 else place ^ base
        settle(source, columns_ref[n], weights_ref[n], bias_ref[n : n + 1, :])
    for ref, base in zip(lates, BASES):
        settle(place ^ (base + 1 - member), *arrived(ref, member, data_rows))
    for q in range(pairs):
        for h in range(2):
            parts = []
            for half in range(2):
                start = (2 * half + h) * width
                pieces = [
                    held_ref[b, q * HALF : (q + 1) * HALF, :][:, start : start + width] for b in range(blocks)
                ]
                parts.append(jnp.concatenate(pieces, axis=1))
            column = jnp.concatenate(parts, axis=0)[:cols]
            row = 2 * q + h
            out_ref[row] = (cot_ref[row].astype(jnp.float32) + column).astype(jnp.bfloat16)


def spare_rows(raw, first, count):
    lanes = raw.shape[1] // 2
    rows = [raw[n * HALF + SPARE : n * HALF + SPARE + 1, lanes:] for n in range(first, first + count)]
    return jnp.concatenate(rows, axis=1)


def weight_rows(raw, data_rows):
    level = spare_rows(raw, 1, 2) * (1.0 / TOP)
    bias = decode(spare_rows(raw, 0, 1)) * level[:, : raw.shape[1] // 2]
    return decode(raw[data_rows:]) * level, bias


def columns_kernel(place_ref, data_ref, cot_ref, out_ref, held_ref, bias_ref):
    rows, cols, _ = cot_ref.shape
    blocks, total_rows, wide = data_ref.shape
    width = wide // 4
    pairs = rows // 2
    values = []
    for b in range(blocks):
        raw = data_ref[b].astype(jnp.float32)
        values.append(decode(raw[: pairs * HALF]) * (spare_rows(raw, 3, 2) * (1.0 / TOP)))
        held_ref[b], bias_ref[b : b + 1, :] = weight_rows(raw, pairs * HALF)
    for q in range(pairs):
        for h in range(2):
            parts = []
            for half in range(2):
                start = (2 * half + h) * width
                pieces = [v[q * HALF : (q + 1) * HALF, start : start + width] for v in values]
                parts.append(jnp.concatenate(pieces, axis=1))
            column = jnp.concatenate(parts, axis=0)[:cols]
            row = 2 * q + h
            out_ref[row] = (cot_ref[row].astype(jnp.float32) + column).astype(jnp.bfloat16)


def weights_kernel(inner, share, place_ref, held_ref, own_bias_ref, *refs):
    pieces, (win_ref, bin_ref, wout_ref) = refs[: inner - 1], refs[inner - 1 :]
    member = place_ref[1]
    blocks, rows, wide = held_ref.shape
    width = wide // 4
    data_rows = pieces[0].shape[1] - rows
    for b in range(blocks):
        held = [(held_ref[b], own_bias_ref[b : b + 1, :])]
        held += [weight_rows(ref[b].astype(jnp.float32), data_rows) for ref in pieces]
        for n in range(inner):
            part, bias = held[0]
            for s in range(1, inner):
                chosen = lax.rem(member - s + inner, inner) == n
                part = jnp.where(chosen, held[s][0], part)
                bias = jnp.where(chosen, held[s][1], bias)
            for i in range(4):
                target = (win_ref, wout_ref)[i // 2]
                target[i % 2, b, n * share : (n + 1) * share, :] = part[:share, i * width : (i + 1) * width]
            if n == 0:
                for k in range(2):
                    bin_ref[k, b : b + 1, :] = bias[:, k * width : (k + 1) * width]


def body(features, cotangent, weight_in, bias_in, weight_out):
    lon_count, lat_count = lax.axis_size("lon"), lax.axis_size("lat")
    blocks, width = weight_in.shape[1:3]
    rows, cols, _ = features.shape
    inner = lon_count // blocks
    pairs = rows // 2
    wide = 4 * width
    modes = 2 * MODE_DEV * blocks
    size = 2 * rows * lat_count * SUB
    subs = modes // (2 * SUB)
    lon_place = lax.axis_index("lon")
    lat_place = lax.axis_index("lat")
    scalars = jnp.stack([lon_place // inner, lon_place % inner, lat_place]).astype(jnp.int32)
    scaling = (rows * lat_count * modes // 2 * inner) ** -0.5
    paired = inner == 2 and blocks == 2 + 2 * len(BASES)
    tables, starts = all_tables(blocks, inner, cols, rows, lat_count, paired)
    lon_start, lat_start, synth_start, _ = starts
    shares = 1 if paired else inner
    share = width // shares
    data_rows = pairs * HALF
    total_rows = data_rows + -(-share // 8) * 8
    sum_rows = -(-(share + 1) // 8) * 8
    f32, bf16 = jnp.float32, jnp.bfloat16
    shape = jax.ShapeDtypeStruct

    places = [[g * inner + i for g in range(blocks)] for i in range(inner)]

    def exchange(values):
        return lax.all_to_all(
            values, "lon", split_axis=0, concat_axis=0, tiled=True, axis_index_groups=places
        )

    def to_member(values, step):
        turn = [(i, i // inner * inner + (i + step) % inner) for i in range(lon_count)]
        return lax.ppermute(values, "lon", turn)

    def to_place(values, first, second):
        turn = [(i, (i // 2 ^ (second if i % 2 else first)) * 2 + i % 2) for i in range(lon_count)]
        return lax.ppermute(values, "lon", turn)

    def to_lat(values, step):
        return lax.ppermute(values, "lat", [(i, (i + step) % lat_count) for i in range(lat_count)])

    def by_place(table):
        return pl.BlockSpec((1, 1, *table.shape[2:]), lambda i, s: (s[0], s[1], 0, 0))

    def serve(slots):
        return [to_place(x, base, base + 1) for x, base in zip(slots, BASES)]

    spectrum = dict(
        outputs=(shape((pairs * modes + PAD, wide), bf16),),
        scratch=(pltpu.VMEM((pairs, modes, wide), f32),),
    )
    if paired:
        rows_in = pairs * PAD
        packed, side = call(
            functools.partial(own_pack_kernel, width),
            scalars,
            (jnp.stack([features, cotangent]),),
            (shape((2 + blocks // 2, rows_in, wide), bf16), shape((rows_in, wide), bf16)),
            flops=10**8,
        )
        own, *slots = call(
            functools.partial(pair_kernel, width),
            scalars,
            (packed, to_member(features, 1), to_member(cotangent, 1)),
            [shape((2, rows_in, wide), bf16)] * (1 + len(BASES)),
            scratch=(pltpu.VMEM((2 + blocks // 2, rows_in, wide), bf16),),
        )
        side = to_place(side, 1, 1)
        sent = [side, *serve(slots)]
        late = [to_member(x, 1) for x in sent]
        sent, late = [side, late[0], *sent[1:]], late[1:]
        table = paired_table(blocks, cols)
        (coded,) = call(
            paired_lon_kernel, scalars, (table, own, *sent, *late), specs={0: by_place(table)}, **spectrum
        )
    else:
        (packed,) = call(
            functools.partial(pack_kernel, width),
            scalars,
            (features, cotangent),
            (shape((blocks, pairs * PAD, wide), bf16),),
        )
        whole = exchange(packed)
        fields = [whole] + [to_member(whole, s) for s in range(1, inner)]
        (coded,) = call(functools.partial(lon_kernel, inner), scalars, (tables, *fields), **spectrum)
    others = [to_lat(coded, s) for s in range(1, lat_count)]
    block_spec = pl.BlockSpec((2, 1, width, width), lambda i, s: (0, s[0], 0, 0))
    part, forms, bias = call(
        functools.partial(ready_kernel, pairs, lat_start),
        scalars,
        (tables, coded, weight_in, bias_in, weight_out),
        (
            shape((size, 2 * subs * width), f32),
            shape((4, 2 * width, 2 * width), bf16),
            shape((8, 2 * width), f32),
        ),
        specs={2: block_spec, 4: block_spec},
        flops=6 * size * size // lat_count * 2 * subs * width,
    )
    back, keep, *send = call(
        functools.partial(mlp_kernel, lat_count, inner, shares, pairs, lat_start, scaling),
        scalars,
        (tables, *others, part, forms, bias),
        (shape((pairs, modes, 2 * width), f32), *[shape((sum_rows, wide), f32)] * shares),
        scratch=(pltpu.VMEM((shares, sum_rows, wide), f32),),
    )
    backs = [back] + [to_member(back, s) for s in range(1, inner)]
    if paired:
        table = served_table(blocks, cols)
        count = table.shape[2] // PAD
        outs = [share + data_rows] * 2 + [share + 2 * data_rows] * len(BASES)
        own, side, *slots = call(
            serve_kernel,
            scalars,
            (table, *backs, keep, to_member(keep, 1)),
            [shape((n, wide), bf16) for n in outs],
            specs={0: by_place(table)},
            scratch=(pltpu.VMEM((count, data_rows, wide), f32),),
        )
        sent = serve(slots)
        side, sent[0] = lax.optimization_barrier((to_place(side, 1, 1), sent[0]))
        firsts, late = [own, side, *sent], [to_member(x, 1) for x in sent]
        held = call(
            functools.partial(first_kernel, data_rows),
            scalars,
            firsts,
            (
                shape((len(firsts), data_rows, wide), f32),
                shape((len(firsts), share, wide), f32),
                shape((len(firsts), 2 * width), f32),
            ),
        )
        return call(
            functools.partial(last_kernel, data_rows),
            scalars,
            (*held, cotangent, *late),
            [shape(x.shape, x.dtype) for x in (features, weight_in, bias_in, weight_out)],
            scratch=(pltpu.VMEM((blocks, data_rows, wide), f32),),
        )
    sums = [keep] + [to_member(send[s - 1], s) for s in range(1, inner)]
    (payload,) = call(
        functools.partial(synth_kernel, inner, synth_start),
        scalars,
        (tables, *backs, *sums),
        (shape((blocks, total_rows, wide), bf16),),
        scratch=(pltpu.VMEM((blocks, pairs * HALF, wide), f32),),
    )
    returned = exchange(payload)
    gathered = [to_member(returned, s) for s in range(1, inner)]
    weight_part = total_rows - pairs * HALF
    grad_features, held, held_bias = call(
        columns_kernel,
        scalars,
        (returned, cotangent),
        (
            shape(features.shape, bf16),
            shape((blocks, weight_part, wide), f32),
            shape((blocks, 2 * width), f32),
        ),
    )
    grad_w_in, grad_b_in, grad_w_out = call(
        functools.partial(weights_kernel, inner, share),
        scalars,
        (held, held_bias, *gathered),
        (shape(weight_in.shape, f32), shape(bias_in.shape, f32), shape(weight_out.shape, f32)),
    )
    return grad_features, grad_w_in, grad_b_in, grad_w_out


def solution(mesh):
    placed = (P("lat", "lon", None), P("lat", "lon", None), P(), P(), P())
    return jax.shard_map(
        body,
        mesh=mesh,
        in_specs=placed,
        out_specs=(P("lat", "lon", None), P(), P(), P()),
        check_vma=False,
    )
```

```python
import functools
import math

import jax
import jax.numpy as jnp
import ml_dtypes
import numpy as np
from jax import lax
from jax.experimental import pallas as pl
from jax.experimental.pallas import tpu as pltpu
from jax.sharding import PartitionSpec as P

MODE_DEV = 4
PAD = 16
HALF = PAD // 2
BASES = (4, 6, 2)
SUB = 4
SPARE = 6
POWER = 13.0
TOP = 2.0**9
VMEM = 40 * 2**20

root_half = math.sqrt(0.5)
density_norm = 1.0 / math.sqrt(2.0 * math.pi)


def halves(table):
    table = table.astype(np.float32)
    high = table.astype(ml_dtypes.bfloat16)
    low = (table - high.astype(np.float32)).astype(ml_dtypes.bfloat16)
    return high, low


def lon_table(columns, mode_count):
    product = np.arange(columns)[:, None] * np.arange(mode_count)[None, :] % columns
    angle = product * (2.0 * math.pi / columns)
    stacked = np.stack([np.cos(angle), -np.sin(angle)], axis=2) * columns**-0.5
    return stacked.reshape(columns, 2 * mode_count)


def lon_tables(blocks, inner, cols):
    modes = MODE_DEV * blocks
    table = lon_table(blocks * inner * cols, modes * inner)
    table = table.reshape(blocks, inner, cols, inner, 2 * modes)
    table = np.pad(table, ((0, 0), (0, 0), (0, PAD - cols), (0, 0), (0, 0)))
    forward = table.transpose(3, 1, 4, 0, 2).reshape(inner, inner, 2 * modes, blocks * PAD)
    split = table.reshape(blocks, inner, 2, HALF, inner, 2 * modes)
    synth = split.transpose(1, 4, 2, 0, 3, 5).reshape(inner, inner, 2 * blocks * HALF, 2 * modes)
    forward, synth = np.concatenate(halves(forward), axis=2), np.concatenate(halves(synth), axis=3)
    return forward.reshape(-1, blocks * PAD), synth.reshape(-1, 4 * modes)


def served(member):
    return [(0, member), (1, member)] + [(base + member, m) for base in BASES for m in range(2)]


def served_table(blocks, cols):
    modes = 2 * MODE_DEV * blocks
    table = lon_table(blocks * 2 * cols, modes).reshape(blocks, 2, cols, 2, modes)
    table = np.pad(table, ((0, 0), (0, 0), (0, PAD - cols), (0, 0), (0, 0)))
    whole = []
    for place in range(blocks):
        for member in range(2):
            rows = np.stack([table[place ^ k, m] for k, m in served(member)])
            rows = np.stack([rows[:, :, member], rows[:, :, 1 - member]], axis=2)
            rows = rows.reshape(len(rows), 2, HALF, 2 * modes).transpose(1, 0, 2, 3)
            whole.append(np.concatenate(halves(rows.reshape(-1, 2 * modes)), axis=1))
    return np.stack(whole).reshape(blocks, 2, *whole[0].shape)


def paired_table(blocks, cols):
    modes = 2 * MODE_DEV * blocks
    table = lon_table(blocks * 2 * cols, modes).reshape(blocks, 2, cols, 2, modes)
    table = np.pad(table, ((0, 0), (0, 0), (0, PAD - cols), (0, 0), (0, 0)))
    whole = []
    for place in range(blocks):
        for member in range(2):
            sources = [(0, 0), (0, 1), (1, member), (1, 1 - member)]
            sources += [(base + m, n) for m in (member, 1 - member) for base in BASES for n in range(2)]
            rows = np.stack([table[place ^ k, n, :, member] for k, n in sources])
            rows = rows.transpose(2, 0, 1).reshape(modes, -1)
            whole.append(np.concatenate(halves(rows)))
    return np.stack(whole).reshape(blocks, 2, *whole[0].shape)


def lat_table(rows, lat_count, group):
    total = rows * lat_count
    product = np.arange(total)[:, None] * np.arange(total)[None, :] % total
    angle = product * (2.0 * math.pi / total)
    c, s = np.cos(angle), np.sin(angle)
    basis = np.stack([np.stack([c, s], -1), np.stack([-s, c], -1)], axis=0) * total**-0.5
    basis = basis.reshape(2, total, lat_count, rows // 2, 2, 2).transpose(0, 1, 2, 4, 3, 5)
    size = 2 * total * group
    return np.einsum("akxhqb,mn->akmxhqnb", basis, np.eye(group)).reshape(size, size)


def all_tables(blocks, inner, cols, rows, lat_count, paired):
    table = lat_table(rows, lat_count, SUB)
    size = table.shape[0]
    lat = np.concatenate(halves(table.reshape(size, lat_count, -1).transpose(1, 0, 2)), axis=1)
    lat = lat.reshape(2 * lat_count * size, -1)
    if paired:
        return lat, [0] * 4
    forward, synth = lon_tables(blocks, inner, cols)
    parts = [forward, lat, synth]
    lanes = max(p.shape[1] for p in parts)
    parts = [np.pad(p, ((0, 0), (0, lanes - p.shape[1]))) for p in parts]
    starts = np.cumsum([0] + [len(p) for p in parts])
    return np.concatenate(parts), [int(n) for n in starts]


def split(values):
    high = values.astype(jnp.bfloat16)
    return high, (values - high.astype(jnp.float32)).astype(jnp.bfloat16)


def dot(left, right, dims=((1,), (0,))):
    return lax.dot_general(left, right, (dims, ((), ())), preferred_element_type=jnp.float32)


def dot3(left, right, dims=((1,), (0,))):
    return dot(left[0], right[0], dims) + (dot(left[0], right[1], dims) + dot(left[1], right[0], dims))


def scaled(values, top):
    level = jnp.maximum(top, 1e-30).astype(jnp.bfloat16).astype(jnp.float32)
    return values * (TOP / level), level


def table_rows(ref, start, count, place):
    return ref[pl.ds(pl.multiple_of(start + place * count, PAD), count), :]


def lat_part(ref, start, size, part, x):
    rows = table_rows(ref, start, 2 * size, x)[:, :part]
    return rows[:size], rows[size:]


def encode(values):
    square = values * values
    fourth = square * square
    return (values * fourth * (fourth * fourth)).astype(jnp.bfloat16)


def decode(coded):
    coded = coded.astype(jnp.float32)
    size = jnp.abs(coded)
    root = jnp.exp(jnp.log(jnp.maximum(size, 1e-37)) * (1.0 / POWER))
    root = jnp.where(size > 0.0, root, 0.0)
    return jnp.where(coded < 0.0, -root, root)


def call(kernel, scalars, inputs, outputs, specs=None, scratch=(), flops=0):
    whole = pl.BlockSpec(memory_space=pltpu.VMEM)
    specs = specs or {}
    in_specs = [specs.get(n, whole) for n in range(len(inputs))]
    out_specs = [whole] * len(outputs)
    moved = sum(math.prod(x.shape) * x.dtype.itemsize for x in (*inputs, *outputs))
    return pl.pallas_call(
        kernel,
        grid_spec=pltpu.PrefetchScalarGridSpec(
            num_scalar_prefetch=1,
            grid=(1,),
            in_specs=in_specs,
            out_specs=out_specs,
            scratch_shapes=list(scratch),
        ),
        out_shape=list(outputs),
        compiler_params=pltpu.CompilerParams(vmem_limit_bytes=VMEM),
        cost_estimate=pl.CostEstimate(flops=flops, bytes_accessed=moved, transcendentals=0),
    )(scalars, *inputs)


def pack_kernel(width, place_ref, x_ref, g_ref, out_ref):
    pack_all(width, x_ref, g_ref, out_ref)


def pack_all(width, x_ref, g_ref, out_ref):
    rows, cols, channels = x_ref.shape
    for q in range(rows // 2):
        lanes = [ref[2 * q + h].astype(jnp.float32) for h in range(2) for ref in (x_ref, g_ref)]
        lanes = [jnp.pad(x, ((0, PAD - cols), (0, 0))) for x in lanes]
        for b in range(channels // width):
            pieces = [x[:, b * width : (b + 1) * width] for x in lanes]
            out_ref[b, q * PAD : (q + 1) * PAD, :] = jnp.concatenate(pieces, axis=1).astype(jnp.bfloat16)


def own_pack_kernel(width, place_ref, fields_ref, pack_ref, side_ref):
    pack_all(width, fields_ref.at[0], fields_ref.at[1], pack_ref)
    side_ref[...] = pack_ref[place_ref[0] ^ 1]


def pair_kernel(width, place_ref, own_ref, x_ref, g_ref, *refs):
    outs, pack_ref = refs[:-1], refs[-1]
    place, member = place_ref[0], place_ref[1]
    pack_all(width, x_ref, g_ref, pack_ref)
    for n, ref in enumerate(outs):
        target = place if n == 0 else place ^ (BASES[n - 1] + member)
        ref[member] = own_ref[target]
        ref[1 - member] = pack_ref[target]


def paired_lon_kernel(place_ref, table_ref, own_ref, side_ref, other_side_ref, *refs):
    pieces = [own_ref.at[0], own_ref.at[1], side_ref, other_side_ref]
    pieces += [ref.at[n] for ref in refs[:-2] for n in range(2)]
    coded_ref, spec_ref = refs[-2:]
    pairs, modes, lanes = spec_ref.shape
    table = table_ref[0, 0]
    tops = []
    for q in range(pairs):
        data = [piece[q * PAD : (q + 1) * PAD, :] for piece in pieces]
        total = dot(table, jnp.concatenate(data, axis=0))
        spec = total[:modes] + total[modes:]
        spec_ref[q] = spec
        tops.append(jnp.max(jnp.abs(spec), axis=0, keepdims=True))
    code_spectrum(coded_ref, spec_ref, tops)


def code_spectrum(coded_ref, spec_ref, tops):
    pairs, modes, lanes = spec_ref.shape
    values, level = scaled(spec_ref[...], functools.reduce(jnp.maximum, tops))
    coded_ref[: pairs * modes, :] = encode(values).reshape(pairs * modes, lanes)
    coded_ref[pairs * modes :, :] = jnp.broadcast_to(level, (PAD, lanes)).astype(jnp.bfloat16)


def lon_kernel(inner, place_ref, table_ref, *refs):
    fields, (coded_ref, spec_ref) = refs[:inner], refs[inner:]
    member = place_ref[1]
    pairs, modes, lanes = spec_ref.shape
    blocks = fields[0].shape[0]
    tops = []
    for q in range(pairs):
        total = None
        for s, field in enumerate(fields):
            source = lax.rem(member - s + inner, inner)
            data = field[:, q * PAD : (q + 1) * PAD, :].reshape(blocks * PAD, lanes)
            term = dot(table_rows(table_ref, 0, 2 * modes, member * inner + source), data)
            total = term if total is None else total + term
        spec = total[:modes] + total[modes:]
        spec_ref[q] = spec
        tops.append(jnp.max(jnp.abs(spec), axis=0, keepdims=True))
    code_spectrum(coded_ref, spec_ref, tops)


def lat_rows(ref, pairs):
    modes = (ref.shape[0] - PAD) // pairs
    wide = ref.shape[1] // 2
    tile = 2 * SUB
    level = ref[pairs * modes :, :].astype(jnp.float32)[:1] * (1.0 / TOP)
    values = [decode(ref[q * modes : (q + 1) * modes, :]) * level for q in range(pairs)]
    rows = []
    for h in range(2):
        for q in range(pairs):
            parts = [
                values[q][n * tile : (n + 1) * tile, h * wide : (h + 1) * wide] for n in range(modes // tile)
            ]
            rows.append(jnp.concatenate(parts, axis=1))
    return jnp.concatenate(rows, axis=0)


def ready_kernel(pairs, start, place_ref, table_ref, spec_ref, win_ref, bin_ref, wout_ref, *outs):
    part_ref, form_ref, bias_ref = outs
    place, x = place_ref[0], place_ref[2]
    for n, ref in enumerate((win_ref, wout_ref)):
        re, im = ref[0, 0], ref[1, 0]
        form = jnp.concatenate([jnp.concatenate([re, im], axis=1), jnp.concatenate([-im, re], axis=1)], axis=0)
        form_ref[2 * n], form_ref[2 * n + 1] = split(form)
    bias = jnp.concatenate([bin_ref[0, pl.ds(place, 1), :], bin_ref[1, pl.ds(place, 1), :]], axis=1)
    bias_ref[...] = jnp.broadcast_to(bias, bias_ref.shape)
    rows = split(lat_rows(spec_ref, pairs))
    part_ref[...] = dot3(lat_part(table_ref, start, part_ref.shape[0], rows[0].shape[0], x), rows)


def mlp_kernel(lat, inner, shares, pairs, start, scaling, place_ref, table_ref, *refs):
    others = refs[: lat - 1]
    part_ref, form_ref, bias_ref = refs[lat - 1 : lat + 2]
    back_ref, *rest = refs[lat + 2 :]
    if shares > 1:
        keep_ref, *send_refs, w_ref = rest
    member, x = place_ref[1], place_ref[2]
    wide = form_ref.shape[1]
    width = wide // 2
    tile = 2 * SUB
    size = part_ref.shape[0]
    points = size // 2
    part = size // lat
    subs = part_ref.shape[1] // wide

    spectra = part_ref[...]
    for s, ref in enumerate(others):
        source = lax.rem(x - s - 1 + lat, lat)
        matrix = lat_part(table_ref, start, size, part, source)
        spectra = spectra + dot3(matrix, split(lat_rows(ref, pairs)))

    def of_points(start):
        rows = []
        for n in range(subs):
            lanes = slice(n * wide + start, n * wide + start + width)
            rows.append(jnp.concatenate([spectra[:points, lanes], spectra[points:, lanes]], axis=1))
        return jnp.concatenate(rows, axis=0)

    spec_x, spec_g = of_points(0), of_points(width)
    m_in, m_out = (form_ref[0], form_ref[1]), (form_ref[2], form_ref[3])
    point = lax.broadcasted_iota(jnp.int32, (subs * points, 1), 0)
    first = ((point & (SUB - 1)) + jnp.where(point < points, 0, SUB) + member * SUB) == 0
    grad_out = spec_g * jnp.where(first, 1.0, 2.0)
    x_parts, g_parts = split(spec_x), split(grad_out)
    pre = dot3(x_parts, m_in) + bias_ref[:1]
    cdf = 0.5 * (1.0 + lax.erf(pre * root_half))
    hidden = pre * cdf
    slopes = cdf + pre * jnp.exp(-0.5 * pre * pre) * density_norm
    grad_pre = dot3(g_parts, m_out, ((1,), (1,))) * slopes
    p_parts = split(grad_pre)
    grad_spec = dot3(p_parts, m_in, ((1,), (1,)))
    lanes = []
    for n in range(subs):
        piece = grad_spec[n * points : (n + 1) * points]
        lanes.append(jnp.concatenate([piece[:, :width], piece[:, width:]], axis=0))
    matrix = lat_part(table_ref, start, size, part, x)
    back = dot3(matrix, split(jnp.concatenate(lanes, axis=1)), ((0,), (0,)))
    for q in range(pairs):
        band = []
        for n in range(subs):
            pieces = [
                back[(h * pairs + q) * tile : (h * pairs + q + 1) * tile, n * width : (n + 1) * width]
                for h in range(2)
            ]
            band.append(jnp.concatenate(pieces, axis=1))
        for n in range(subs):
            if shares > 1:
                back_ref[q, n * tile : (n + 1) * tile, :] = band[n]
            elif n < subs // 2:
                row = (q * subs // 2 + n) * tile
                back_ref[row : row + tile, :] = jnp.concatenate([band[n], band[n + subs // 2]], axis=1)

    pieces = []
    for left, right in ((x_parts, p_parts), (split(hidden), g_parts)):
        total = dot3(left, right, ((0,), (0,)))
        pieces.append(total[:width, :width] + total[width:, width:])
        pieces.append(total[:width, width:] - total[width:, :width])
    weights = jnp.concatenate(pieces, axis=1) * scaling
    bias = jnp.sum(grad_pre, axis=0, keepdims=True) * scaling
    if shares == 1:
        start = pairs * subs // 2 * tile
        back_ref[start : start + width, :] = weights
        rest = jnp.concatenate([bias, jnp.zeros_like(bias)], axis=1)
        back_ref[start + width :, :] = jnp.broadcast_to(rest, (back_ref.shape[0] - start - width, 2 * wide))
        return
    share = width // shares
    w_ref[...] = jnp.zeros_like(w_ref)
    for n in range(shares):
        w_ref[n, :share, :] = weights[n * share : (n + 1) * share]
    w_ref[0, share : share + 1, :wide] = bias
    keep_ref[...] = w_ref[member]
    for s in range(1, shares):
        send_refs[s - 1][...] = w_ref[lax.rem(member + s, shares)]


def synth_kernel(inner, start, place_ref, table_ref, *refs):
    backs, sums, (out_ref, wide_ref) = refs[:inner], refs[inner : 2 * inner], refs[2 * inner :]
    member = place_ref[1]
    pairs, modes, lanes = backs[0].shape
    blocks, total_rows, wide = out_ref.shape
    data_rows = pairs * HALF
    share = lanes // 2 // inner
    for q in range(pairs):
        total = None
        for s, back in enumerate(backs):
            source = lax.rem(member - s + inner, inner)
            rows = table_rows(table_ref, start, 2 * blocks * HALF, member * inner + source)
            term = dot3((rows[:, :modes], rows[:, modes : 2 * modes]), split(back[q]))
            total = term if total is None else total + term
        part = blocks * HALF
        columns = jnp.concatenate([total[:part], total[part:]], axis=1)
        wide_ref[:, q * HALF : (q + 1) * HALF, :] = columns.reshape(blocks, HALF, wide)
    weights = sums[0][...]
    for ref in sums[1:]:
        weights = weights + ref[...]
    coded, tail = code_all(wide_ref[...], weights, share)
    tail = tail[: total_rows - data_rows]
    for b in range(blocks):
        out_ref[b] = jnp.concatenate([coded[b], tail], axis=0).astype(jnp.bfloat16)


def code_all(columns, weights, share):
    rows, wide = columns.shape[1:]
    lanes = wide // 2
    weights, level_w = scaled(weights, jnp.max(jnp.abs(weights), axis=0, keepdims=True))
    top = jnp.max(jnp.max(jnp.abs(columns), axis=0), axis=0, keepdims=True)
    columns, level = scaled(columns, top)
    tail = encode(weights).astype(jnp.float32)
    bias = tail[share : share + 1, :lanes]
    spare = (bias, level_w[:, :lanes], level_w[:, lanes:], level[:, :lanes], level[:, lanes:])
    extra = []
    for n in range(rows // HALF):
        row = jnp.zeros((1, lanes), jnp.float32) if n >= len(spare) else spare[n]
        row = jnp.concatenate([jnp.zeros((1, lanes), jnp.float32), row], axis=1)
        place_row = lax.broadcasted_iota(jnp.int32, (HALF, 1), 0)
        extra.append(jnp.where(place_row == SPARE, row, 0.0))
    extra = jnp.concatenate(extra, axis=0)
    return encode(columns).astype(jnp.float32) + extra, tail


def serve_kernel(pairs, place_ref, table_ref, own_ref, other_ref, *refs):
    outs, wide_ref = refs[:-1], refs[-1]
    count = wide_ref.shape[0]
    modes, lanes = table_ref.shape[3] // 4, own_ref.shape[1] // 2
    half = modes // 2
    share = lanes // 2
    table = table_ref[0, 0]
    matrix = (table[:, : 2 * modes], table[:, 2 * modes :])
    for q in range(pairs):
        bands = [ref[q * half : (q + 1) * half, :] for ref in (own_ref, other_ref)]
        bands = [x[:, start : start + lanes] for x in bands for start in (0, lanes)]
        total = dot3(matrix, split(jnp.concatenate(bands, axis=0)))
        part = count * HALF
        columns = jnp.concatenate([total[:part], total[part:]], axis=1)
        wide_ref[:, q * HALF : (q + 1) * HALF, :] = columns.reshape(count, HALF, 2 * lanes)
    coded, tail = code_all(wide_ref[...], own_ref[pairs * half :, :] + other_ref[pairs * half :, :], share)
    tail = tail[:share]
    for n, ref in enumerate(outs):
        parts = [coded[n]] if n < 2 else [coded[2 * n - 2], coded[2 * n - 1]]
        ref[...] = jnp.concatenate([*parts, tail], axis=0).astype(jnp.bfloat16)


def arrived(ref, member, data_rows):
    raw = ref[...].astype(jnp.float32)
    level = spare_rows(raw, 3, 2) * (1.0 / TOP)
    columns = raw[:data_rows]
    start = data_rows
    if raw.shape[0] == 2 * data_rows + raw.shape[1] // 4:
        start = 2 * data_rows
        columns = jnp.where(member == 0, columns, raw[data_rows:start])
    weights, bias = weight_rows(raw, start)
    return decode(columns) * level, weights, bias


def first_kernel(data_rows, place_ref, *refs):
    member = place_ref[1]
    count = len(refs) - 3
    columns_ref, weights_ref, bias_ref = refs[count:]
    for n in range(count):
        columns_ref[n], weights_ref[n], bias_ref[n : n + 1, :] = arrived(refs[n], member, data_rows)


def last_kernel(data_rows, place_ref, columns_ref, weights_ref, bias_ref, cot_ref, *refs):
    place, member = place_ref[0], place_ref[1]
    lates = refs[: len(BASES)]
    out_ref, win_ref, bin_ref, wout_ref, held_ref = refs[len(BASES) :]
    rows, cols, _ = cot_ref.shape
    blocks = win_ref.shape[1]
    width = win_ref.shape[2]
    pairs = rows // 2

    def settle(source, columns, weights, bias):
        held_ref[source] = columns
        for i in range(4):
            target = (win_ref, wout_ref)[i // 2]
            target[i % 2, source] = weights[:, i * width : (i + 1) * width]
        for k in range(2):
            bin_ref[k, pl.ds(source, 1), :] = bias[:, k * width : (k + 1) * width]

    for n, base in enumerate((0, 1) + BASES):
        source = place ^ (base + member) if n >= 2 else place ^ base
        settle(source, columns_ref[n], weights_ref[n], bias_ref[n : n + 1, :])
    for ref, base in zip(lates, BASES):
        settle(place ^ (base + 1 - member), *arrived(ref, member, data_rows))
    for q in range(pairs):
        for h in range(2):
            parts = []
            for half in range(2):
                start = (2 * half + h) * width
                pieces = [
                    held_ref[b, q * HALF : (q + 1) * HALF, :][:, start : start + width] for b in range(blocks)
                ]
                parts.append(jnp.concatenate(pieces, axis=1))
            column = jnp.concatenate(parts, axis=0)[:cols]
            row = 2 * q + h
            out_ref[row] = (cot_ref[row].astype(jnp.float32) + column).astype(jnp.bfloat16)


def spare_rows(raw, first, count):
    lanes = raw.shape[1] // 2
    rows = [raw[n * HALF + SPARE : n * HALF + SPARE + 1, lanes:] for n in range(first, first + count)]
    return jnp.concatenate(rows, axis=1)


def weight_rows(raw, data_rows):
    level = spare_rows(raw, 1, 2) * (1.0 / TOP)
    bias = decode(spare_rows(raw, 0, 1)) * level[:, : raw.shape[1] // 2]
    return decode(raw[data_rows:]) * level, bias


def columns_kernel(place_ref, data_ref, cot_ref, out_ref, held_ref, bias_ref):
    rows, cols, _ = cot_ref.shape
    blocks, total_rows, wide = data_ref.shape
    width = wide // 4
    pairs = rows // 2
    values = []
    for b in range(blocks):
        raw = data_ref[b].astype(jnp.float32)
        values.append(decode(raw[: pairs * HALF]) * (spare_rows(raw, 3, 2) * (1.0 / TOP)))
        held_ref[b], bias_ref[b : b + 1, :] = weight_rows(raw, pairs * HALF)
    for q in range(pairs):
        for h in range(2):
            parts = []
            for half in range(2):
                start = (2 * half + h) * width
                pieces = [v[q * HALF : (q + 1) * HALF, start : start + width] for v in values]
                parts.append(jnp.concatenate(pieces, axis=1))
            column = jnp.concatenate(parts, axis=0)[:cols]
            row = 2 * q + h
            out_ref[row] = (cot_ref[row].astype(jnp.float32) + column).astype(jnp.bfloat16)


def weights_kernel(inner, share, place_ref, held_ref, own_bias_ref, *refs):
    pieces, (win_ref, bin_ref, wout_ref) = refs[: inner - 1], refs[inner - 1 :]
    member = place_ref[1]
    blocks, rows, wide = held_ref.shape
    width = wide // 4
    data_rows = pieces[0].shape[1] - rows
    for b in range(blocks):
        held = [(held_ref[b], own_bias_ref[b : b + 1, :])]
        held += [weight_rows(ref[b].astype(jnp.float32), data_rows) for ref in pieces]
        for n in range(inner):
            part, bias = held[0]
            for s in range(1, inner):
                chosen = lax.rem(member - s + inner, inner) == n
                part = jnp.where(chosen, held[s][0], part)
                bias = jnp.where(chosen, held[s][1], bias)
            for i in range(4):
                target = (win_ref, wout_ref)[i // 2]
                target[i % 2, b, n * share : (n + 1) * share, :] = part[:share, i * width : (i + 1) * width]
            if n == 0:
                for k in range(2):
                    bin_ref[k, b : b + 1, :] = bias[:, k * width : (k + 1) * width]


def body(features, cotangent, weight_in, bias_in, weight_out):
    lon_count, lat_count = lax.axis_size("lon"), lax.axis_size("lat")
    blocks, width = weight_in.shape[1:3]
    rows, cols, _ = features.shape
    inner = lon_count // blocks
    pairs = rows // 2
    wide = 4 * width
    modes = 2 * MODE_DEV * blocks
    size = 2 * rows * lat_count * SUB
    subs = modes // (2 * SUB)
    lon_place = lax.axis_index("lon")
    lat_place = lax.axis_index("lat")
    scalars = jnp.stack([lon_place // inner, lon_place % inner, lat_place]).astype(jnp.int32)
    scaling = (rows * lat_count * modes // 2 * inner) ** -0.5
    paired = inner == 2 and blocks == 2 + 2 * len(BASES)
    tables, starts = all_tables(blocks, inner, cols, rows, lat_count, paired)
    lon_start, lat_start, synth_start, _ = starts
    shares = 1 if paired else inner
    share = width // shares
    data_rows = pairs * HALF
    total_rows = data_rows + -(-share // 8) * 8
    sum_rows = -(-(share + 1) // 8) * 8
    f32, bf16 = jnp.float32, jnp.bfloat16
    shape = jax.ShapeDtypeStruct

    places = [[g * inner + i for g in range(blocks)] for i in range(inner)]

    def exchange(values):
        return lax.all_to_all(
            values, "lon", split_axis=0, concat_axis=0, tiled=True, axis_index_groups=places
        )

    def to_member(values, step):
        turn = [(i, i // inner * inner + (i + step) % inner) for i in range(lon_count)]
        return lax.ppermute(values, "lon", turn)

    def to_place(values, first, second):
        turn = [(i, (i // 2 ^ (second if i % 2 else first)) * 2 + i % 2) for i in range(lon_count)]
        return lax.ppermute(values, "lon", turn)

    def to_lat(values, step):
        return lax.ppermute(values, "lat", [(i, (i + step) % lat_count) for i in range(lat_count)])

    def by_place(table):
        return pl.BlockSpec((1, 1, *table.shape[2:]), lambda i, s: (s[0], s[1], 0, 0))

    def serve(slots):
        return [to_place(x, base, base + 1) for x, base in zip(slots, BASES)]

    spectrum = dict(
        outputs=(shape((pairs * modes + PAD, wide), bf16),),
        scratch=(pltpu.VMEM((pairs, modes, wide), f32),),
    )
    if paired:
        rows_in = pairs * PAD
        packed, side = call(
            functools.partial(own_pack_kernel, width),
            scalars,
            (jnp.stack([features, cotangent]),),
            (shape((blocks, rows_in, wide), bf16), shape((rows_in, wide), bf16)),
            flops=10**8,
        )
        own, *slots = call(
            functools.partial(pair_kernel, width),
            scalars,
            (packed, to_member(features, 1), to_member(cotangent, 1)),
            [shape((2, rows_in, wide), bf16)] * (1 + len(BASES)),
            scratch=(pltpu.VMEM((blocks, rows_in, wide), bf16),),
        )
        side = to_place(side, 1, 1)
        sent = [side, *serve(slots)]
        late = [to_member(x, 1) for x in sent]
        sent, late = [side, late[0], *sent[1:]], late[1:]
        table = paired_table(blocks, cols)
        (coded,) = call(
            paired_lon_kernel, scalars, (table, own, *sent, *late), specs={0: by_place(table)}, **spectrum
        )
    else:
        (packed,) = call(
            functools.partial(pack_kernel, width),
            scalars,
            (features, cotangent),
            (shape((blocks, pairs * PAD, wide), bf16),),
        )
        whole = exchange(packed)
        fields = [whole] + [to_member(whole, s) for s in range(1, inner)]
        (coded,) = call(functools.partial(lon_kernel, inner), scalars, (tables, *fields), **spectrum)
    others = [to_lat(coded, s) for s in range(1, lat_count)]
    block_spec = pl.BlockSpec((2, 1, width, width), lambda i, s: (0, s[0], 0, 0))
    part, forms, bias = call(
        functools.partial(ready_kernel, pairs, lat_start),
        scalars,
        (tables, coded, weight_in, bias_in, weight_out),
        (
            shape((size, 2 * subs * width), f32),
            shape((4, 2 * width, 2 * width), bf16),
            shape((8, 2 * width), f32),
        ),
        specs={2: block_spec, 4: block_spec},
        flops=6 * size * size // lat_count * 2 * subs * width,
    )
    if paired:
        outs = [shape((pairs * modes // 2 + sum_rows, wide), f32)]
    else:
        outs = [shape((pairs, modes, 2 * width), f32), *[shape((sum_rows, wide), f32)] * shares]
    back, *rest = call(
        functools.partial(mlp_kernel, lat_count, inner, shares, pairs, lat_start, scaling),
        scalars,
        (tables, *others, part, forms, bias),
        outs,
        scratch=() if paired else (pltpu.VMEM((shares, sum_rows, wide), f32),),
    )
    backs = [back] + [to_member(back, s) for s in range(1, inner)]
    if paired:
        table = served_table(blocks, cols)
        count = table.shape[2] // PAD
        outs = [share + data_rows] * 2 + [share + 2 * data_rows] * len(BASES)
        own, side, *slots = call(
            functools.partial(serve_kernel, pairs),
            scalars,
            (table, *backs),
            [shape((n, wide), bf16) for n in outs],
            specs={0: by_place(table)},
            scratch=(pltpu.VMEM((count, data_rows, wide), f32),),
        )
        sent = serve(slots)
        side, sent[0] = lax.optimization_barrier((to_place(side, 1, 1), sent[0]))
        firsts, late = [own, side, *sent], [to_member(x, 1) for x in sent]
        held = call(
            functools.partial(first_kernel, data_rows),
            scalars,
            firsts,
            (
                shape((len(firsts), data_rows, wide), f32),
                shape((len(firsts), share, wide), f32),
                shape((len(firsts), 2 * width), f32),
            ),
        )
        return call(
            functools.partial(last_kernel, data_rows),
            scalars,
            (*held, cotangent, *late),
            [shape(x.shape, x.dtype) for x in (features, weight_in, bias_in, weight_out)],
            scratch=(pltpu.VMEM((blocks, data_rows, wide), f32),),
        )
    keep, *send = rest
    sums = [keep] + [to_member(send[s - 1], s) for s in range(1, inner)]
    (payload,) = call(
        functools.partial(synth_kernel, inner, synth_start),
        scalars,
        (tables, *backs, *sums),
        (shape((blocks, total_rows, wide), bf16),),
        scratch=(pltpu.VMEM((blocks, pairs * HALF, wide), f32),),
    )
    returned = exchange(payload)
    gathered = [to_member(returned, s) for s in range(1, inner)]
    weight_part = total_rows - pairs * HALF
    grad_features, held, held_bias = call(
        columns_kernel,
        scalars,
        (returned, cotangent),
        (
            shape(features.shape, bf16),
            shape((blocks, weight_part, wide), f32),
            shape((blocks, 2 * width), f32),
        ),
    )
    grad_w_in, grad_b_in, grad_w_out = call(
        functools.partial(weights_kernel, inner, share),
        scalars,
        (held, held_bias, *gathered),
        (shape(weight_in.shape, f32), shape(bias_in.shape, f32), shape(weight_out.shape, f32)),
    )
    return grad_features, grad_w_in, grad_b_in, grad_w_out


def solution(mesh):
    placed = (P("lat", "lon", None), P("lat", "lon", None), P(), P(), P())
    return jax.shard_map(
        body,
        mesh=mesh,
        in_specs=placed,
        out_specs=(P("lat", "lon", None), P(), P(), P()),
        check_vma=False,
    )
```

```python
import functools
import math

import jax
import jax.numpy as jnp
import ml_dtypes
import numpy as np
from jax import lax
from jax.experimental import pallas as pl
from jax.experimental.pallas import tpu as pltpu
from jax.sharding import PartitionSpec as P

MODE_DEV = 4
PAD = 16
HALF = PAD // 2
BASES = (6, 2, 4)
SUB = 4
SPARE = 6
POWER = 13.0
TOP = 2.0**9
VMEM = 40 * 2**20

root_half = math.sqrt(0.5)
density_norm = 1.0 / math.sqrt(2.0 * math.pi)


def halves(table):
    table = table.astype(np.float32)
    high = table.astype(ml_dtypes.bfloat16)
    low = (table - high.astype(np.float32)).astype(ml_dtypes.bfloat16)
    return high, low


def lon_table(columns, mode_count):
    product = np.arange(columns)[:, None] * np.arange(mode_count)[None, :] % columns
    angle = product * (2.0 * math.pi / columns)
    stacked = np.stack([np.cos(angle), -np.sin(angle)], axis=2) * columns**-0.5
    return stacked.reshape(columns, 2 * mode_count)


def lon_tables(blocks, inner, cols):
    modes = MODE_DEV * blocks
    table = lon_table(blocks * inner * cols, modes * inner)
    table = table.reshape(blocks, inner, cols, inner, 2 * modes)
    table = np.pad(table, ((0, 0), (0, 0), (0, PAD - cols), (0, 0), (0, 0)))
    forward = table.transpose(3, 1, 4, 0, 2).reshape(inner, inner, 2 * modes, blocks * PAD)
    split = table.reshape(blocks, inner, 2, HALF, inner, 2 * modes)
    synth = split.transpose(1, 4, 2, 0, 3, 5).reshape(inner, inner, 2 * blocks * HALF, 2 * modes)
    forward, synth = np.concatenate(halves(forward), axis=2), np.concatenate(halves(synth), axis=3)
    return forward.reshape(-1, blocks * PAD), synth.reshape(-1, 4 * modes)


def served(member):
    return [(0, member), (1, member)] + [(base + member, m) for base in BASES for m in range(2)]


def served_table(blocks, cols):
    modes = 2 * MODE_DEV * blocks
    table = lon_table(blocks * 2 * cols, modes).reshape(blocks, 2, cols, 2, modes)
    table = np.pad(table, ((0, 0), (0, 0), (0, PAD - cols), (0, 0), (0, 0)))
    whole = []
    for place in range(blocks):
        for member in range(2):
            rows = np.stack([table[place ^ k, m] for k, m in served(member)])
            rows = np.stack([rows[:, :, member], rows[:, :, 1 - member]], axis=2)
            rows = rows.reshape(len(rows), 2, HALF, 2 * modes).transpose(1, 0, 2, 3)
            whole.append(np.concatenate(halves(rows.reshape(-1, 2 * modes)), axis=1))
    return np.stack(whole).reshape(blocks, 2, *whole[0].shape)


def paired_table(blocks, cols):
    modes = 2 * MODE_DEV * blocks
    table = lon_table(blocks * 2 * cols, modes).reshape(blocks, 2, cols, 2, modes)
    table = np.pad(table, ((0, 0), (0, 0), (0, PAD - cols), (0, 0), (0, 0)))
    whole = []
    for place in range(blocks):
        for member in range(2):
            sources = [(0, 0), (0, 1), (1, member), (1, 1 - member)]
            sources += [(base + m, n) for m in (member, 1 - member) for base in BASES for n in range(2)]
            rows = np.stack([table[place ^ k, n, :, member] for k, n in sources])
            rows = rows.transpose(2, 0, 1).reshape(modes, -1)
            whole.append(np.concatenate(halves(rows)))
    return np.stack(whole).reshape(blocks, 2, *whole[0].shape)


def lat_table(rows, lat_count, group):
    total = rows * lat_count
    product = np.arange(total)[:, None] * np.arange(total)[None, :] % total
    angle = product * (2.0 * math.pi / total)
    c, s = np.cos(angle), np.sin(angle)
    basis = np.stack([np.stack([c, s], -1), np.stack([-s, c], -1)], axis=0) * total**-0.5
    basis = basis.reshape(2, total, lat_count, rows // 2, 2, 2).transpose(0, 1, 2, 4, 3, 5)
    size = 2 * total * group
    return np.einsum("akxhqb,mn->akmxhqnb", basis, np.eye(group)).reshape(size, size)


def all_tables(blocks, inner, cols, rows, lat_count, paired):
    table = lat_table(rows, lat_count, SUB)
    size = table.shape[0]
    lat = np.concatenate(halves(table.reshape(size, lat_count, -1).transpose(1, 0, 2)), axis=1)
    lat = lat.reshape(2 * lat_count * size, -1)
    if paired:
        return lat, [0] * 4
    forward, synth = lon_tables(blocks, inner, cols)
    parts = [forward, lat, synth]
    lanes = max(p.shape[1] for p in parts)
    parts = [np.pad(p, ((0, 0), (0, lanes - p.shape[1]))) for p in parts]
    starts = np.cumsum([0] + [len(p) for p in parts])
    return np.concatenate(parts), [int(n) for n in starts]


def split(values):
    high = values.astype(jnp.bfloat16)
    return high, (values - high.astype(jnp.float32)).astype(jnp.bfloat16)


def dot(left, right, dims=((1,), (0,))):
    return lax.dot_general(left, right, (dims, ((), ())), preferred_element_type=jnp.float32)


def dot3(left, right, dims=((1,), (0,))):
    return dot(left[0], right[0], dims) + (dot(left[0], right[1], dims) + dot(left[1], right[0], dims))


def scaled(values, top):
    level = jnp.maximum(top, 1e-30).astype(jnp.bfloat16).astype(jnp.float32)
    return values * (TOP / level), level


def table_rows(ref, start, count, place):
    return ref[pl.ds(pl.multiple_of(start + place * count, PAD), count), :]


def lat_part(ref, start, size, part, x):
    rows = table_rows(ref, start, 2 * size, x)[:, :part]
    return rows[:size], rows[size:]


def encode(values):
    square = values * values
    fourth = square * square
    return (values * fourth * (fourth * fourth)).astype(jnp.bfloat16)


def decode(coded):
    coded = coded.astype(jnp.float32)
    size = jnp.abs(coded)
    root = jnp.exp(jnp.log(jnp.maximum(size, 1e-37)) * (1.0 / POWER))
    root = jnp.where(size > 0.0, root, 0.0)
    return jnp.where(coded < 0.0, -root, root)


def call(kernel, scalars, inputs, outputs, specs=None, scratch=(), flops=0):
    whole = pl.BlockSpec(memory_space=pltpu.VMEM)
    specs = specs or {}
    in_specs = [specs.get(n, whole) for n in range(len(inputs))]
    out_specs = [whole] * len(outputs)
    moved = sum(math.prod(x.shape) * x.dtype.itemsize for x in (*inputs, *outputs))
    return pl.pallas_call(
        kernel,
        grid_spec=pltpu.PrefetchScalarGridSpec(
            num_scalar_prefetch=1,
            grid=(1,),
            in_specs=in_specs,
            out_specs=out_specs,
            scratch_shapes=list(scratch),
        ),
        out_shape=list(outputs),
        compiler_params=pltpu.CompilerParams(vmem_limit_bytes=VMEM),
        cost_estimate=pl.CostEstimate(flops=flops, bytes_accessed=moved, transcendentals=0),
    )(scalars, *inputs)


def pack_kernel(width, place_ref, x_ref, g_ref, out_ref):
    pack_all(width, x_ref, g_ref, out_ref)


def pack_all(width, x_ref, g_ref, out_ref):
    rows, cols, channels = x_ref.shape
    for q in range(rows // 2):
        lanes = [ref[2 * q + h].astype(jnp.float32) for h in range(2) for ref in (x_ref, g_ref)]
        lanes = [jnp.pad(x, ((0, PAD - cols), (0, 0))) for x in lanes]
        for b in range(channels // width):
            pieces = [x[:, b * width : (b + 1) * width] for x in lanes]
            out_ref[b, q * PAD : (q + 1) * PAD, :] = jnp.concatenate(pieces, axis=1).astype(jnp.bfloat16)


def own_pack_kernel(width, place_ref, fields_ref, pack_ref, side_ref):
    pack_all(width, fields_ref.at[0], fields_ref.at[1], pack_ref)
    side_ref[...] = pack_ref[place_ref[0] ^ 1]


def pair_kernel(width, place_ref, own_ref, x_ref, g_ref, *refs):
    outs, pack_ref = refs[:-1], refs[-1]
    place, member = place_ref[0], place_ref[1]
    pack_all(width, x_ref, g_ref, pack_ref)
    for n, ref in enumerate(outs):
        target = place if n == 0 else place ^ (BASES[n - 1] + member)
        ref[member] = own_ref[target]
        ref[1 - member] = pack_ref[target]


def paired_lon_kernel(place_ref, table_ref, own_ref, side_ref, other_side_ref, *refs):
    pieces = [own_ref.at[0], own_ref.at[1], side_ref, other_side_ref]
    pieces += [ref.at[n] for ref in refs[:-2] for n in range(2)]
    coded_ref, spec_ref = refs[-2:]
    pairs, modes, lanes = spec_ref.shape
    table = table_ref[0, 0]
    tops = []
    for q in range(pairs):
        data = [piece[q * PAD : (q + 1) * PAD, :] for piece in pieces]
        total = dot(table, jnp.concatenate(data, axis=0))
        spec = total[:modes] + total[modes:]
        spec_ref[q] = spec
        tops.append(jnp.max(jnp.abs(spec), axis=0, keepdims=True))
    code_spectrum(coded_ref, spec_ref, tops)


def code_spectrum(coded_ref, spec_ref, tops):
    pairs, modes, lanes = spec_ref.shape
    values, level = scaled(spec_ref[...], functools.reduce(jnp.maximum, tops))
    coded_ref[: pairs * modes, :] = encode(values).reshape(pairs * modes, lanes)
    coded_ref[pairs * modes :, :] = jnp.broadcast_to(level, (PAD, lanes)).astype(jnp.bfloat16)


def lon_kernel(inner, place_ref, table_ref, *refs):
    fields, (coded_ref, spec_ref) = refs[:inner], refs[inner:]
    member = place_ref[1]
    pairs, modes, lanes = spec_ref.shape
    blocks = fields[0].shape[0]
    tops = []
    for q in range(pairs):
        total = None
        for s, field in enumerate(fields):
            source = lax.rem(member - s + inner, inner)
            data = field[:, q * PAD : (q + 1) * PAD, :].reshape(blocks * PAD, lanes)
            term = dot(table_rows(table_ref, 0, 2 * modes, member * inner + source), data)
            total = term if total is None else total + term
        spec = total[:modes] + total[modes:]
        spec_ref[q] = spec
        tops.append(jnp.max(jnp.abs(spec), axis=0, keepdims=True))
    code_spectrum(coded_ref, spec_ref, tops)


def lat_rows(ref, pairs):
    modes = (ref.shape[0] - PAD) // pairs
    wide = ref.shape[1] // 2
    tile = 2 * SUB
    level = ref[pairs * modes :, :].astype(jnp.float32)[:1] * (1.0 / TOP)
    values = [decode(ref[q * modes : (q + 1) * modes, :]) * level for q in range(pairs)]
    rows = []
    for h in range(2):
        for q in range(pairs):
            parts = [
                values[q][n * tile : (n + 1) * tile, h * wide : (h + 1) * wide] for n in range(modes // tile)
            ]
            rows.append(jnp.concatenate(parts, axis=1))
    return jnp.concatenate(rows, axis=0)


def ready_kernel(pairs, start, place_ref, table_ref, spec_ref, win_ref, bin_ref, wout_ref, *outs):
    part_ref, form_ref, bias_ref = outs
    place, x = place_ref[0], place_ref[2]
    for n, ref in enumerate((win_ref, wout_ref)):
        re, im = ref[0, 0], ref[1, 0]
        form = jnp.concatenate([jnp.concatenate([re, im], axis=1), jnp.concatenate([-im, re], axis=1)], axis=0)
        form_ref[2 * n], form_ref[2 * n + 1] = split(form)
    bias = jnp.concatenate([bin_ref[0, pl.ds(place, 1), :], bin_ref[1, pl.ds(place, 1), :]], axis=1)
    bias_ref[...] = jnp.broadcast_to(bias, bias_ref.shape)
    rows = split(lat_rows(spec_ref, pairs))
    part_ref[...] = dot3(lat_part(table_ref, start, part_ref.shape[0], rows[0].shape[0], x), rows)


def mlp_kernel(lat, inner, shares, pairs, start, scaling, place_ref, table_ref, *refs):
    others = refs[: lat - 1]
    part_ref, form_ref, bias_ref = refs[lat - 1 : lat + 2]
    back_ref, *rest = refs[lat + 2 :]
    if shares > 1:
        keep_ref, *send_refs, w_ref = rest
    member, x = place_ref[1], place_ref[2]
    wide = form_ref.shape[1]
    width = wide // 2
    tile = 2 * SUB
    size = part_ref.shape[0]
    points = size // 2
    part = size // lat
    subs = part_ref.shape[1] // wide

    spectra = part_ref[...]
    for s, ref in enumerate(others):
        source = lax.rem(x - s - 1 + lat, lat)
        matrix = lat_part(table_ref, start, size, part, source)
        spectra = spectra + dot3(matrix, split(lat_rows(ref, pairs)))

    def of_points(start):
        rows = []
        for n in range(subs):
            lanes = slice(n * wide + start, n * wide + start + width)
            rows.append(jnp.concatenate([spectra[:points, lanes], spectra[points:, lanes]], axis=1))
        return jnp.concatenate(rows, axis=0)

    spec_x, spec_g = of_points(0), of_points(width)
    m_in, m_out = (form_ref[0], form_ref[1]), (form_ref[2], form_ref[3])
    point = lax.broadcasted_iota(jnp.int32, (subs * points, 1), 0)
    first = ((point & (SUB - 1)) + jnp.where(point < points, 0, SUB) + member * SUB) == 0
    grad_out = spec_g * jnp.where(first, 1.0, 2.0)
    x_parts, g_parts = split(spec_x), split(grad_out)
    pre = dot3(x_parts, m_in) + bias_ref[:1]
    cdf = 0.5 * (1.0 + lax.erf(pre * root_half))
    hidden = pre * cdf
    slopes = cdf + pre * jnp.exp(-0.5 * pre * pre) * density_norm
    grad_pre = dot3(g_parts, m_out, ((1,), (1,))) * slopes
    p_parts = split(grad_pre)
    grad_spec = dot3(p_parts, m_in, ((1,), (1,)))
    lanes = []
    for n in range(subs):
        piece = grad_spec[n * points : (n + 1) * points]
        lanes.append(jnp.concatenate([piece[:, :width], piece[:, width:]], axis=0))
    matrix = lat_part(table_ref, start, size, part, x)
    back = dot3(matrix, split(jnp.concatenate(lanes, axis=1)), ((0,), (0,)))
    for q in range(pairs):
        band = []
        for n in range(subs):
            pieces = [
                back[(h * pairs + q) * tile : (h * pairs + q + 1) * tile, n * width : (n + 1) * width]
                for h in range(2)
            ]
            band.append(jnp.concatenate(pieces, axis=1))
        for n in range(subs):
            if shares > 1:
                back_ref[q, n * tile : (n + 1) * tile, :] = band[n]
            elif n < subs // 2:
                row = (q * subs // 2 + n) * tile
                back_ref[row : row + tile, :] = jnp.concatenate([band[n], band[n + subs // 2]], axis=1)

    pieces = []
    for left, right in ((x_parts, p_parts), (split(hidden), g_parts)):
        total = dot3(left, right, ((0,), (0,)))
        pieces.append(total[:width, :width] + total[width:, width:])
        pieces.append(total[:width, width:] - total[width:, :width])
    weights = jnp.concatenate(pieces, axis=1) * scaling
    bias = jnp.sum(grad_pre, axis=0, keepdims=True) * scaling
    if shares == 1:
        start = pairs * subs // 2 * tile
        back_ref[start : start + width, :] = weights
        rest = jnp.concatenate([bias, jnp.zeros_like(bias)], axis=1)
        back_ref[start + width :, :] = jnp.broadcast_to(rest, (back_ref.shape[0] - start - width, 2 * wide))
        return
    share = width // shares
    w_ref[...] = jnp.zeros_like(w_ref)
    for n in range(shares):
        w_ref[n, :share, :] = weights[n * share : (n + 1) * share]
    w_ref[0, share : share + 1, :wide] = bias
    keep_ref[...] = w_ref[member]
    for s in range(1, shares):
        send_refs[s - 1][...] = w_ref[lax.rem(member + s, shares)]


def synth_kernel(inner, start, place_ref, table_ref, *refs):
    backs, sums, (out_ref, wide_ref) = refs[:inner], refs[inner : 2 * inner], refs[2 * inner :]
    member = place_ref[1]
    pairs, modes, lanes = backs[0].shape
    blocks, total_rows, wide = out_ref.shape
    data_rows = pairs * HALF
    share = lanes // 2 // inner
    for q in range(pairs):
        total = None
        for s, back in enumerate(backs):
            source = lax.rem(member - s + inner, inner)
            rows = table_rows(table_ref, start, 2 * blocks * HALF, member * inner + source)
            term = dot3((rows[:, :modes], rows[:, modes : 2 * modes]), split(back[q]))
            total = term if total is None else total + term
        part = blocks * HALF
        columns = jnp.concatenate([total[:part], total[part:]], axis=1)
        wide_ref[:, q * HALF : (q + 1) * HALF, :] = columns.reshape(blocks, HALF, wide)
    weights = sums[0][...]
    for ref in sums[1:]:
        weights = weights + ref[...]
    coded, tail = code_all(wide_ref[...], weights, share)
    tail = tail[: total_rows - data_rows]
    for b in range(blocks):
        out_ref[b] = jnp.concatenate([coded[b], tail], axis=0).astype(jnp.bfloat16)


def code_all(columns, weights, share):
    rows, wide = columns.shape[1:]
    lanes = wide // 2
    weights, level_w = scaled(weights, jnp.max(jnp.abs(weights), axis=0, keepdims=True))
    top = jnp.max(jnp.max(jnp.abs(columns), axis=0), axis=0, keepdims=True)
    columns, level = scaled(columns, top)
    tail = encode(weights).astype(jnp.float32)
    bias = tail[share : share + 1, :lanes]
    spare = (bias, level_w[:, :lanes], level_w[:, lanes:], level[:, :lanes], level[:, lanes:])
    extra = []
    for n in range(rows // HALF):
        row = jnp.zeros((1, lanes), jnp.float32) if n >= len(spare) else spare[n]
        row = jnp.concatenate([jnp.zeros((1, lanes), jnp.float32), row], axis=1)
        place_row = lax.broadcasted_iota(jnp.int32, (HALF, 1), 0)
        extra.append(jnp.where(place_row == SPARE, row, 0.0))
    extra = jnp.concatenate(extra, axis=0)
    return encode(columns).astype(jnp.float32) + extra, tail


def serve_kernel(pairs, place_ref, table_ref, own_ref, other_ref, *refs):
    outs, wide_ref = refs[:-1], refs[-1]
    count = wide_ref.shape[0]
    modes, lanes = table_ref.shape[3] // 4, own_ref.shape[1] // 2
    half = modes // 2
    share = lanes // 2
    table = table_ref[0, 0]
    matrix = (table[:, : 2 * modes], table[:, 2 * modes :])
    for q in range(pairs):
        bands = [ref[q * half : (q + 1) * half, :] for ref in (own_ref, other_ref)]
        bands = [x[:, start : start + lanes] for x in bands for start in (0, lanes)]
        total = dot3(matrix, split(jnp.concatenate(bands, axis=0)))
        part = count * HALF
        columns = jnp.concatenate([total[:part], total[part:]], axis=1)
        wide_ref[:, q * HALF : (q + 1) * HALF, :] = columns.reshape(count, HALF, 2 * lanes)
    coded, tail = code_all(wide_ref[...], own_ref[pairs * half :, :] + other_ref[pairs * half :, :], share)
    tail = tail[:share]
    for n, ref in enumerate(outs):
        parts = [coded[n]] if n < 2 else [coded[2 * n - 2], coded[2 * n - 1]]
        ref[...] = jnp.concatenate([*parts, tail], axis=0).astype(jnp.bfloat16)


def arrived(ref, member, data_rows):
    raw = ref[...].astype(jnp.float32)
    level = spare_rows(raw, 3, 2) * (1.0 / TOP)
    columns = raw[:data_rows]
    start = data_rows
    if raw.shape[0] == 2 * data_rows + raw.shape[1] // 4:
        start = 2 * data_rows
        columns = jnp.where(member == 0, columns, raw[data_rows:start])
    weights, bias = weight_rows(raw, start)
    return decode(columns) * level, weights, bias


def first_kernel(data_rows, place_ref, *refs):
    member = place_ref[1]
    count = len(refs) - 3
    columns_ref, weights_ref, bias_ref = refs[count:]
    for n in range(count):
        columns_ref[n], weights_ref[n], bias_ref[n : n + 1, :] = arrived(refs[n], member, data_rows)


def last_kernel(data_rows, place_ref, columns_ref, weights_ref, bias_ref, cot_ref, *refs):
    place, member = place_ref[0], place_ref[1]
    lates = refs[: len(BASES)]
    out_ref, win_ref, bin_ref, wout_ref, held_ref = refs[len(BASES) :]
    rows, cols, _ = cot_ref.shape
    blocks = win_ref.shape[1]
    width = win_ref.shape[2]
    pairs = rows // 2

    def settle(source, columns, weights, bias):
        held_ref[source] = columns
        for i in range(4):
            target = (win_ref, wout_ref)[i // 2]
            target[i % 2, source] = weights[:, i * width : (i + 1) * width]
        for k in range(2):
            bin_ref[k, pl.ds(source, 1), :] = bias[:, k * width : (k + 1) * width]

    for n, base in enumerate((0, 1) + BASES):
        source = place ^ (base + member) if n >= 2 else place ^ base
        settle(source, columns_ref[n], weights_ref[n], bias_ref[n : n + 1, :])
    for ref, base in zip(lates, BASES):
        settle(place ^ (base + 1 - member), *arrived(ref, member, data_rows))
    for q in range(pairs):
        for h in range(2):
            parts = []
            for half in range(2):
                start = (2 * half + h) * width
                pieces = [
                    held_ref[b, q * HALF : (q + 1) * HALF, :][:, start : start + width] for b in range(blocks)
                ]
                parts.append(jnp.concatenate(pieces, axis=1))
            column = jnp.concatenate(parts, axis=0)[:cols]
            row = 2 * q + h
            out_ref[row] = (cot_ref[row].astype(jnp.float32) + column).astype(jnp.bfloat16)


def spare_rows(raw, first, count):
    lanes = raw.shape[1] // 2
    rows = [raw[n * HALF + SPARE : n * HALF + SPARE + 1, lanes:] for n in range(first, first + count)]
    return jnp.concatenate(rows, axis=1)


def weight_rows(raw, data_rows):
    level = spare_rows(raw, 1, 2) * (1.0 / TOP)
    bias = decode(spare_rows(raw, 0, 1)) * level[:, : raw.shape[1] // 2]
    return decode(raw[data_rows:]) * level, bias


def columns_kernel(place_ref, data_ref, cot_ref, out_ref, held_ref, bias_ref):
    rows, cols, _ = cot_ref.shape
    blocks, total_rows, wide = data_ref.shape
    width = wide // 4
    pairs = rows // 2
    values = []
    for b in range(blocks):
        raw = data_ref[b].astype(jnp.float32)
        values.append(decode(raw[: pairs * HALF]) * (spare_rows(raw, 3, 2) * (1.0 / TOP)))
        held_ref[b], bias_ref[b : b + 1, :] = weight_rows(raw, pairs * HALF)
    for q in range(pairs):
        for h in range(2):
            parts = []
            for half in range(2):
                start = (2 * half + h) * width
                pieces = [v[q * HALF : (q + 1) * HALF, start : start + width] for v in values]
                parts.append(jnp.concatenate(pieces, axis=1))
            column = jnp.concatenate(parts, axis=0)[:cols]
            row = 2 * q + h
            out_ref[row] = (cot_ref[row].astype(jnp.float32) + column).astype(jnp.bfloat16)


def weights_kernel(inner, share, place_ref, held_ref, own_bias_ref, *refs):
    pieces, (win_ref, bin_ref, wout_ref) = refs[: inner - 1], refs[inner - 1 :]
    member = place_ref[1]
    blocks, rows, wide = held_ref.shape
    width = wide // 4
    data_rows = pieces[0].shape[1] - rows
    for b in range(blocks):
        held = [(held_ref[b], own_bias_ref[b : b + 1, :])]
        held += [weight_rows(ref[b].astype(jnp.float32), data_rows) for ref in pieces]
        for n in range(inner):
            part, bias = held[0]
            for s in range(1, inner):
                chosen = lax.rem(member - s + inner, inner) == n
                part = jnp.where(chosen, held[s][0], part)
                bias = jnp.where(chosen, held[s][1], bias)
            for i in range(4):
                target = (win_ref, wout_ref)[i // 2]
                target[i % 2, b, n * share : (n + 1) * share, :] = part[:share, i * width : (i + 1) * width]
            if n == 0:
                for k in range(2):
                    bin_ref[k, b : b + 1, :] = bias[:, k * width : (k + 1) * width]


def body(features, cotangent, weight_in, bias_in, weight_out):
    lon_count, lat_count = lax.axis_size("lon"), lax.axis_size("lat")
    blocks, width = weight_in.shape[1:3]
    rows, cols, _ = features.shape
    inner = lon_count // blocks
    pairs = rows // 2
    wide = 4 * width
    modes = 2 * MODE_DEV * blocks
    size = 2 * rows * lat_count * SUB
    subs = modes // (2 * SUB)
    lon_place = lax.axis_index("lon")
    lat_place = lax.axis_index("lat")
    scalars = jnp.stack([lon_place // inner, lon_place % inner, lat_place]).astype(jnp.int32)
    scaling = (rows * lat_count * modes // 2 * inner) ** -0.5
    paired = inner == 2 and blocks == 2 + 2 * len(BASES)
    tables, starts = all_tables(blocks, inner, cols, rows, lat_count, paired)
    lon_start, lat_start, synth_start, _ = starts
    shares = 1 if paired else inner
    share = width // shares
    data_rows = pairs * HALF
    total_rows = data_rows + -(-share // 8) * 8
    sum_rows = -(-(share + 1) // 8) * 8
    f32, bf16 = jnp.float32, jnp.bfloat16
    shape = jax.ShapeDtypeStruct

    places = [[g * inner + i for g in range(blocks)] for i in range(inner)]

    def exchange(values):
        return lax.all_to_all(
            values, "lon", split_axis=0, concat_axis=0, tiled=True, axis_index_groups=places
        )

    def to_member(values, step):
        turn = [(i, i // inner * inner + (i + step) % inner) for i in range(lon_count)]
        return lax.ppermute(values, "lon", turn)

    def to_place(values, first, second):
        turn = [(i, (i // 2 ^ (second if i % 2 else first)) * 2 + i % 2) for i in range(lon_count)]
        return lax.ppermute(values, "lon", turn)

    def to_lat(values, step):
        return lax.ppermute(values, "lat", [(i, (i + step) % lat_count) for i in range(lat_count)])

    def by_place(table):
        return pl.BlockSpec((1, 1, *table.shape[2:]), lambda i, s: (s[0], s[1], 0, 0))

    def serve(slots):
        return [to_place(x, base, base + 1) for x, base in zip(slots, BASES)]

    spectrum = dict(
        outputs=(shape((pairs * modes + PAD, wide), bf16),),
        scratch=(pltpu.VMEM((pairs, modes, wide), f32),),
    )
    if paired:
        rows_in = pairs * PAD
        packed, side = call(
            functools.partial(own_pack_kernel, width),
            scalars,
            (jnp.stack([features, cotangent]),),
            (shape((blocks, rows_in, wide), bf16), shape((rows_in, wide), bf16)),
            flops=10**8,
        )
        own, *slots = call(
            functools.partial(pair_kernel, width),
            scalars,
            (packed, to_member(features, 1), to_member(cotangent, 1)),
            [shape((2, rows_in, wide), bf16)] * (1 + len(BASES)),
            scratch=(pltpu.VMEM((blocks, rows_in, wide), bf16),),
        )
        side = to_place(side, 1, 1)
        sent = [side, *serve(slots)]
        late = [to_member(x, 1) for x in sent]
        sent, late = [side, late[0], *sent[1:]], late[1:]
        table = paired_table(blocks, cols)
        (coded,) = call(
            paired_lon_kernel, scalars, (table, own, *sent, *late), specs={0: by_place(table)}, **spectrum
        )
    else:
        (packed,) = call(
            functools.partial(pack_kernel, width),
            scalars,
            (features, cotangent),
            (shape((blocks, pairs * PAD, wide), bf16),),
        )
        whole = exchange(packed)
        fields = [whole] + [to_member(whole, s) for s in range(1, inner)]
        (coded,) = call(functools.partial(lon_kernel, inner), scalars, (tables, *fields), **spectrum)
    others = [to_lat(coded, s) for s in range(1, lat_count)]
    block_spec = pl.BlockSpec((2, 1, width, width), lambda i, s: (0, s[0], 0, 0))
    part, forms, bias = call(
        functools.partial(ready_kernel, pairs, lat_start),
        scalars,
        (tables, coded, weight_in, bias_in, weight_out),
        (
            shape((size, 2 * subs * width), f32),
            shape((4, 2 * width, 2 * width), bf16),
            shape((8, 2 * width), f32),
        ),
        specs={2: block_spec, 4: block_spec},
        flops=6 * size * size // lat_count * 2 * subs * width,
    )
    if paired:
        outs = [shape((pairs * modes // 2 + sum_rows, wide), f32)]
    else:
        outs = [shape((pairs, modes, 2 * width), f32), *[shape((sum_rows, wide), f32)] * shares]
    back, *rest = call(
        functools.partial(mlp_kernel, lat_count, inner, shares, pairs, lat_start, scaling),
        scalars,
        (tables, *others, part, forms, bias),
        outs,
        scratch=() if paired else (pltpu.VMEM((shares, sum_rows, wide), f32),),
    )
    backs = [back] + [to_member(back, s) for s in range(1, inner)]
    if paired:
        table = served_table(blocks, cols)
        count = table.shape[2] // PAD
        outs = [share + data_rows] * 2 + [share + 2 * data_rows] * len(BASES)
        own, side, *slots = call(
            functools.partial(serve_kernel, pairs),
            scalars,
            (table, *backs),
            [shape((n, wide), bf16) for n in outs],
            specs={0: by_place(table)},
            scratch=(pltpu.VMEM((count, data_rows, wide), f32),),
        )
        sent = serve(slots)
        side, sent[0] = lax.optimization_barrier((to_place(side, 1, 1), sent[0]))
        firsts, late = [own, side, *sent], [to_member(x, 1) for x in sent]
        held = call(
            functools.partial(first_kernel, data_rows),
            scalars,
            firsts,
            (
                shape((len(firsts), data_rows, wide), f32),
                shape((len(firsts), share, wide), f32),
                shape((len(firsts), 2 * width), f32),
            ),
        )
        return call(
            functools.partial(last_kernel, data_rows),
            scalars,
            (*held, cotangent, *late),
            [shape(x.shape, x.dtype) for x in (features, weight_in, bias_in, weight_out)],
            scratch=(pltpu.VMEM((blocks, data_rows, wide), f32),),
        )
    keep, *send = rest
    sums = [keep] + [to_member(send[s - 1], s) for s in range(1, inner)]
    (payload,) = call(
        functools.partial(synth_kernel, inner, synth_start),
        scalars,
        (tables, *backs, *sums),
        (shape((blocks, total_rows, wide), bf16),),
        scratch=(pltpu.VMEM((blocks, pairs * HALF, wide), f32),),
    )
    returned = exchange(payload)
    gathered = [to_member(returned, s) for s in range(1, inner)]
    weight_part = total_rows - pairs * HALF
    grad_features, held, held_bias = call(
        columns_kernel,
        scalars,
        (returned, cotangent),
        (
            shape(features.shape, bf16),
            shape((blocks, weight_part, wide), f32),
            shape((blocks, 2 * width), f32),
        ),
    )
    grad_w_in, grad_b_in, grad_w_out = call(
        functools.partial(weights_kernel, inner, share),
        scalars,
        (held, held_bias, *gathered),
        (shape(weight_in.shape, f32), shape(bias_in.shape, f32), shape(weight_out.shape, f32)),
    )
    return grad_features, grad_w_in, grad_b_in, grad_w_out


def solution(mesh):
    placed = (P("lat", "lon", None), P("lat", "lon", None), P(), P(), P())
    return jax.shard_map(
        body,
        mesh=mesh,
        in_specs=placed,
        out_specs=(P("lat", "lon", None), P(), P(), P()),
        check_vma=False,
    )
```

```python
import functools
import math

import jax
import jax.numpy as jnp
import ml_dtypes
import numpy as np
from jax import lax
from jax.experimental import pallas as pl
from jax.experimental.pallas import tpu as pltpu
from jax.sharding import PartitionSpec as P

MODE_DEV = 4
PAD = 16
HALF = PAD // 2
BASES = (6, 2, 4)
SUB = 4
SPARE = 6
POWER = 13.0
TOP = 2.0**9
VMEM = 40 * 2**20

root_half = math.sqrt(0.5)
density_norm = 1.0 / math.sqrt(2.0 * math.pi)


def halves(table):
    table = table.astype(np.float32)
    high = table.astype(ml_dtypes.bfloat16)
    low = (table - high.astype(np.float32)).astype(ml_dtypes.bfloat16)
    return high, low


def lon_table(columns, mode_count):
    product = np.arange(columns)[:, None] * np.arange(mode_count)[None, :] % columns
    angle = product * (2.0 * math.pi / columns)
    stacked = np.stack([np.cos(angle), -np.sin(angle)], axis=2) * columns**-0.5
    return stacked.reshape(columns, 2 * mode_count)


def lon_tables(blocks, inner, cols):
    modes = MODE_DEV * blocks
    table = lon_table(blocks * inner * cols, modes * inner)
    table = table.reshape(blocks, inner, cols, inner, 2 * modes)
    table = np.pad(table, ((0, 0), (0, 0), (0, PAD - cols), (0, 0), (0, 0)))
    forward = table.transpose(3, 1, 4, 0, 2).reshape(inner, inner, 2 * modes, blocks * PAD)
    split = table.reshape(blocks, inner, 2, HALF, inner, 2 * modes)
    synth = split.transpose(1, 4, 2, 0, 3, 5).reshape(inner, inner, 2 * blocks * HALF, 2 * modes)
    forward, synth = np.concatenate(halves(forward), axis=2), np.concatenate(halves(synth), axis=3)
    return forward.reshape(-1, blocks * PAD), synth.reshape(-1, 4 * modes)


def served(member):
    return [(0, member), (1, member)] + [(base + member, m) for base in BASES for m in range(2)]


def served_table(blocks, cols):
    modes = 2 * MODE_DEV * blocks
    table = lon_table(blocks * 2 * cols, modes).reshape(blocks, 2, cols, 2, modes)
    table = np.pad(table, ((0, 0), (0, 0), (0, PAD - cols), (0, 0), (0, 0)))
    whole = []
    for place in range(blocks):
        for member in range(2):
            rows = np.stack([table[place ^ k, m] for k, m in served(member)])
            rows = np.stack([rows[:, :, member], rows[:, :, 1 - member]], axis=2)
            rows = rows.reshape(len(rows), 2, HALF, 2 * modes).transpose(1, 0, 2, 3)
            whole.append(np.concatenate(halves(rows.reshape(-1, 2 * modes)), axis=1))
    return np.stack(whole).reshape(blocks, 2, *whole[0].shape)


def paired_table(blocks, cols):
    modes = 2 * MODE_DEV * blocks
    table = lon_table(blocks * 2 * cols, modes).reshape(blocks, 2, cols, 2, modes)
    table = np.pad(table, ((0, 0), (0, 0), (0, PAD - cols), (0, 0), (0, 0)))
    whole = []
    for place in range(blocks):
        for member in range(2):
            sources = [(0, 0), (0, 1), (1, member), (1, 1 - member)]
            sources += [(base + m, n) for m in (member, 1 - member) for base in BASES for n in range(2)]
            rows = np.stack([table[place ^ k, n, :, member] for k, n in sources])
            rows = rows.transpose(2, 0, 1).reshape(modes, -1)
            whole.append(np.concatenate(halves(rows)))
    return np.stack(whole).reshape(blocks, 2, *whole[0].shape)


def lat_table(rows, lat_count, group):
    total = rows * lat_count
    product = np.arange(total)[:, None] * np.arange(total)[None, :] % total
    angle = product * (2.0 * math.pi / total)
    c, s = np.cos(angle), np.sin(angle)
    basis = np.stack([np.stack([c, s], -1), np.stack([-s, c], -1)], axis=0) * total**-0.5
    basis = basis.reshape(2, total, lat_count, rows // 2, 2, 2).transpose(0, 1, 2, 4, 3, 5)
    size = 2 * total * group
    return np.einsum("akxhqb,mn->akmxhqnb", basis, np.eye(group)).reshape(size, size)


def all_tables(blocks, inner, cols, rows, lat_count, paired):
    table = lat_table(rows, lat_count, SUB)
    size = table.shape[0]
    lat = np.concatenate(halves(table.reshape(size, lat_count, -1).transpose(1, 0, 2)), axis=1)
    lat = lat.reshape(2 * lat_count * size, -1)
    if paired:
        return lat, [0] * 4
    forward, synth = lon_tables(blocks, inner, cols)
    parts = [forward, lat, synth]
    lanes = max(p.shape[1] for p in parts)
    parts = [np.pad(p, ((0, 0), (0, lanes - p.shape[1]))) for p in parts]
    starts = np.cumsum([0] + [len(p) for p in parts])
    return np.concatenate(parts), [int(n) for n in starts]


def split(values):
    high = values.astype(jnp.bfloat16)
    return high, (values - high.astype(jnp.float32)).astype(jnp.bfloat16)


def dot(left, right, dims=((1,), (0,))):
    return lax.dot_general(left, right, (dims, ((), ())), preferred_element_type=jnp.float32)


def dot3(left, right, dims=((1,), (0,))):
    return dot(left[0], right[0], dims) + (dot(left[0], right[1], dims) + dot(left[1], right[0], dims))


def scaled(values, top):
    level = jnp.maximum(top, 1e-30).astype(jnp.bfloat16).astype(jnp.float32)
    return values * (TOP / level), level


def table_rows(ref, start, count, place):
    return ref[pl.ds(pl.multiple_of(start + place * count, PAD), count), :]


def lat_part(ref, start, size, part, x):
    rows = table_rows(ref, start, 2 * size, x)[:, :part]
    return rows[:size], rows[size:]


def encode(values):
    square = values * values
    fourth = square * square
    return (values * fourth * (fourth * fourth)).astype(jnp.bfloat16)


def decode(coded):
    coded = coded.astype(jnp.float32)
    size = jnp.abs(coded)
    root = jnp.exp(jnp.log(jnp.maximum(size, 1e-37)) * (1.0 / POWER))
    root = jnp.where(size > 0.0, root, 0.0)
    return jnp.where(coded < 0.0, -root, root)


def call(kernel, scalars, inputs, outputs, specs=None, scratch=(), flops=0):
    whole = pl.BlockSpec(memory_space=pltpu.VMEM)
    specs = specs or {}
    in_specs = [specs.get(n, whole) for n in range(len(inputs))]
    out_specs = [whole] * len(outputs)
    moved = sum(math.prod(x.shape) * x.dtype.itemsize for x in (*inputs, *outputs))
    return pl.pallas_call(
        kernel,
        grid_spec=pltpu.PrefetchScalarGridSpec(
            num_scalar_prefetch=1,
            grid=(1,),
            in_specs=in_specs,
            out_specs=out_specs,
            scratch_shapes=list(scratch),
        ),
        out_shape=list(outputs),
        compiler_params=pltpu.CompilerParams(vmem_limit_bytes=VMEM),
        cost_estimate=pl.CostEstimate(flops=flops, bytes_accessed=moved, transcendentals=0),
    )(scalars, *inputs)


def pack_kernel(width, place_ref, x_ref, g_ref, out_ref):
    pack_all(width, x_ref, g_ref, out_ref)


def pack_all(width, x_ref, g_ref, out_ref):
    rows, cols, channels = x_ref.shape
    for q in range(rows // 2):
        lanes = [ref[2 * q + h].astype(jnp.float32) for h in range(2) for ref in (x_ref, g_ref)]
        lanes = [jnp.pad(x, ((0, PAD - cols), (0, 0))) for x in lanes]
        for b in range(channels // width):
            pieces = [x[:, b * width : (b + 1) * width] for x in lanes]
            out_ref[b, q * PAD : (q + 1) * PAD, :] = jnp.concatenate(pieces, axis=1).astype(jnp.bfloat16)


def own_pack_kernel(width, place_ref, fields_ref, pack_ref, side_ref):
    pack_all(width, fields_ref.at[0], fields_ref.at[1], pack_ref)
    side_ref[...] = pack_ref[place_ref[0] ^ 1]


def pair_kernel(width, place_ref, own_ref, x_ref, g_ref, *refs):
    outs, pack_ref = refs[:-1], refs[-1]
    place, member = place_ref[0], place_ref[1]
    pack_all(width, x_ref, g_ref, pack_ref)
    for n, ref in enumerate(outs):
        target = place if n == 0 else place ^ (BASES[n - 1] + member)
        ref[member] = own_ref[target]
        ref[1 - member] = pack_ref[target]


def paired_lon_kernel(place_ref, table_ref, own_ref, side_ref, other_side_ref, *refs):
    pieces = [own_ref.at[0], own_ref.at[1], side_ref, other_side_ref]
    pieces += [ref.at[n] for ref in refs[:-2] for n in range(2)]
    coded_ref, spec_ref = refs[-2:]
    pairs, modes, lanes = spec_ref.shape
    table = table_ref[0, 0]
    tops = []
    for q in range(pairs):
        data = [piece[q * PAD : (q + 1) * PAD, :] for piece in pieces]
        total = dot(table, jnp.concatenate(data, axis=0))
        spec = total[:modes] + total[modes:]
        spec_ref[q] = spec
        tops.append(jnp.max(jnp.abs(spec), axis=0, keepdims=True))
    code_spectrum(coded_ref, spec_ref, tops)


def code_spectrum(coded_ref, spec_ref, tops):
    pairs, modes, lanes = spec_ref.shape
    values, level = scaled(spec_ref[...], functools.reduce(jnp.maximum, tops))
    coded_ref[: pairs * modes, :] = encode(values).reshape(pairs * modes, lanes)
    coded_ref[pairs * modes :, :] = jnp.broadcast_to(level, (PAD, lanes)).astype(jnp.bfloat16)


def lon_kernel(inner, place_ref, table_ref, *refs):
    fields, (coded_ref, spec_ref) = refs[:inner], refs[inner:]
    member = place_ref[1]
    pairs, modes, lanes = spec_ref.shape
    blocks = fields[0].shape[0]
    tops = []
    for q in range(pairs):
        total = None
        for s, field in enumerate(fields):
            source = lax.rem(member - s + inner, inner)
            data = field[:, q * PAD : (q + 1) * PAD, :].reshape(blocks * PAD, lanes)
            term = dot(table_rows(table_ref, 0, 2 * modes, member * inner + source), data)
            total = term if total is None else total + term
        spec = total[:modes] + total[modes:]
        spec_ref[q] = spec
        tops.append(jnp.max(jnp.abs(spec), axis=0, keepdims=True))
    code_spectrum(coded_ref, spec_ref, tops)


def lat_rows(ref, pairs):
    modes = (ref.shape[0] - PAD) // pairs
    wide = ref.shape[1] // 2
    tile = 2 * SUB
    level = ref[pairs * modes :, :].astype(jnp.float32)[:1] * (1.0 / TOP)
    values = [decode(ref[q * modes : (q + 1) * modes, :]) * level for q in range(pairs)]
    rows = []
    for h in range(2):
        for q in range(pairs):
            parts = [
                values[q][n * tile : (n + 1) * tile, h * wide : (h + 1) * wide] for n in range(modes // tile)
            ]
            rows.append(jnp.concatenate(parts, axis=1))
    return jnp.concatenate(rows, axis=0)


def ready_kernel(pairs, start, place_ref, table_ref, spec_ref, win_ref, bin_ref, wout_ref, *outs):
    part_ref, form_ref, bias_ref = outs
    place, x = place_ref[0], place_ref[2]
    for n, ref in enumerate((win_ref, wout_ref)):
        re, im = ref[0, 0], ref[1, 0]
        form = jnp.concatenate([jnp.concatenate([re, im], axis=1), jnp.concatenate([-im, re], axis=1)], axis=0)
        form_ref[2 * n], form_ref[2 * n + 1] = split(form)
    bias = jnp.concatenate([bin_ref[0, pl.ds(place, 1), :], bin_ref[1, pl.ds(place, 1), :]], axis=1)
    bias_ref[...] = jnp.broadcast_to(bias, bias_ref.shape)
    rows = split(lat_rows(spec_ref, pairs))
    part_ref[...] = dot3(lat_part(table_ref, start, part_ref.shape[0], rows[0].shape[0], x), rows)


def mlp_kernel(lat, inner, shares, pairs, start, scaling, place_ref, table_ref, *refs):
    others = refs[: lat - 1]
    part_ref, form_ref, bias_ref = refs[lat - 1 : lat + 2]
    back_ref, *rest = refs[lat + 2 :]
    if shares > 1:
        keep_ref, *send_refs, w_ref = rest
    member, x = place_ref[1], place_ref[2]
    wide = form_ref.shape[1]
    width = wide // 2
    tile = 2 * SUB
    size = part_ref.shape[0]
    points = size // 2
    part = size // lat
    subs = part_ref.shape[1] // wide

    spectra = part_ref[...]
    for s, ref in enumerate(others):
        source = lax.rem(x - s - 1 + lat, lat)
        matrix = lat_part(table_ref, start, size, part, source)
        spectra = spectra + dot3(matrix, split(lat_rows(ref, pairs)))

    def of_points(start):
        rows = []
        for n in range(subs):
            lanes = slice(n * wide + start, n * wide + start + width)
            rows.append(jnp.concatenate([spectra[:points, lanes], spectra[points:, lanes]], axis=1))
        return jnp.concatenate(rows, axis=0)

    spec_x, spec_g = of_points(0), of_points(width)
    m_in, m_out = (form_ref[0], form_ref[1]), (form_ref[2], form_ref[3])
    point = lax.broadcasted_iota(jnp.int32, (subs * points, 1), 0)
    first = ((point & (SUB - 1)) + jnp.where(point < points, 0, SUB) + member * SUB) == 0
    grad_out = spec_g * jnp.where(first, 1.0, 2.0)
    x_parts, g_parts = split(spec_x), split(grad_out)
    pre = dot3(x_parts, m_in) + bias_ref[:1]
    cdf = 0.5 * (1.0 + lax.erf(pre * root_half))
    hidden = pre * cdf
    slopes = cdf + pre * jnp.exp(-0.5 * pre * pre) * density_norm
    grad_pre = dot3(g_parts, m_out, ((1,), (1,))) * slopes
    p_parts = split(grad_pre)
    grad_spec = dot3(p_parts, m_in, ((1,), (1,)))
    lanes = []
    for n in range(subs):
        piece = grad_spec[n * points : (n + 1) * points]
        lanes.append(jnp.concatenate([piece[:, :width], piece[:, width:]], axis=0))
    matrix = lat_part(table_ref, start, size, part, x)
    back = dot3(matrix, split(jnp.concatenate(lanes, axis=1)), ((0,), (0,)))
    for q in range(pairs):
        band = []
        for n in range(subs):
            pieces = [
                back[(h * pairs + q) * tile : (h * pairs + q + 1) * tile, n * width : (n + 1) * width]
                for h in range(2)
            ]
            band.append(jnp.concatenate(pieces, axis=1))
        for n in range(subs):
            if shares > 1:
                back_ref[q, n * tile : (n + 1) * tile, :] = band[n]
            elif n < subs // 2:
                row = (q * subs // 2 + n) * tile
                back_ref[row : row + tile, :] = jnp.concatenate([band[n], band[n + subs // 2]], axis=1)

    pieces = []
    for left, right in ((x_parts, p_parts), (split(hidden), g_parts)):
        total = dot3(left, right, ((0,), (0,)))
        pieces.append(total[:width, :width] + total[width:, width:])
        pieces.append(total[:width, width:] - total[width:, :width])
    weights = jnp.concatenate(pieces, axis=1) * scaling
    bias = jnp.sum(grad_pre, axis=0, keepdims=True) * scaling
    if shares == 1:
        start = pairs * subs // 2 * tile
        back_ref[start : start + width, :] = weights
        rest = jnp.concatenate([bias, jnp.zeros_like(bias)], axis=1)
        back_ref[start + width :, :] = jnp.broadcast_to(rest, (back_ref.shape[0] - start - width, 2 * wide))
        return
    share = width // shares
    w_ref[...] = jnp.zeros_like(w_ref)
    for n in range(shares):
        w_ref[n, :share, :] = weights[n * share : (n + 1) * share]
    w_ref[0, share : share + 1, :wide] = bias
    keep_ref[...] = w_ref[member]
    for s in range(1, shares):
        send_refs[s - 1][...] = w_ref[lax.rem(member + s, shares)]


def synth_kernel(inner, start, place_ref, table_ref, *refs):
    backs, sums, (out_ref, wide_ref) = refs[:inner], refs[inner : 2 * inner], refs[2 * inner :]
    member = place_ref[1]
    pairs, modes, lanes = backs[0].shape
    blocks, total_rows, wide = out_ref.shape
    data_rows = pairs * HALF
    share = lanes // 2 // inner
    for q in range(pairs):
        total = None
        for s, back in enumerate(backs):
            source = lax.rem(member - s + inner, inner)
            rows = table_rows(table_ref, start, 2 * blocks * HALF, member * inner + source)
            term = dot3((rows[:, :modes], rows[:, modes : 2 * modes]), split(back[q]))
            total = term if total is None else total + term
        part = blocks * HALF
        columns = jnp.concatenate([total[:part], total[part:]], axis=1)
        wide_ref[:, q * HALF : (q + 1) * HALF, :] = columns.reshape(blocks, HALF, wide)
    weights = sums[0][...]
    for ref in sums[1:]:
        weights = weights + ref[...]
    coded, tail = code_all(wide_ref[...], weights, share)
    tail = tail[: total_rows - data_rows]
    for b in range(blocks):
        out_ref[b] = jnp.concatenate([coded[b], tail], axis=0).astype(jnp.bfloat16)


def code_all(columns, weights, share):
    rows, wide = columns.shape[1:]
    lanes = wide // 2
    weights, level_w = scaled(weights, jnp.max(jnp.abs(weights), axis=0, keepdims=True))
    top = jnp.max(jnp.max(jnp.abs(columns), axis=0), axis=0, keepdims=True)
    columns, level = scaled(columns, top)
    tail = encode(weights).astype(jnp.float32)
    bias = tail[share : share + 1, :lanes]
    spare = (bias, level_w[:, :lanes], level_w[:, lanes:], level[:, :lanes], level[:, lanes:])
    extra = []
    for n in range(rows // HALF):
        row = jnp.zeros((1, lanes), jnp.float32) if n >= len(spare) else spare[n]
        row = jnp.concatenate([jnp.zeros((1, lanes), jnp.float32), row], axis=1)
        place_row = lax.broadcasted_iota(jnp.int32, (HALF, 1), 0)
        extra.append(jnp.where(place_row == SPARE, row, 0.0))
    extra = jnp.concatenate(extra, axis=0)
    return encode(columns).astype(jnp.float32) + extra, tail


def serve_kernel(pairs, place_ref, table_ref, own_ref, other_ref, *refs):
    outs, wide_ref = refs[:-1], refs[-1]
    count = wide_ref.shape[0]
    modes, lanes = table_ref.shape[3] // 4, own_ref.shape[1] // 2
    half = modes // 2
    share = lanes // 2
    table = table_ref[0, 0]
    matrix = (table[:, : 2 * modes], table[:, 2 * modes :])
    for q in range(pairs):
        bands = [ref[q * half : (q + 1) * half, :] for ref in (own_ref, other_ref)]
        bands = [x[:, start : start + lanes] for x in bands for start in (0, lanes)]
        total = dot3(matrix, split(jnp.concatenate(bands, axis=0)))
        part = count * HALF
        columns = jnp.concatenate([total[:part], total[part:]], axis=1)
        wide_ref[:, q * HALF : (q + 1) * HALF, :] = columns.reshape(count, HALF, 2 * lanes)
    coded, tail = code_all(wide_ref[...], own_ref[pairs * half :, :] + other_ref[pairs * half :, :], share)
    tail = tail[:share]
    for n, ref in enumerate(outs):
        parts = [coded[n]] if n < 2 else [coded[2 * n - 2], coded[2 * n - 1]]
        ref[...] = jnp.concatenate([*parts, tail], axis=0).astype(jnp.bfloat16)


def arrived(ref, member, data_rows):
    raw = ref[...].astype(jnp.float32)
    level = spare_rows(raw, 3, 2) * (1.0 / TOP)
    columns = raw[:data_rows]
    start = data_rows
    if raw.shape[0] == 2 * data_rows + raw.shape[1] // 4:
        start = 2 * data_rows
        columns = jnp.where(member == 0, columns, raw[data_rows:start])
    weights, bias = weight_rows(raw, start)
    return decode(columns) * level, weights, bias


def first_kernel(data_rows, place_ref, *refs):
    member = place_ref[1]
    count = len(refs) - 3
    columns_ref, weights_ref, bias_ref = refs[count:]
    for n in range(count):
        columns_ref[n], weights, bias_ref[n : n + 1, :] = arrived(refs[n], member, data_rows)
        width = weights_ref.shape[3]
        for i in range(4):
            weights_ref[n, i] = weights[:, i * width : (i + 1) * width]


def last_kernel(data_rows, place_ref, *refs):
    place, member = place_ref[0], place_ref[1]
    early, (cot_ref, *refs) = (refs[:3], refs[3:6]), refs[6:]
    lates = refs[: len(BASES)]
    out_ref, win_ref, bin_ref, wout_ref, held_ref = refs[len(BASES) :]
    rows, cols, _ = cot_ref.shape
    blocks = win_ref.shape[1]
    width = win_ref.shape[2]
    pairs = rows // 2

    def settle(source, columns, weights, bias):
        held_ref[source] = columns
        for i in range(4):
            target = (win_ref, wout_ref)[i // 2]
            target[i % 2, source] = weights[i]
        for k in range(2):
            bin_ref[k, pl.ds(source, 1), :] = bias[:, k * width : (k + 1) * width]

    sources = ([place, place ^ 1], [place ^ (base + member) for base in BASES])
    for group, (columns_ref, weights_ref, bias_ref) in zip(sources, early):
        for n, source in enumerate(group):
            settle(source, columns_ref[n], weights_ref.at[n], bias_ref[n : n + 1, :])
    for ref, base in zip(lates, BASES):
        columns, weights, bias = arrived(ref, member, data_rows)
        parts = [weights[:, i * width : (i + 1) * width] for i in range(4)]
        settle(place ^ (base + 1 - member), columns, parts, bias)
    for q in range(pairs):
        for h in range(2):
            parts = []
            for half in range(2):
                start = (2 * half + h) * width
                pieces = [
                    held_ref[b, q * HALF : (q + 1) * HALF, :][:, start : start + width] for b in range(blocks)
                ]
                parts.append(jnp.concatenate(pieces, axis=1))
            column = jnp.concatenate(parts, axis=0)[:cols]
            row = 2 * q + h
            out_ref[row] = (cot_ref[row].astype(jnp.float32) + column).astype(jnp.bfloat16)


def spare_rows(raw, first, count):
    lanes = raw.shape[1] // 2
    rows = [raw[n * HALF + SPARE : n * HALF + SPARE + 1, lanes:] for n in range(first, first + count)]
    return jnp.concatenate(rows, axis=1)


def weight_rows(raw, data_rows):
    level = spare_rows(raw, 1, 2) * (1.0 / TOP)
    bias = decode(spare_rows(raw, 0, 1)) * level[:, : raw.shape[1] // 2]
    return decode(raw[data_rows:]) * level, bias


def columns_kernel(place_ref, data_ref, cot_ref, out_ref, held_ref, bias_ref):
    rows, cols, _ = cot_ref.shape
    blocks, total_rows, wide = data_ref.shape
    width = wide // 4
    pairs = rows // 2
    values = []
    for b in range(blocks):
        raw = data_ref[b].astype(jnp.float32)
        values.append(decode(raw[: pairs * HALF]) * (spare_rows(raw, 3, 2) * (1.0 / TOP)))
        held_ref[b], bias_ref[b : b + 1, :] = weight_rows(raw, pairs * HALF)
    for q in range(pairs):
        for h in range(2):
            parts = []
            for half in range(2):
                start = (2 * half + h) * width
                pieces = [v[q * HALF : (q + 1) * HALF, start : start + width] for v in values]
                parts.append(jnp.concatenate(pieces, axis=1))
            column = jnp.concatenate(parts, axis=0)[:cols]
            row = 2 * q + h
            out_ref[row] = (cot_ref[row].astype(jnp.float32) + column).astype(jnp.bfloat16)


def weights_kernel(inner, share, place_ref, held_ref, own_bias_ref, *refs):
    pieces, (win_ref, bin_ref, wout_ref) = refs[: inner - 1], refs[inner - 1 :]
    member = place_ref[1]
    blocks, rows, wide = held_ref.shape
    width = wide // 4
    data_rows = pieces[0].shape[1] - rows
    for b in range(blocks):
        held = [(held_ref[b], own_bias_ref[b : b + 1, :])]
        held += [weight_rows(ref[b].astype(jnp.float32), data_rows) for ref in pieces]
        for n in range(inner):
            part, bias = held[0]
            for s in range(1, inner):
                chosen = lax.rem(member - s + inner, inner) == n
                part = jnp.where(chosen, held[s][0], part)
                bias = jnp.where(chosen, held[s][1], bias)
            for i in range(4):
                target = (win_ref, wout_ref)[i // 2]
                target[i % 2, b, n * share : (n + 1) * share, :] = part[:share, i * width : (i + 1) * width]
            if n == 0:
                for k in range(2):
                    bin_ref[k, b : b + 1, :] = bias[:, k * width : (k + 1) * width]


def body(features, cotangent, weight_in, bias_in, weight_out):
    lon_count, lat_count = lax.axis_size("lon"), lax.axis_size("lat")
    blocks, width = weight_in.shape[1:3]
    rows, cols, _ = features.shape
    inner = lon_count // blocks
    pairs = rows // 2
    wide = 4 * width
    modes = 2 * MODE_DEV * blocks
    size = 2 * rows * lat_count * SUB
    subs = modes // (2 * SUB)
    lon_place = lax.axis_index("lon")
    lat_place = lax.axis_index("lat")
    scalars = jnp.stack([lon_place // inner, lon_place % inner, lat_place]).astype(jnp.int32)
    scaling = (rows * lat_count * modes // 2 * inner) ** -0.5
    paired = inner == 2 and blocks == 2 + 2 * len(BASES)
    tables, starts = all_tables(blocks, inner, cols, rows, lat_count, paired)
    lon_start, lat_start, synth_start, _ = starts
    shares = 1 if paired else inner
    share = width // shares
    data_rows = pairs * HALF
    total_rows = data_rows + -(-share // 8) * 8
    sum_rows = -(-(share + 1) // 8) * 8
    f32, bf16 = jnp.float32, jnp.bfloat16
    shape = jax.ShapeDtypeStruct

    places = [[g * inner + i for g in range(blocks)] for i in range(inner)]

    def exchange(values):
        return lax.all_to_all(
            values, "lon", split_axis=0, concat_axis=0, tiled=True, axis_index_groups=places
        )

    def to_member(values, step):
        turn = [(i, i // inner * inner + (i + step) % inner) for i in range(lon_count)]
        return lax.ppermute(values, "lon", turn)

    def to_place(values, first, second):
        turn = [(i, (i // 2 ^ (second if i % 2 else first)) * 2 + i % 2) for i in range(lon_count)]
        return lax.ppermute(values, "lon", turn)

    def to_lat(values, step):
        return lax.ppermute(values, "lat", [(i, (i + step) % lat_count) for i in range(lat_count)])

    def by_place(table):
        return pl.BlockSpec((1, 1, *table.shape[2:]), lambda i, s: (s[0], s[1], 0, 0))

    def serve(slots):
        return [to_place(x, base, base + 1) for x, base in zip(slots, BASES)]

    spectrum = dict(
        outputs=(shape((pairs * modes + PAD, wide), bf16),),
        scratch=(pltpu.VMEM((pairs, modes, wide), f32),),
    )
    if paired:
        rows_in = pairs * PAD
        packed, side = call(
            functools.partial(own_pack_kernel, width),
            scalars,
            (jnp.stack([features, cotangent]),),
            (shape((blocks, rows_in, wide), bf16), shape((rows_in, wide), bf16)),
            flops=10**8,
        )
        own, *slots = call(
            functools.partial(pair_kernel, width),
            scalars,
            (packed, to_member(features, 1), to_member(cotangent, 1)),
            [shape((2, rows_in, wide), bf16)] * (1 + len(BASES)),
            scratch=(pltpu.VMEM((blocks, rows_in, wide), bf16),),
        )
        side = to_place(side, 1, 1)
        sent = [side, *serve(slots)]
        late = [to_member(x, 1) for x in sent]
        sent, late = [side, late[0], *sent[1:]], late[1:]
        table = paired_table(blocks, cols)
        (coded,) = call(
            paired_lon_kernel, scalars, (table, own, *sent, *late), specs={0: by_place(table)}, **spectrum
        )
    else:
        (packed,) = call(
            functools.partial(pack_kernel, width),
            scalars,
            (features, cotangent),
            (shape((blocks, pairs * PAD, wide), bf16),),
        )
        whole = exchange(packed)
        fields = [whole] + [to_member(whole, s) for s in range(1, inner)]
        (coded,) = call(functools.partial(lon_kernel, inner), scalars, (tables, *fields), **spectrum)
    others = [to_lat(coded, s) for s in range(1, lat_count)]
    block_spec = pl.BlockSpec((2, 1, width, width), lambda i, s: (0, s[0], 0, 0))
    part, forms, bias = call(
        functools.partial(ready_kernel, pairs, lat_start),
        scalars,
        (tables, coded, weight_in, bias_in, weight_out),
        (
            shape((size, 2 * subs * width), f32),
            shape((4, 2 * width, 2 * width), bf16),
            shape((8, 2 * width), f32),
        ),
        specs={2: block_spec, 4: block_spec},
        flops=6 * size * size // lat_count * 2 * subs * width,
    )
    if paired:
        outs = [shape((pairs * modes // 2 + sum_rows, wide), f32)]
    else:
        outs = [shape((pairs, modes, 2 * width), f32), *[shape((sum_rows, wide), f32)] * shares]
    back, *rest = call(
        functools.partial(mlp_kernel, lat_count, inner, shares, pairs, lat_start, scaling),
        scalars,
        (tables, *others, part, forms, bias),
        outs,
        scratch=() if paired else (pltpu.VMEM((shares, sum_rows, wide), f32),),
    )
    backs = [back] + [to_member(back, s) for s in range(1, inner)]
    if paired:
        table = served_table(blocks, cols)
        count = table.shape[2] // PAD
        outs = [share + data_rows] * 2 + [share + 2 * data_rows] * len(BASES)
        own, side, *slots = call(
            functools.partial(serve_kernel, pairs),
            scalars,
            (table, *backs),
            [shape((n, wide), bf16) for n in outs],
            specs={0: by_place(table)},
            scratch=(pltpu.VMEM((count, data_rows, wide), f32),),
        )
        sent = serve(slots)

        def first(group):
            n = len(group)
            return call(
                functools.partial(first_kernel, data_rows),
                scalars,
                group,
                (
                    shape((n, data_rows, wide), f32),
                    shape((n, 4, share, width), f32),
                    shape((n, 2 * width), f32),
                ),
            )

        held, sent[0] = lax.optimization_barrier((first([own, to_place(side, 1, 1)]), sent[0]))
        late = [to_member(x, 1) for x in sent]
        held = [*held, *first(sent)]
        return call(
            functools.partial(last_kernel, data_rows),
            scalars,
            (*held, cotangent, *late),
            [shape(x.shape, x.dtype) for x in (features, weight_in, bias_in, weight_out)],
            scratch=(pltpu.VMEM((blocks, data_rows, wide), f32),),
        )
    keep, *send = rest
    sums = [keep] + [to_member(send[s - 1], s) for s in range(1, inner)]
    (payload,) = call(
        functools.partial(synth_kernel, inner, synth_start),
        scalars,
        (tables, *backs, *sums),
        (shape((blocks, total_rows, wide), bf16),),
        scratch=(pltpu.VMEM((blocks, pairs * HALF, wide), f32),),
    )
    returned = exchange(payload)
    gathered = [to_member(returned, s) for s in range(1, inner)]
    weight_part = total_rows - pairs * HALF
    grad_features, held, held_bias = call(
        columns_kernel,
        scalars,
        (returned, cotangent),
        (
            shape(features.shape, bf16),
            shape((blocks, weight_part, wide), f32),
            shape((blocks, 2 * width), f32),
        ),
    )
    grad_w_in, grad_b_in, grad_w_out = call(
        functools.partial(weights_kernel, inner, share),
        scalars,
        (held, held_bias, *gathered),
        (shape(weight_in.shape, f32), shape(bias_in.shape, f32), shape(weight_out.shape, f32)),
    )
    return grad_features, grad_w_in, grad_b_in, grad_w_out


def solution(mesh):
    placed = (P("lat", "lon", None), P("lat", "lon", None), P(), P(), P())
    return jax.shard_map(
        body,
        mesh=mesh,
        in_specs=placed,
        out_specs=(P("lat", "lon", None), P(), P(), P()),
        check_vma=False,
    )
```

```python
import functools
import math

import jax
import jax.numpy as jnp
import ml_dtypes
import numpy as np
from jax import lax
from jax.experimental import pallas as pl
from jax.experimental.pallas import tpu as pltpu
from jax.sharding import PartitionSpec as P

MODE_DEV = 4
PAD = 16
HALF = PAD // 2
BASES = (6, 2, 4)
SUB = 4
SPARE = 6
POWER = 13.0
TOP = 2.0**9
VMEM = 40 * 2**20

root_half = math.sqrt(0.5)
density_norm = 1.0 / math.sqrt(2.0 * math.pi)


def halves(table):
    table = table.astype(np.float32)
    high = table.astype(ml_dtypes.bfloat16)
    low = (table - high.astype(np.float32)).astype(ml_dtypes.bfloat16)
    return high, low


def lon_table(columns, mode_count):
    product = np.arange(columns)[:, None] * np.arange(mode_count)[None, :] % columns
    angle = product * (2.0 * math.pi / columns)
    stacked = np.stack([np.cos(angle), -np.sin(angle)], axis=2) * columns**-0.5
    return stacked.reshape(columns, 2 * mode_count)


def lon_tables(blocks, inner, cols):
    modes = MODE_DEV * blocks
    table = lon_table(blocks * inner * cols, modes * inner)
    table = table.reshape(blocks, inner, cols, inner, 2 * modes)
    table = np.pad(table, ((0, 0), (0, 0), (0, PAD - cols), (0, 0), (0, 0)))
    forward = table.transpose(3, 1, 4, 0, 2).reshape(inner, inner, 2 * modes, blocks * PAD)
    split = table.reshape(blocks, inner, 2, HALF, inner, 2 * modes)
    synth = split.transpose(1, 4, 2, 0, 3, 5).reshape(inner, inner, 2 * blocks * HALF, 2 * modes)
    forward, synth = np.concatenate(halves(forward), axis=2), np.concatenate(halves(synth), axis=3)
    return forward.reshape(-1, blocks * PAD), synth.reshape(-1, 4 * modes)


def served(member):
    return [(0, member), (1, member)] + [(base + member, m) for base in BASES for m in range(2)]


def served_table(blocks, cols):
    modes = 2 * MODE_DEV * blocks
    table = lon_table(blocks * 2 * cols, modes).reshape(blocks, 2, cols, 2, modes)
    table = np.pad(table, ((0, 0), (0, 0), (0, PAD - cols), (0, 0), (0, 0)))
    whole = []
    for place in range(blocks):
        for member in range(2):
            rows = np.stack([table[place ^ k, m] for k, m in served(member)])
            rows = np.stack([rows[:, :, member], rows[:, :, 1 - member]], axis=2)
            rows = rows.reshape(len(rows), 2, HALF, 2 * modes).transpose(1, 0, 2, 3)
            whole.append(np.concatenate(halves(rows.reshape(-1, 2 * modes)), axis=1))
    return np.stack(whole).reshape(blocks, 2, *whole[0].shape)


def paired_table(blocks, cols):
    modes = 2 * MODE_DEV * blocks
    table = lon_table(blocks * 2 * cols, modes).reshape(blocks, 2, cols, 2, modes)
    table = np.pad(table, ((0, 0), (0, 0), (0, PAD - cols), (0, 0), (0, 0)))
    whole = []
    for place in range(blocks):
        for member in range(2):
            sources = [(0, 0), (0, 1), (1, member)]
            sources += [(base + member, n) for base in BASES for n in range(2)] + [(1, 1 - member)]
            sources += [(base + 1 - member, n) for base in BASES for n in range(2)]
            rows = np.stack([table[place ^ k, n, :, member] for k, n in sources])
            rows = rows.transpose(2, 0, 1).reshape(modes, -1)
            whole.append(np.concatenate(halves(rows)))
    return np.stack(whole).reshape(blocks, 2, *whole[0].shape)


def lat_table(rows, lat_count, group):
    total = rows * lat_count
    product = np.arange(total)[:, None] * np.arange(total)[None, :] % total
    angle = product * (2.0 * math.pi / total)
    c, s = np.cos(angle), np.sin(angle)
    basis = np.stack([np.stack([c, s], -1), np.stack([-s, c], -1)], axis=0) * total**-0.5
    basis = basis.reshape(2, total, lat_count, rows // 2, 2, 2).transpose(0, 1, 2, 4, 3, 5)
    size = 2 * total * group
    return np.einsum("akxhqb,mn->akmxhqnb", basis, np.eye(group)).reshape(size, size)


def all_tables(blocks, inner, cols, rows, lat_count, paired):
    table = lat_table(rows, lat_count, SUB)
    size = table.shape[0]
    lat = np.concatenate(halves(table.reshape(size, lat_count, -1).transpose(1, 0, 2)), axis=1)
    lat = lat.reshape(2 * lat_count * size, -1)
    if paired:
        return lat, [0] * 4
    forward, synth = lon_tables(blocks, inner, cols)
    parts = [forward, lat, synth]
    lanes = max(p.shape[1] for p in parts)
    parts = [np.pad(p, ((0, 0), (0, lanes - p.shape[1]))) for p in parts]
    starts = np.cumsum([0] + [len(p) for p in parts])
    return np.concatenate(parts), [int(n) for n in starts]


def split(values):
    high = values.astype(jnp.bfloat16)
    return high, (values - high.astype(jnp.float32)).astype(jnp.bfloat16)


def dot(left, right, dims=((1,), (0,))):
    return lax.dot_general(left, right, (dims, ((), ())), preferred_element_type=jnp.float32)


def dot3(left, right, dims=((1,), (0,))):
    return dot(left[0], right[0], dims) + (dot(left[0], right[1], dims) + dot(left[1], right[0], dims))


def scaled(values, top):
    level = jnp.maximum(top, 1e-30).astype(jnp.bfloat16).astype(jnp.float32)
    return values * (TOP / level), level


def table_rows(ref, start, count, place):
    return ref[pl.ds(pl.multiple_of(start + place * count, PAD), count), :]


def lat_part(ref, start, size, part, x):
    rows = table_rows(ref, start, 2 * size, x)[:, :part]
    return rows[:size], rows[size:]


def encode(values):
    square = values * values
    fourth = square * square
    return (values * fourth * (fourth * fourth)).astype(jnp.bfloat16)


def decode(coded):
    coded = coded.astype(jnp.float32)
    size = jnp.abs(coded)
    root = jnp.exp(jnp.log(jnp.maximum(size, 1e-37)) * (1.0 / POWER))
    root = jnp.where(size > 0.0, root, 0.0)
    return jnp.where(coded < 0.0, -root, root)


def call(kernel, scalars, inputs, outputs, specs=None, scratch=(), flops=0):
    whole = pl.BlockSpec(memory_space=pltpu.VMEM)
    specs = specs or {}
    in_specs = [specs.get(n, whole) for n in range(len(inputs))]
    out_specs = [whole] * len(outputs)
    moved = sum(math.prod(x.shape) * x.dtype.itemsize for x in (*inputs, *outputs))
    return pl.pallas_call(
        kernel,
        grid_spec=pltpu.PrefetchScalarGridSpec(
            num_scalar_prefetch=1,
            grid=(1,),
            in_specs=in_specs,
            out_specs=out_specs,
            scratch_shapes=list(scratch),
        ),
        out_shape=list(outputs),
        compiler_params=pltpu.CompilerParams(vmem_limit_bytes=VMEM),
        cost_estimate=pl.CostEstimate(flops=flops, bytes_accessed=moved, transcendentals=0),
    )(scalars, *inputs)


def pack_kernel(width, place_ref, x_ref, g_ref, out_ref):
    pack_all(width, x_ref, g_ref, out_ref)


def pack_all(width, x_ref, g_ref, out_ref):
    rows, cols, channels = x_ref.shape
    for q in range(rows // 2):
        lanes = [ref[2 * q + h].astype(jnp.float32) for h in range(2) for ref in (x_ref, g_ref)]
        lanes = [jnp.pad(x, ((0, PAD - cols), (0, 0))) for x in lanes]
        for b in range(channels // width):
            pieces = [x[:, b * width : (b + 1) * width] for x in lanes]
            out_ref[b, q * PAD : (q + 1) * PAD, :] = jnp.concatenate(pieces, axis=1).astype(jnp.bfloat16)


def own_pack_kernel(width, place_ref, fields_ref, pack_ref, side_ref):
    pack_all(width, fields_ref.at[0], fields_ref.at[1], pack_ref)
    side_ref[...] = pack_ref[place_ref[0] ^ 1]


def pair_kernel(width, place_ref, own_ref, x_ref, g_ref, *refs):
    outs, pack_ref = refs[:-1], refs[-1]
    place, member = place_ref[0], place_ref[1]
    pack_all(width, x_ref, g_ref, pack_ref)
    for n, ref in enumerate(outs):
        target = place if n == 0 else place ^ (BASES[n - 1] + member)
        ref[member] = own_ref[target]
        ref[1 - member] = pack_ref[target]


def early_lon_kernel(place_ref, table_ref, own_ref, side_ref, *refs):
    sent, out_ref = refs[:-1], refs[-1]
    pieces = [own_ref.at[0], own_ref.at[1], side_ref] + [ref.at[n] for ref in sent for n in range(2)]
    table = table_ref[0, 0][:, : len(pieces) * PAD]
    for q in range(out_ref.shape[0]):
        data = [piece[q * PAD : (q + 1) * PAD, :] for piece in pieces]
        out_ref[q] = dot(table, jnp.concatenate(data, axis=0))


def late_lon_kernel(place_ref, table_ref, early_ref, side_ref, *refs):
    late, (coded_ref, spec_ref) = refs[:-2], refs[-2:]
    pieces = [side_ref] + [ref.at[n] for ref in late for n in range(2)]
    pairs, modes, lanes = spec_ref.shape
    table = table_ref[0, 0][:, table_ref.shape[3] - len(pieces) * PAD :]
    tops = []
    for q in range(pairs):
        data = [piece[q * PAD : (q + 1) * PAD, :] for piece in pieces]
        total = early_ref[q] + dot(table, jnp.concatenate(data, axis=0))
        spec = total[:modes] + total[modes:]
        spec_ref[q] = spec
        tops.append(jnp.max(jnp.abs(spec), axis=0, keepdims=True))
    code_spectrum(coded_ref, spec_ref, tops)


def code_spectrum(coded_ref, spec_ref, tops):
    pairs, modes, lanes = spec_ref.shape
    values, level = scaled(spec_ref[...], functools.reduce(jnp.maximum, tops))
    coded_ref[: pairs * modes, :] = encode(values).reshape(pairs * modes, lanes)
    coded_ref[pairs * modes :, :] = jnp.broadcast_to(level, (PAD, lanes)).astype(jnp.bfloat16)


def lon_kernel(inner, place_ref, table_ref, *refs):
    fields, (coded_ref, spec_ref) = refs[:inner], refs[inner:]
    member = place_ref[1]
    pairs, modes, lanes = spec_ref.shape
    blocks = fields[0].shape[0]
    tops = []
    for q in range(pairs):
        total = None
        for s, field in enumerate(fields):
            source = lax.rem(member - s + inner, inner)
            data = field[:, q * PAD : (q + 1) * PAD, :].reshape(blocks * PAD, lanes)
            term = dot(table_rows(table_ref, 0, 2 * modes, member * inner + source), data)
            total = term if total is None else total + term
        spec = total[:modes] + total[modes:]
        spec_ref[q] = spec
        tops.append(jnp.max(jnp.abs(spec), axis=0, keepdims=True))
    code_spectrum(coded_ref, spec_ref, tops)


def lat_rows(ref, pairs):
    modes = (ref.shape[0] - PAD) // pairs
    wide = ref.shape[1] // 2
    tile = 2 * SUB
    level = ref[pairs * modes :, :].astype(jnp.float32)[:1] * (1.0 / TOP)
    values = [decode(ref[q * modes : (q + 1) * modes, :]) * level for q in range(pairs)]
    rows = []
    for h in range(2):
        for q in range(pairs):
            parts = [
                values[q][n * tile : (n + 1) * tile, h * wide : (h + 1) * wide] for n in range(modes // tile)
            ]
            rows.append(jnp.concatenate(parts, axis=1))
    return jnp.concatenate(rows, axis=0)


def ready_kernel(pairs, start, place_ref, table_ref, spec_ref, win_ref, bin_ref, wout_ref, *outs):
    part_ref, form_ref, bias_ref = outs
    place, x = place_ref[0], place_ref[2]
    for n, ref in enumerate((win_ref, wout_ref)):
        re, im = ref[0, 0], ref[1, 0]
        form = jnp.concatenate([jnp.concatenate([re, im], axis=1), jnp.concatenate([-im, re], axis=1)], axis=0)
        form_ref[2 * n], form_ref[2 * n + 1] = split(form)
    bias = jnp.concatenate([bin_ref[0, pl.ds(place, 1), :], bin_ref[1, pl.ds(place, 1), :]], axis=1)
    bias_ref[...] = jnp.broadcast_to(bias, bias_ref.shape)
    rows = split(lat_rows(spec_ref, pairs))
    part_ref[...] = dot3(lat_part(table_ref, start, part_ref.shape[0], rows[0].shape[0], x), rows)


def mlp_kernel(lat, inner, shares, pairs, start, scaling, place_ref, table_ref, *refs):
    others = refs[: lat - 1]
    part_ref, form_ref, bias_ref = refs[lat - 1 : lat + 2]
    back_ref, *rest = refs[lat + 2 :]
    if shares > 1:
        keep_ref, *send_refs, w_ref = rest
    member, x = place_ref[1], place_ref[2]
    wide = form_ref.shape[1]
    width = wide // 2
    tile = 2 * SUB
    size = part_ref.shape[0]
    points = size // 2
    part = size // lat
    subs = part_ref.shape[1] // wide

    spectra = part_ref[...]
    for s, ref in enumerate(others):
        source = lax.rem(x - s - 1 + lat, lat)
        matrix = lat_part(table_ref, start, size, part, source)
        spectra = spectra + dot3(matrix, split(lat_rows(ref, pairs)))

    def of_points(start):
        rows = []
        for n in range(subs):
            lanes = slice(n * wide + start, n * wide + start + width)
            rows.append(jnp.concatenate([spectra[:points, lanes], spectra[points:, lanes]], axis=1))
        return jnp.concatenate(rows, axis=0)

    spec_x, spec_g = of_points(0), of_points(width)
    m_in, m_out = (form_ref[0], form_ref[1]), (form_ref[2], form_ref[3])
    point = lax.broadcasted_iota(jnp.int32, (subs * points, 1), 0)
    first = ((point & (SUB - 1)) + jnp.where(point < points, 0, SUB) + member * SUB) == 0
    grad_out = spec_g * jnp.where(first, 1.0, 2.0)
    x_parts, g_parts = split(spec_x), split(grad_out)
    pre = dot3(x_parts, m_in) + bias_ref[:1]
    cdf = 0.5 * (1.0 + lax.erf(pre * root_half))
    hidden = pre * cdf
    slopes = cdf + pre * jnp.exp(-0.5 * pre * pre) * density_norm
    grad_pre = dot3(g_parts, m_out, ((1,), (1,))) * slopes
    p_parts = split(grad_pre)
    products = []
    for left, right in ((x_parts, p_parts), (split(hidden), g_parts)):
        total = dot3(left, right, ((0,), (0,)))
        products.append(total[:width, :width] + total[width:, width:])
        products.append(total[:width, width:] - total[width:, :width])
    weights = jnp.concatenate(products, axis=1) * scaling
    grad_spec = dot3(p_parts, m_in, ((1,), (1,)))
    lanes = []
    for n in range(subs):
        piece = grad_spec[n * points : (n + 1) * points]
        lanes.append(jnp.concatenate([piece[:, :width], piece[:, width:]], axis=0))
    matrix = lat_part(table_ref, start, size, part, x)
    back = dot3(matrix, split(jnp.concatenate(lanes, axis=1)), ((0,), (0,)))
    for q in range(pairs):
        band = []
        for n in range(subs):
            pieces = [
                back[(h * pairs + q) * tile : (h * pairs + q + 1) * tile, n * width : (n + 1) * width]
                for h in range(2)
            ]
            band.append(jnp.concatenate(pieces, axis=1))
        for n in range(subs):
            if shares > 1:
                back_ref[q, n * tile : (n + 1) * tile, :] = band[n]
            elif n < subs // 2:
                row = (q * subs // 2 + n) * tile
                back_ref[row : row + tile, :] = jnp.concatenate([band[n], band[n + subs // 2]], axis=1)

    bias = jnp.sum(grad_pre, axis=0, keepdims=True) * scaling
    if shares == 1:
        start = pairs * subs // 2 * tile
        back_ref[start : start + width, :] = weights
        rest = jnp.concatenate([bias, jnp.zeros_like(bias)], axis=1)
        back_ref[start + width :, :] = jnp.broadcast_to(rest, (back_ref.shape[0] - start - width, 2 * wide))
        return
    share = width // shares
    w_ref[...] = jnp.zeros_like(w_ref)
    for n in range(shares):
        w_ref[n, :share, :] = weights[n * share : (n + 1) * share]
    w_ref[0, share : share + 1, :wide] = bias
    keep_ref[...] = w_ref[member]
    for s in range(1, shares):
        send_refs[s - 1][...] = w_ref[lax.rem(member + s, shares)]


def synth_kernel(inner, start, place_ref, table_ref, *refs):
    backs, sums, (out_ref, wide_ref) = refs[:inner], refs[inner : 2 * inner], refs[2 * inner :]
    member = place_ref[1]
    pairs, modes, lanes = backs[0].shape
    blocks, total_rows, wide = out_ref.shape
    data_rows = pairs * HALF
    share = lanes // 2 // inner
    for q in range(pairs):
        total = None
        for s, back in enumerate(backs):
            source = lax.rem(member - s + inner, inner)
            rows = table_rows(table_ref, start, 2 * blocks * HALF, member * inner + source)
            term = dot3((rows[:, :modes], rows[:, modes : 2 * modes]), split(back[q]))
            total = term if total is None else total + term
        part = blocks * HALF
        columns = jnp.concatenate([total[:part], total[part:]], axis=1)
        wide_ref[:, q * HALF : (q + 1) * HALF, :] = columns.reshape(blocks, HALF, wide)
    weights = sums[0][...]
    for ref in sums[1:]:
        weights = weights + ref[...]
    coded, tail = code_all(wide_ref[...], weights, share)
    tail = tail[: total_rows - data_rows]
    for b in range(blocks):
        out_ref[b] = jnp.concatenate([coded[b], tail], axis=0).astype(jnp.bfloat16)


def code_all(columns, weights, share):
    rows, wide = columns.shape[1:]
    lanes = wide // 2
    weights, level_w = scaled(weights, jnp.max(jnp.abs(weights), axis=0, keepdims=True))
    top = jnp.max(jnp.max(jnp.abs(columns), axis=0), axis=0, keepdims=True)
    columns, level = scaled(columns, top)
    tail = encode(weights).astype(jnp.float32)
    bias = tail[share : share + 1, :lanes]
    spare = (bias, level_w[:, :lanes], level_w[:, lanes:], level[:, :lanes], level[:, lanes:])
    extra = []
    for n in range(rows // HALF):
        row = jnp.zeros((1, lanes), jnp.float32) if n >= len(spare) else spare[n]
        row = jnp.concatenate([jnp.zeros((1, lanes), jnp.float32), row], axis=1)
        place_row = lax.broadcasted_iota(jnp.int32, (HALF, 1), 0)
        extra.append(jnp.where(place_row == SPARE, row, 0.0))
    extra = jnp.concatenate(extra, axis=0)
    return encode(columns).astype(jnp.float32) + extra, tail


def serve_kernel(pairs, place_ref, table_ref, own_ref, other_ref, *refs):
    outs, wide_ref = refs[:-1], refs[-1]
    count = wide_ref.shape[0]
    modes, lanes = table_ref.shape[3] // 4, own_ref.shape[1] // 2
    half = modes // 2
    share = lanes // 2
    table = table_ref[0, 0]
    matrix = (table[:, : 2 * modes], table[:, 2 * modes :])
    for q in range(pairs):
        bands = [ref[q * half : (q + 1) * half, :] for ref in (own_ref, other_ref)]
        bands = [x[:, start : start + lanes] for x in bands for start in (0, lanes)]
        total = dot3(matrix, split(jnp.concatenate(bands, axis=0)))
        part = count * HALF
        columns = jnp.concatenate([total[:part], total[part:]], axis=1)
        wide_ref[:, q * HALF : (q + 1) * HALF, :] = columns.reshape(count, HALF, 2 * lanes)
    coded, tail = code_all(wide_ref[...], own_ref[pairs * half :, :] + other_ref[pairs * half :, :], share)
    tail = tail[:share]
    for n, ref in enumerate(outs):
        parts = [coded[n]] if n < 2 else [coded[2 * n - 2], coded[2 * n - 1]]
        ref[...] = jnp.concatenate([*parts, tail], axis=0).astype(jnp.bfloat16)


def arrived(ref, member, data_rows):
    raw = ref[...].astype(jnp.float32)
    level = spare_rows(raw, 3, 2) * (1.0 / TOP)
    columns = raw[:data_rows]
    start = data_rows
    if raw.shape[0] == 2 * data_rows + raw.shape[1] // 4:
        start = 2 * data_rows
        columns = jnp.where(member == 0, columns, raw[data_rows:start])
    weights, bias = weight_rows(raw, start)
    return decode(columns) * level, weights, bias


def first_kernel(data_rows, place_ref, *refs):
    member = place_ref[1]
    count = len(refs) - 3
    columns_ref, weights_ref, bias_ref = refs[count:]
    for n in range(count):
        columns_ref[n], weights, bias_ref[n : n + 1, :] = arrived(refs[n], member, data_rows)
        width = weights_ref.shape[3]
        for i in range(4):
            weights_ref[n, i] = weights[:, i * width : (i + 1) * width]


def last_kernel(data_rows, place_ref, *refs):
    place, member = place_ref[0], place_ref[1]
    early, (cot_ref, *refs) = (refs[:3], refs[3:6]), refs[6:]
    lates = refs[: len(BASES)]
    out_ref, win_ref, bin_ref, wout_ref, held_ref = refs[len(BASES) :]
    rows, cols, _ = cot_ref.shape
    blocks = win_ref.shape[1]
    width = win_ref.shape[2]
    pairs = rows // 2

    def settle(source, columns, weights, bias):
        held_ref[source] = columns
        for i in range(4):
            target = (win_ref, wout_ref)[i // 2]
            target[i % 2, source] = weights[i]
        for k in range(2):
            bin_ref[k, pl.ds(source, 1), :] = bias[:, k * width : (k + 1) * width]

    sources = ([place, place ^ 1], [place ^ (base + member) for base in BASES])
    for group, (columns_ref, weights_ref, bias_ref) in zip(sources, early):
        for n, source in enumerate(group):
            settle(source, columns_ref[n], weights_ref.at[n], bias_ref[n : n + 1, :])
    for ref, base in zip(lates, BASES):
        columns, weights, bias = arrived(ref, member, data_rows)
        parts = [weights[:, i * width : (i + 1) * width] for i in range(4)]
        settle(place ^ (base + 1 - member), columns, parts, bias)
    for q in range(pairs):
        for h in range(2):
            parts = []
            for half in range(2):
                start = (2 * half + h) * width
                pieces = [
                    held_ref[b, q * HALF : (q + 1) * HALF, :][:, start : start + width] for b in range(blocks)
                ]
                parts.append(jnp.concatenate(pieces, axis=1))
            column = jnp.concatenate(parts, axis=0)[:cols]
            row = 2 * q + h
            out_ref[row] = (cot_ref[row].astype(jnp.float32) + column).astype(jnp.bfloat16)


def spare_rows(raw, first, count):
    lanes = raw.shape[1] // 2
    rows = [raw[n * HALF + SPARE : n * HALF + SPARE + 1, lanes:] for n in range(first, first + count)]
    return jnp.concatenate(rows, axis=1)


def weight_rows(raw, data_rows):
    level = spare_rows(raw, 1, 2) * (1.0 / TOP)
    bias = decode(spare_rows(raw, 0, 1)) * level[:, : raw.shape[1] // 2]
    return decode(raw[data_rows:]) * level, bias


def columns_kernel(place_ref, data_ref, cot_ref, out_ref, held_ref, bias_ref):
    rows, cols, _ = cot_ref.shape
    blocks, total_rows, wide = data_ref.shape
    width = wide // 4
    pairs = rows // 2
    values = []
    for b in range(blocks):
        raw = data_ref[b].astype(jnp.float32)
        values.append(decode(raw[: pairs * HALF]) * (spare_rows(raw, 3, 2) * (1.0 / TOP)))
        held_ref[b], bias_ref[b : b + 1, :] = weight_rows(raw, pairs * HALF)
    for q in range(pairs):
        for h in range(2):
            parts = []
            for half in range(2):
                start = (2 * half + h) * width
                pieces = [v[q * HALF : (q + 1) * HALF, start : start + width] for v in values]
                parts.append(jnp.concatenate(pieces, axis=1))
            column = jnp.concatenate(parts, axis=0)[:cols]
            row = 2 * q + h
            out_ref[row] = (cot_ref[row].astype(jnp.float32) + column).astype(jnp.bfloat16)


def weights_kernel(inner, share, place_ref, held_ref, own_bias_ref, *refs):
    pieces, (win_ref, bin_ref, wout_ref) = refs[: inner - 1], refs[inner - 1 :]
    member = place_ref[1]
    blocks, rows, wide = held_ref.shape
    width = wide // 4
    data_rows = pieces[0].shape[1] - rows
    for b in range(blocks):
        held = [(held_ref[b], own_bias_ref[b : b + 1, :])]
        held += [weight_rows(ref[b].astype(jnp.float32), data_rows) for ref in pieces]
        for n in range(inner):
            part, bias = held[0]
            for s in range(1, inner):
                chosen = lax.rem(member - s + inner, inner) == n
                part = jnp.where(chosen, held[s][0], part)
                bias = jnp.where(chosen, held[s][1], bias)
            for i in range(4):
                target = (win_ref, wout_ref)[i // 2]
                target[i % 2, b, n * share : (n + 1) * share, :] = part[:share, i * width : (i + 1) * width]
            if n == 0:
                for k in range(2):
                    bin_ref[k, b : b + 1, :] = bias[:, k * width : (k + 1) * width]


def body(features, cotangent, weight_in, bias_in, weight_out):
    lon_count, lat_count = lax.axis_size("lon"), lax.axis_size("lat")
    blocks, width = weight_in.shape[1:3]
    rows, cols, _ = features.shape
    inner = lon_count // blocks
    pairs = rows // 2
    wide = 4 * width
    modes = 2 * MODE_DEV * blocks
    size = 2 * rows * lat_count * SUB
    subs = modes // (2 * SUB)
    lon_place = lax.axis_index("lon")
    lat_place = lax.axis_index("lat")
    scalars = jnp.stack([lon_place // inner, lon_place % inner, lat_place]).astype(jnp.int32)
    scaling = (rows * lat_count * modes // 2 * inner) ** -0.5
    paired = inner == 2 and blocks == 2 + 2 * len(BASES)
    tables, starts = all_tables(blocks, inner, cols, rows, lat_count, paired)
    lon_start, lat_start, synth_start, _ = starts
    shares = 1 if paired else inner
    share = width // shares
    data_rows = pairs * HALF
    total_rows = data_rows + -(-share // 8) * 8
    sum_rows = -(-(share + 1) // 8) * 8
    f32, bf16 = jnp.float32, jnp.bfloat16
    shape = jax.ShapeDtypeStruct

    places = [[g * inner + i for g in range(blocks)] for i in range(inner)]

    def exchange(values):
        return lax.all_to_all(
            values, "lon", split_axis=0, concat_axis=0, tiled=True, axis_index_groups=places
        )

    def to_member(values, step):
        turn = [(i, i // inner * inner + (i + step) % inner) for i in range(lon_count)]
        return lax.ppermute(values, "lon", turn)

    def to_place(values, first, second):
        turn = [(i, (i // 2 ^ (second if i % 2 else first)) * 2 + i % 2) for i in range(lon_count)]
        return lax.ppermute(values, "lon", turn)

    def to_lat(values, step):
        return lax.ppermute(values, "lat", [(i, (i + step) % lat_count) for i in range(lat_count)])

    def by_place(table):
        return pl.BlockSpec((1, 1, *table.shape[2:]), lambda i, s: (s[0], s[1], 0, 0))

    def serve(slots):
        return [to_place(x, base, base + 1) for x, base in zip(slots, BASES)]

    spectrum = dict(
        outputs=(shape((pairs * modes + PAD, wide), bf16),),
        scratch=(pltpu.VMEM((pairs, modes, wide), f32),),
    )
    if paired:
        rows_in = pairs * PAD
        packed, side = call(
            functools.partial(own_pack_kernel, width),
            scalars,
            (jnp.stack([features, cotangent]),),
            (shape((blocks, rows_in, wide), bf16), shape((rows_in, wide), bf16)),
            flops=10**8,
        )
        own, *slots = call(
            functools.partial(pair_kernel, width),
            scalars,
            (packed, to_member(features, 1), to_member(cotangent, 1)),
            [shape((2, rows_in, wide), bf16)] * (1 + len(BASES)),
            scratch=(pltpu.VMEM((blocks, rows_in, wide), bf16),),
        )
        side = to_place(side, 1, 1)
        sent = [side, *serve(slots)]
        late = [to_member(x, 1) for x in sent]
        table = paired_table(blocks, cols)
        specs = {0: by_place(table)}
        (early,) = call(
            early_lon_kernel, scalars, (table, own, *sent), (shape((pairs, 2 * modes, wide), f32),), specs=specs
        )
        (coded,) = call(late_lon_kernel, scalars, (table, early, *late), specs=specs, **spectrum)
    else:
        (packed,) = call(
            functools.partial(pack_kernel, width),
            scalars,
            (features, cotangent),
            (shape((blocks, pairs * PAD, wide), bf16),),
        )
        whole = exchange(packed)
        fields = [whole] + [to_member(whole, s) for s in range(1, inner)]
        (coded,) = call(functools.partial(lon_kernel, inner), scalars, (tables, *fields), **spectrum)
    others = [to_lat(coded, s) for s in range(1, lat_count)]
    block_spec = pl.BlockSpec((2, 1, width, width), lambda i, s: (0, s[0], 0, 0))
    part, forms, bias = call(
        functools.partial(ready_kernel, pairs, lat_start),
        scalars,
        (tables, coded, weight_in, bias_in, weight_out),
        (
            shape((size, 2 * subs * width), f32),
            shape((4, 2 * width, 2 * width), bf16),
            shape((8, 2 * width), f32),
        ),
        specs={2: block_spec, 4: block_spec},
        flops=6 * size * size // lat_count * 2 * subs * width,
    )
    if paired:
        outs = [shape((pairs * modes // 2 + sum_rows, wide), f32)]
    else:
        outs = [shape((pairs, modes, 2 * width), f32), *[shape((sum_rows, wide), f32)] * shares]
    back, *rest = call(
        functools.partial(mlp_kernel, lat_count, inner, shares, pairs, lat_start, scaling),
        scalars,
        (tables, *others, part, forms, bias),
        outs,
        scratch=() if paired else (pltpu.VMEM((shares, sum_rows, wide), f32),),
    )
    backs = [back] + [to_member(back, s) for s in range(1, inner)]
    if paired:
        table = served_table(blocks, cols)
        count = table.shape[2] // PAD
        outs = [share + data_rows] * 2 + [share + 2 * data_rows] * len(BASES)
        own, side, *slots = call(
            functools.partial(serve_kernel, pairs),
            scalars,
            (table, *backs),
            [shape((n, wide), bf16) for n in outs],
            specs={0: by_place(table)},
            scratch=(pltpu.VMEM((count, data_rows, wide), f32),),
        )
        sent = serve(slots)

        def first(group):
            n = len(group)
            return call(
                functools.partial(first_kernel, data_rows),
                scalars,
                group,
                (
                    shape((n, data_rows, wide), f32),
                    shape((n, 4, share, width), f32),
                    shape((n, 2 * width), f32),
                ),
            )

        held, sent[0] = lax.optimization_barrier((first([own, to_place(side, 1, 1)]), sent[0]))
        late = [to_member(x, 1) for x in sent]
        held = [*held, *first(sent)]
        return call(
            functools.partial(last_kernel, data_rows),
            scalars,
            (*held, cotangent, *late),
            [shape(x.shape, x.dtype) for x in (features, weight_in, bias_in, weight_out)],
            scratch=(pltpu.VMEM((blocks, data_rows, wide), f32),),
        )
    keep, *send = rest
    sums = [keep] + [to_member(send[s - 1], s) for s in range(1, inner)]
    (payload,) = call(
        functools.partial(synth_kernel, inner, synth_start),
        scalars,
        (tables, *backs, *sums),
        (shape((blocks, total_rows, wide), bf16),),
        scratch=(pltpu.VMEM((blocks, pairs * HALF, wide), f32),),
    )
    returned = exchange(payload)
    gathered = [to_member(returned, s) for s in range(1, inner)]
    weight_part = total_rows - pairs * HALF
    grad_features, held, held_bias = call(
        columns_kernel,
        scalars,
        (returned, cotangent),
        (
            shape(features.shape, bf16),
            shape((blocks, weight_part, wide), f32),
            shape((blocks, 2 * width), f32),
        ),
    )
    grad_w_in, grad_b_in, grad_w_out = call(
        functools.partial(weights_kernel, inner, share),
        scalars,
        (held, held_bias, *gathered),
        (shape(weight_in.shape, f32), shape(bias_in.shape, f32), shape(weight_out.shape, f32)),
    )
    return grad_features, grad_w_in, grad_b_in, grad_w_out


def solution(mesh):
    placed = (P("lat", "lon", None), P("lat", "lon", None), P(), P(), P())
    return jax.shard_map(
        body,
        mesh=mesh,
        in_specs=placed,
        out_specs=(P("lat", "lon", None), P(), P(), P()),
        check_vma=False,
    )
```
